32 devices in a mesh: dp: 4 (over x, core), row: 2 (over y), col: 4 (over z).
Axes of the slice: x: 2, y: 2, z: 4, core: 2. Of those that a mesh axis runs over, the one named last changes fastest.
Arguments:
- tokens: bfloat16 [2, 5120, 1024], P(None, ('dp', 'row'), 'col'), may hold values from -110 to 110
- segment_ids: int32 [2, 5120], P(None, 'dp'), may hold values from 0 to 2, as said below
- prompt_reach: int32 [2, 5120], P(None, 'dp'), may hold values from 0 to 1024, as said below
- attn_gain_1: float32 [1024], P('col'), may hold values from 0.5 to 1.5
- query_weight_1: bfloat16 [1024, 1024], P('row', 'col'), may hold values from -0.1875 to 0.1875
- key_weight_1: bfloat16 [1024, 1024], P('row', 'col'), may hold values from -0.1875 to 0.1875
- value_weight_1: bfloat16 [1024, 1024], P('row', 'col'), may hold values from -0.1875 to 0.1875
- out_weight_1: bfloat16 [1024, 1024], P('col', 'row'), may hold values from -3 to 3
- ffn_gain_1: float32 [1024], P('col'), may hold values from 0.5 to 1.5
- gate_weight_1: bfloat16 [1024, 2816], P('row', 'col'), may hold values from -0.1875 to 0.1875
- up_weight_1: bfloat16 [1024, 2816], P('row', 'col'), may hold values from -0.1875 to 0.1875
- down_weight_1: bfloat16 [2816, 1024], P('col', 'row'), may hold values from -0.109375 to 0.109375
- attn_gain_2: float32 [1024], P('col'), may hold values from 0.5 to 1.5
- query_weight_2: bfloat16 [1024, 1024], P('row', 'col'), may hold values from -0.1875 to 0.1875
- key_weight_2: bfloat16 [1024, 1024], P('row', 'col'), may hold values from -0.1875 to 0.1875
- value_weight_2: bfloat16 [1024, 1024], P('row', 'col'), may hold values from -0.1875 to 0.1875
- out_weight_2: bfloat16 [1024, 1024], P('col', 'row'), may hold values from -3 to 3
- ffn_gain_2: float32 [1024], P('col'), may hold values from 0.5 to 1.5
- gate_weight_2: bfloat16 [1024, 2816], P('row', 'col'), may hold values from -0.1875 to 0.1875
- up_weight_2: bfloat16 [1024, 2816], P('row', 'col'), may hold values from -0.1875 to 0.1875
- down_weight_2: bfloat16 [2816, 1024], P('col', 'row'), may hold values from -0.109375 to 0.109375
- out_grad: bfloat16 [2, 5120, 1024], P(None, ('dp', 'row'), 'col'), may hold values from -6 to 6
Outputs:
- output: bfloat16 [2, 5120, 1024], P(None, ('dp', 'row'), 'col')
- input_grad: float32 [2, 5120, 1024], P(None, ('dp', 'row'), 'col')
- grad_attn_gain_1: float32 [1024], P('col')
- grad_query_1: float32 [1024, 1024], P('row', 'col')
- grad_key_1: float32 [1024, 1024], P('row', 'col')
- grad_value_1: float32 [1024, 1024], P('row', 'col')
- grad_out_1: float32 [1024, 1024], P('col', 'row')
- grad_ffn_gain_1: float32 [1024], P('col')
- grad_gate_1: float32 [1024, 2816], P('row', 'col')
- grad_up_1: float32 [1024, 2816], P('row', 'col')
- grad_down_1: float32 [2816, 1024], P('col', 'row')
- grad_attn_gain_2: float32 [1024], P('col')
- grad_query_2: float32 [1024, 1024], P('row', 'col')
- grad_key_2: float32 [1024, 1024], P('row', 'col')
- grad_value_2: float32 [1024, 1024], P('row', 'col')
- grad_out_2: float32 [1024, 1024], P('col', 'row')
- grad_ffn_gain_2: float32 [1024], P('col')
- grad_gate_2: float32 [1024, 2816], P('row', 'col')
- grad_up_2: float32 [1024, 2816], P('row', 'col')
- grad_down_2: float32 [2816, 1024], P('col', 'row')
The draws below stay inside these ranges and needn't reach their ends.
Inputs may be any that keep to these rules, and one draw needn't show every extreme that they name: `segment_ids`: in each group the first 1024 tokens are segment 0, the prompt; then come 2 continuations numbered 1 to 2 in order, of 64 to 192 tokens each, 256 tokens together, one of exactly the largest length in every group. `prompt_reach`: 0 on prompt tokens; one value for all tokens of a continuation, 512 or more; in every group some continuation has 1024.
All inputs are finite; a program needn't handle non-finite values.
Results may differ from the reference program's by a relative error of at most 0.033.
Values may be sent and summed in bfloat16 or wider, within the bound.
No kernel may reach another device: no remote copies, remote signals or barrier semaphores. Data moves between devices by JAX's collectives and lax.ppermute only.
A program may use at most 320 MiB of HBM per device.

```python
import math
import jax
import jax.numpy as jnp
from jax import lax

D = 1024
HEADS = 16
HEAD_DIM = 64
FF = 2816
PROMPT = 1024
BRANCHES = 2
BRANCH_LEN = 128
MICRO = 2
GROUP = 1280
TOKENS = 5120


def branch_layout(key):
    groups = TOKENS // GROUP
    mean_len = BRANCH_LEN
    half_len = mean_len // 2
    pairs = BRANCHES // 2
    lead_shape = (MICRO, groups)
    delta_key, pick_key, order_key, reach_key, full_key = jax.random.split(jax.random.fold_in(key, 4242), 5)
    deltas = jax.random.randint(delta_key, lead_shape + (pairs,), 0, half_len + 1)
    chosen = jax.random.randint(pick_key, lead_shape + (1,), 0, pairs)
    deltas = jnp.where(jnp.arange(pairs)[None, None, :] == chosen, half_len, deltas)
    lengths = jnp.concatenate([mean_len + deltas, mean_len - deltas], axis=2)
    order_scores = jax.random.randint(order_key, lead_shape + (BRANCHES,), 0, 1 << 20) * BRANCHES + jnp.arange(BRANCHES)[None, None, :]
    order_idx = jnp.argsort(order_scores, axis=2)
    lengths = jnp.take_along_axis(lengths, order_idx, axis=2)
    branch_ends = jnp.cumsum(lengths, axis=2)
    offsets = jnp.arange(BRANCHES * BRANCH_LEN)
    branch_seg = 1 + jnp.sum((offsets[None, None, :, None] >= branch_ends[:, :, None, :]).astype(jnp.int32), axis=3)
    segments = jnp.concatenate([jnp.zeros(lead_shape + (PROMPT,), jnp.int32), branch_seg.astype(jnp.int32)], axis=2)
    reach_each = jax.random.randint(reach_key, lead_shape + (BRANCHES,), PROMPT // 2, PROMPT + 1)
    full_at = jax.random.randint(full_key, lead_shape + (1,), 0, BRANCHES)
    reach_each = jnp.where(jnp.arange(BRANCHES)[None, None, :] == full_at, PROMPT, reach_each)
    onehot = (branch_seg[..., None] == jnp.arange(1, BRANCHES + 1)[None, None, None, :]).astype(jnp.int32)
    branch_reach = jnp.sum(onehot * reach_each[:, :, None, :], axis=3)
    reach = jnp.concatenate([jnp.zeros(lead_shape + (PROMPT,), jnp.int32), branch_reach.astype(jnp.int32)], axis=2)
    return (segments.reshape(MICRO, TOKENS).astype(jnp.int32), reach.reshape(MICRO, TOKENS).astype(jnp.int32))


def draw_segment_ids(key, part):
    return branch_layout(key)[0]


def draw_prompt_reach(key, part):
    return branch_layout(key)[1]


def draw_tokens(key, part):
    base_key, row_key, col_key = jax.random.split(jax.random.fold_in(key, 77), 3)
    base = jnp.clip(jax.random.normal(base_key, (MICRO, TOKENS, D), jnp.float32), -6.0, 6.0)
    row_scale = jnp.exp(jax.random.uniform(row_key, (MICRO, TOKENS, 1), jnp.float32, math.log(0.4), math.log(4.0)))
    trend = jnp.arange(D, dtype=jnp.float32) / (D - 1) * math.log(3.0)
    col_scale = 0.45 * jnp.exp(trend + jax.random.uniform(col_key, (D,), jnp.float32, 0.0, math.log(3.3)))
    return (base * row_scale * col_scale[None, None, :]).astype(jnp.bfloat16)


def levels(own_key, extent, cuts, smallest, high):
    loudness = 1.0
    for dim, blocks in cuts:
        draws = jax.random.uniform(jax.random.fold_in(jax.random.fold_in(own_key, 6), dim), (blocks,), jnp.float32, smallest / len(cuts), high / len(cuts))
        loudness = loudness * jnp.repeat(jnp.exp(draws), extent[dim] // blocks).reshape((-1,) + (1,) * (len(extent) - 1 - dim))
    return loudness


def normal_values(stream_key, shape, scale, most, pieces=(), held_as=jnp.bfloat16):
    loudness = levels(stream_key, shape, pieces, -0.22, 0.18) if pieces else 1.0
    drawn = jax.random.normal(stream_key, shape, jnp.float32) * scale * loudness
    return jnp.minimum(jnp.maximum(drawn, -most), most).astype(held_as)


def setup_inputs(seed: int = 0) -> dict:
    streams_of = jax.random.split(jax.random.key(seed), 23)
    return {
        "tokens": draw_tokens(jax.random.fold_in(streams_of[22], 71), 0),
        "segment_ids": draw_segment_ids(jax.random.fold_in(streams_of[22], 71), 0),
        "prompt_reach": draw_prompt_reach(jax.random.fold_in(streams_of[22], 71), 0),
        "attn_gain_1": jnp.clip(1.0 + 0.1 * jax.random.normal(streams_of[3], (D,), jnp.float32), 0.5, 1.5),
        "query_weight_1": normal_values(streams_of[4], (D, D), D ** -0.5, 0.1875, ((0, 2), (1, 4))),
        "key_weight_1": normal_values(streams_of[5], (D, D), D ** -0.5, 0.1875, ((0, 2), (1, 4))),
        "value_weight_1": normal_values(streams_of[6], (D, D), D ** -0.5, 0.1875, ((0, 2), (1, 4))),
        "out_weight_1": normal_values(streams_of[7], (D, D), (max(D // 256, 1)) ** -0.5, 3.0, ((0, 4), (1, 2))),
        "ffn_gain_1": jnp.clip(1.0 + 0.1 * jax.random.normal(streams_of[8], (D,), jnp.float32), 0.5, 1.5),
        "gate_weight_1": normal_values(streams_of[9], (D, FF), D ** -0.5, 0.1875, ((0, 2), (1, 4))),
        "up_weight_1": normal_values(streams_of[10], (D, FF), D ** -0.5, 0.1875, ((0, 2), (1, 4))),
        "down_weight_1": normal_values(streams_of[11], (FF, D), FF ** -0.5, 0.109375, ((0, 4), (1, 2))),
        "attn_gain_2": jnp.clip(1.0 + 0.1 * jax.random.normal(streams_of[12], (D,), jnp.float32), 0.5, 1.5),
        "query_weight_2": normal_values(streams_of[13], (D, D), D ** -0.5, 0.1875, ((0, 2), (1, 4))),
        "key_weight_2": normal_values(streams_of[14], (D, D), D ** -0.5, 0.1875, ((0, 2), (1, 4))),
        "value_weight_2": normal_values(streams_of[15], (D, D), D ** -0.5, 0.1875, ((0, 2), (1, 4))),
        "out_weight_2": normal_values(streams_of[16], (D, D), (max(D // 256, 1)) ** -0.5, 3.0, ((0, 4), (1, 2))),
        "ffn_gain_2": jnp.clip(1.0 + 0.1 * jax.random.normal(streams_of[17], (D,), jnp.float32), 0.5, 1.5),
        "gate_weight_2": normal_values(streams_of[18], (D, FF), D ** -0.5, 0.1875, ((0, 2), (1, 4))),
        "up_weight_2": normal_values(streams_of[19], (D, FF), D ** -0.5, 0.1875, ((0, 2), (1, 4))),
        "down_weight_2": normal_values(streams_of[20], (FF, D), FF ** -0.5, 0.109375, ((0, 4), (1, 2))),
        "out_grad": normal_values(streams_of[21], (MICRO, TOKENS, D), 1.0, 6.0, ((1, 8), (2, 4))),
    }


norm_eps = 1e-06
rope_base = 10000.0
top_precision = lax.Precision.HIGHEST

@jax.custom_vjp
def low(v):
    return lax.optimization_barrier(v.astype(jnp.bfloat16)).astype(jnp.float32)

@jax.custom_vjp
def low_back(v):
    return v

def low_keep(v):
    return (low(v), None)

def low_pass(kept, grad):
    return (grad,)

def back_keep(v):
    return (v, None)

def back_low(kept, grad):
    return (low(grad),)
low.defvjp(low_keep, low_pass)
low_back.defvjp(back_keep, back_low)

def token_positions(segments, reach, seg_count):
    seg_labels = jnp.arange(seg_count, dtype=jnp.int32)
    onehot = (segments[:, None] == seg_labels[None, :]).astype(jnp.int32)
    seg_sizes = lax.optimization_barrier(jnp.sum(onehot, axis=0))
    seg_starts = jnp.cumsum(seg_sizes) - seg_sizes
    first_token = lax.optimization_barrier(jnp.sum(onehot * seg_starts[None, :], axis=1))
    return jnp.arange(segments.shape[0], dtype=jnp.int32) - first_token + reach

def rope_tables(position, head_dim):
    half_dim = head_dim // 2
    inverse = rope_base ** (-(jnp.arange(half_dim, dtype=jnp.float32) * 2.0) / head_dim)
    angles = position.astype(jnp.float32)[:, None] * inverse[None, :]
    return (jnp.cos(angles)[:, None, :], jnp.sin(angles)[:, None, :])

def rotate(values, cosine, sine):
    half_dim = values.shape[-1] // 2
    first_half = values[..., :half_dim]
    second_half = values[..., half_dim:]
    return jnp.concatenate([first_half * cosine - second_half * sine, second_half * cosine + first_half * sine], axis=-1)

def matmul(left, right):
    return jnp.dot(left, right, precision=top_precision, preferred_element_type=jnp.float32)

def rms_norm(residual, gain):
    factor = lax.rsqrt(lax.optimization_barrier(jnp.mean(residual * residual, axis=1)) + norm_eps)
    return residual * factor[:, None] * gain[None, :]

def attention(queries, key_rows, values, segments, reach):
    group_len = queries.shape[0]
    block_rows = group_len // max(1, group_len // 512)
    block_count = group_len // block_rows
    key_index = jnp.arange(group_len, dtype=jnp.int32)

    def one_block(block_item):
        query_block, query_index, query_seg, query_reach = block_item
        scores = jnp.einsum('qhd,khd->hqk', query_block, key_rows, precision=top_precision) * HEAD_DIM ** (-0.5)
        allowed = (query_seg[:, None] == segments[None, :]) & (key_index[None, :] <= query_index[:, None]) | (key_index[None, :] < query_reach[:, None])
        scores = low_back(jnp.where(allowed[None], scores, -1e+30))
        probability = low(jax.nn.softmax(scores, axis=2))
        return jnp.einsum('hqk,khd->qhd', probability, values, precision=top_precision)
    block_items = (queries.reshape(block_count, block_rows, HEADS, HEAD_DIM), key_index.reshape(block_count, block_rows), segments.reshape(block_count, block_rows), reach.reshape(block_count, block_rows))
    return lax.map(jax.checkpoint(one_block), block_items).reshape(group_len, HEADS * HEAD_DIM)

def layer(residual, weight_set, first_values, segments, reach, cosine, sine):
    attn_gain, w_query, w_key, w_value, w_out, ffn_gain, w_gate, w_up, w_down = weight_set
    group_len = residual.shape[0]
    normed = low(rms_norm(residual, attn_gain))
    queries = low_back(matmul(normed, w_query)).reshape(group_len, HEADS, HEAD_DIM)
    key_rows = low_back(matmul(normed, w_key)).reshape(group_len, HEADS, HEAD_DIM)
    queries = low(rotate(queries, cosine, sine))
    key_rows = low(rotate(key_rows, cosine, sine))
    raw_values = matmul(normed, w_value)
    if first_values is None:
        values = low(low_back(raw_values))
    else:
        values = low(low_back(0.5 * raw_values + 0.5 * first_values))
    mixture = attention(queries, key_rows, values.reshape(group_len, HEADS, HEAD_DIM), segments, reach)
    mixture = low(low_back(mixture))
    residual = residual + low_back(matmul(mixture, w_out))
    normed_ffn = low(rms_norm(residual, ffn_gain))
    gate_act = low_back(matmul(normed_ffn, w_gate))
    up_act = low_back(matmul(normed_ffn, w_up))
    hidden = low(jax.nn.silu(gate_act) * up_act)
    residual = residual + low_back(matmul(hidden, w_down))
    return (residual, values)

def forward(residual, weight_set, segments, reach):
    positions = token_positions(segments, reach, BRANCHES + 1)
    cosine, sine = rope_tables(positions, HEAD_DIM)
    residual, first_values = layer(residual, weight_set[:9], None, segments, reach, cosine, sine)
    residual, unused_values = layer(residual, weight_set[9:], first_values, segments, reach, cosine, sine)
    return residual

def reference(tokens, segment_ids, prompt_reach, attn_gain_1, query_weight_1, key_weight_1, value_weight_1, out_weight_1, ffn_gain_1, gate_weight_1, up_weight_1, down_weight_1, attn_gain_2, query_weight_2, key_weight_2, value_weight_2, out_weight_2, ffn_gain_2, gate_weight_2, up_weight_2, down_weight_2, out_grad):
    weight_set = tuple((matrix.astype(jnp.float32) for matrix in (attn_gain_1, query_weight_1, key_weight_1, value_weight_1, out_weight_1, ffn_gain_1, gate_weight_1, up_weight_1, down_weight_1, attn_gain_2, query_weight_2, key_weight_2, value_weight_2, out_weight_2, ffn_gain_2, gate_weight_2, up_weight_2, down_weight_2)))
    group_len = GROUP
    group_count = MICRO * (TOKENS // group_len)
    inputs = tokens.astype(jnp.float32).reshape(group_count, group_len, D)
    group_segs = segment_ids.reshape(group_count, group_len)
    group_reach = prompt_reach.reshape(group_count, group_len)
    cotangents = out_grad.astype(jnp.float32).reshape(group_count, group_len, D)

    def group_step(totals, group_item):
        residual, segments, reach, cotangent = group_item
        result, pullback = jax.vjp(lambda residual_in, weights_in: forward(residual_in, weights_in, segments, reach), residual, weight_set)
        grad_residual, grad_weights = pullback(cotangent)
        totals = tuple((left_term + right_term for left_term, right_term in zip(totals, grad_weights)))
        return (totals, (result, grad_residual))
    zeros_set = tuple((jnp.zeros_like(matrix) for matrix in weight_set))
    totals, (results, grad_inputs) = lax.scan(group_step, zeros_set, (inputs, group_segs, group_reach, cotangents))
    output = results.reshape(MICRO, TOKENS, D).astype(jnp.bfloat16)
    input_grad = grad_inputs.reshape(MICRO, TOKENS, D)
    return (output, input_grad, totals[0], totals[1], totals[2], totals[3], totals[4], totals[5], totals[6], totals[7], totals[8], totals[9], totals[10], totals[11], totals[12], totals[13], totals[14], totals[15], totals[16], totals[17])
```

```python
import jax
import jax.numpy as jnp
from jax import lax
from jax.sharding import Mesh, PartitionSpec as P

D = 1024
HEAD_DIM = 64
norm_eps = 1e-06
rope_base = 10000.0
bf16 = jnp.bfloat16
f32 = jnp.float32

SWAP = [(0, 1), (1, 0)]


def dot_nt(left, right):
    return lax.dot_general(left, right, (((1,), (1,)), ((), ())), preferred_element_type=f32)


def dot_nn(left, right):
    return lax.dot_general(left, right, (((1,), (0,)), ((), ())), preferred_element_type=f32)


def dot_tn(left, right):
    return lax.dot_general(left, right, (((0,), (0,)), ((), ())), preferred_element_type=f32)


class Lane:
    def __init__(self, axis, window):
        self.axis, self.window, self.sent = axis, window, []

    def send(self, value, perm):
        if self.window and len(self.sent) >= self.window:
            value, _ = lax.optimization_barrier((value, self.sent[-self.window]))
        value = lax.ppermute(value, self.axis, perm)
        self.sent.append(value)
        return value


def swap_core(value):
    return lax.ppermute(value, "core", SWAP)


def make_body(col_count):
    ring_up = [(i, (i + 1) % col_count) for i in range(col_count)]
    ring_down = [(i, (i - 1) % col_count) for i in range(col_count)]
    rounds = []
    for k in range(col_count):
        pairs = []
        for core in range(2):
            for col in range(col_count):
                j = col ^ k
                pairs.append((core * col_count + col, (j & 1) * col_count + (j & ~1) + core))
        rounds.append(pairs)

    def body(
        tokens, segment_ids, prompt_reach,
        attn_gain_1, query_weight_1, key_weight_1, value_weight_1, out_weight_1,
        ffn_gain_1, gate_weight_1, up_weight_1, down_weight_1,
        attn_gain_2, query_weight_2, key_weight_2, value_weight_2, out_weight_2,
        ffn_gain_2, gate_weight_2, up_weight_2, down_weight_2,
        out_grad,
    ):
        xo_count = lax.axis_size("xo")
        xi, core = lax.axis_index("xi"), lax.axis_index("core")
        row, col = lax.axis_index("row"), lax.axis_index("col")
        chip_rows = tokens.shape[1]
        own_rows = chip_rows // 2
        half_d = D // 2
        quarter = tokens.shape[2]
        slot = (col // 2) * 2 + core

        lane_x, lane_y, lane_z = Lane("xi", 2), Lane("row", 2), Lane("col", 2)

        def spread(array):
            pieces = array.reshape(col_count, own_rows, quarter)
            got = []
            for k in range(col_count):
                piece = lax.dynamic_index_in_dim(pieces, col ^ k, 0, keepdims=False)
                got.append(lax.ppermute(piece, ("core", "col"), rounds[k]))
            got = jnp.stack(got)
            return jnp.concatenate(
                [
                    lax.dynamic_index_in_dim(got, p ^ (2 * row) ^ slot, 0, keepdims=False)
                    for p in range(col_count)
                ],
                axis=1,
            )

        def unspread(array):
            pieces = jnp.stack([array[:, p * quarter : (p + 1) * quarter] for p in range(col_count)])
            got = []
            for k in range(col_count):
                piece = lax.dynamic_index_in_dim(
                    pieces, slot ^ k ^ (2 * row), 0, keepdims=False
                )
                back = [(b, a) for a, b in rounds[k]]
                got.append(lax.ppermute(piece, ("core", "col"), back))
            got = jnp.stack(got)
            got = jnp.concatenate(
                [lax.dynamic_index_in_dim(got, j ^ col, 0) for j in range(col_count)], axis=0
            )
            return got.reshape(tokens.shape)

        def turn(array, by, axis):
            first, second = jnp.split(array, 2, axis=axis)
            return jnp.where(
                by == 0, array, jnp.concatenate([second, first], axis=axis)
            )

        residual = spread(tokens).astype(f32)

        both = jnp.stack([segment_ids, prompt_reach])
        both = jnp.where(core == col % 2, both, swap_core(both))
        both = lax.dynamic_index_in_dim(both, col // 2, 1, keepdims=False)
        segments, reach = both[0], both[1]
        group_len = segments.shape[0]
        size_0 = jnp.sum((segments == 0).astype(jnp.int32))
        size_1 = jnp.sum((segments == 1).astype(jnp.int32))
        starts = jnp.where(segments == 0, 0, jnp.where(segments == 1, size_0, size_0 + size_1))
        index = jnp.arange(group_len, dtype=jnp.int32)
        positions = index - starts + reach

        def mine(array):
            part = lax.dynamic_slice_in_dim(array, row * chip_rows, chip_rows, 0)
            return turn(part, core, 0)

        inverse = rope_base ** (-(jnp.arange(HEAD_DIM // 2, dtype=f32) * 2.0) / HEAD_DIM)
        angles = mine(positions).astype(f32)[:, None] * inverse[None, :]
        cosine, sine = jnp.cos(angles)[:, None, :], jnp.sin(angles)[:, None, :]
        query_index, query_seg, query_reach = mine(index), mine(segments), mine(reach)
        first_index = jnp.where(row == 0, group_len, turn(index[:chip_rows], core, 0))
        key_index = jnp.concatenate([first_index, query_index])
        key_seg = jnp.concatenate([turn(segments[:chip_rows], core, 0), query_seg])
        allowed = (query_seg[:, None] == key_seg[None, :]) & (
            key_index[None, :] <= query_index[:, None]
        ) | (key_index[None, :] < query_reach[:, None])
        bias = jnp.where(allowed, 0.0, -1e30).astype(f32)

        gains = jnp.stack([attn_gain_1, ffn_gain_1, attn_gain_2, ffn_gain_2])
        gains = turn(lax.all_gather(gains, "col", axis=1, tiled=True), row, 1)

        def units(block, transposed):
            if transposed:
                size = block.shape[1] // 2
                return lax.dynamic_slice_in_dim(block, core * size, size, 1).T
            size = block.shape[0] // 2
            return lax.dynamic_slice_in_dim(block, core * size, size, 0)

        def x_halves(blocks):
            packed = jnp.concatenate([b.reshape(2, -1, half_d) for b in blocks], axis=1)
            return turn(packed, xi, 0)

        def join(pieces, blocks):
            result, at = [], 0
            for b in blocks:
                size = b.shape[0] // 2
                result.append(
                    jnp.concatenate([p[at : at + size] for pair in pieces for p in pair], axis=0)
                )
                at += size
            return result

        def gather_y_first(blocks):
            halves = x_halves(blocks)
            rows = halves.shape[1]
            other = lane_y.send(halves.reshape(2 * rows, half_d), SWAP).reshape(halves.shape)
            here = jnp.concatenate([halves, other], axis=2)
            pieces, moving = [(here[0], here[1])], here[0]
            for _ in range(col_count - 1):
                moving = lane_z.send(moving, ring_up)
                pieces.append((moving, lane_x.send(moving, SWAP)))
            return join(pieces, blocks)

        def gather_y_last(blocks):
            halves = x_halves(blocks)
            rows = halves.shape[1]
            pairs, moving = [halves.reshape(2 * rows, half_d)], halves[0]
            for _ in range(col_count - 1):
                moving = lane_z.send(moving, ring_up)
                pairs.append(jnp.concatenate([moving, lane_x.send(moving, SWAP)], axis=0))
            pieces = []
            for pair in pairs:
                whole = jnp.concatenate([pair, lane_y.send(pair, SWAP)], axis=1)
                pieces.append((whole[:rows], whole[rows:]))
            return join(pieces, blocks)

        def gather_layer(w_query, w_key, w_value, w_out, w_gate, w_up, w_down, down_first):
            query, key = gather_y_first([units(w_query, True), units(w_key, True)])
            value, out = gather_y_last([units(w_value, True), units(w_out, False)])
            gate_u, up_u, down_u = units(w_gate, True), units(w_up, True), units(w_down, False)
            if down_first:
                gate, down = gather_y_first([gate_u, down_u])
                (up,) = gather_y_last([up_u])
            else:
                (gate,) = gather_y_first([gate_u])
                up, down = gather_y_last([up_u, down_u])
            return query, key, value, out, gate, up, down

        weights_one = gather_layer(
            query_weight_1, key_weight_1, value_weight_1, out_weight_1,
            gate_weight_1, up_weight_1, down_weight_1, True,
        )
        weights_two = gather_layer(
            query_weight_2, key_weight_2, value_weight_2, out_weight_2,
            gate_weight_2, up_weight_2, down_weight_2, False,
        )

        def settle(block_halves, blocks_units):
            result, at = [], 0
            for size in blocks_units:
                half = size // 2
                result.append(block_halves[:, at : at + half].reshape(size, half_d))
                at += half
            return result

        def pack(grads):
            return jnp.concatenate(
                [g.reshape(col_count, 2, -1, D) for g in grads], axis=2
            )

        def ring_sum(parts):
            total = parts[col_count - 1].astype(f32)
            for k in reversed(range(col_count - 1)):
                total = lane_z.send(total.astype(bf16), ring_down).astype(f32) + parts[k].astype(f32)
            return total

        def over_xo(total):
            if xo_count > 1:
                total = lax.psum(total.astype(bf16), "xo").astype(f32)
            return total

        def scatter_x_first(grads):
            packed = pack(grads)
            rows = packed.shape[2]
            parts = []
            for k in reversed(range(col_count)):
                parts.append(packed[k, 0].astype(f32) + lane_x.send(packed[k, 1], SWAP).astype(f32))
            total = ring_sum(parts[::-1])
            total = total[:, :half_d] + lane_y.send(
                total[:, half_d:].astype(bf16), SWAP
            ).astype(f32)
            total = over_xo(total).astype(bf16)
            halves = turn(jnp.stack([total, lane_x.send(total, SWAP)]), xi, 0)
            return settle(halves, [g.shape[0] // col_count for g in grads])

        def scatter_y_first(grads):
            packed = pack(grads)
            rows = packed.shape[2]
            packed = packed.reshape(col_count, 2 * rows, D)
            parts = []
            for k in reversed(range(col_count)):
                parts.append(
                    packed[k, :, :half_d].astype(f32)
                    + lane_y.send(packed[k, :, half_d:], SWAP).astype(f32)
                )
            total = over_xo(ring_sum(parts[::-1]))
            halves = turn(total.reshape(2, rows, half_d), xi, 0)
            halves = halves + lane_x.send(halves.astype(bf16), SWAP).astype(f32)
            return settle(halves.astype(bf16), [g.shape[0] // col_count for g in grads])

        def finish(block, transposed):
            pair = turn(jnp.concatenate([block, swap_core(block)], axis=0), core, 0)
            return (pair.T if transposed else pair).astype(f32)

        def rotate(values, sine_signed):
            values = values.reshape(chip_rows, -1, HEAD_DIM)
            half = HEAD_DIM // 2
            first, second = values[..., :half], values[..., half:]
            turned = jnp.concatenate(
                [first * cosine - second * sine_signed, second * cosine + first * sine_signed],
                axis=-1,
            )
            return turned.reshape(chip_rows, -1)

        def both_cores(own):
            return jnp.concatenate([own, swap_core(own)], axis=0)

        def core_sum(partial):
            sent = swap_core(partial[own_rows:].astype(bf16))
            return partial[:own_rows].astype(bf16).astype(f32) + sent.astype(f32)

        def normalize(value, gain):
            factor = lax.rsqrt(jnp.mean(value * value, axis=1, keepdims=True) + norm_eps)
            return both_cores((value * factor * gain[None, :]).astype(bf16)), factor

        def normalize_back(partial, value, factor, gain):
            grad_normed = core_sum(partial)
            unit = value * factor
            gain_grad = jnp.sum(grad_normed * unit, axis=0)
            grad_unit = grad_normed * gain[None, :]
            inner = jnp.mean(grad_unit * unit, axis=1, keepdims=True)
            return factor * (grad_unit - unit * inner), gain_grad

        def heads(array):
            return array.reshape(array.shape[0], -1, HEAD_DIM)

        def from_first(array):
            return lane_y.send(array, [(0, 1)])

        def to_first(array):
            return lane_y.send(array, [(1, 0)])

        def attend(queries, keys, values):
            scores = jnp.einsum("qhd,khd->hqk", heads(queries), heads(keys), preferred_element_type=f32)
            scores = scores * HEAD_DIM ** (-0.5) + bias[None]
            peak = jnp.max(scores, axis=2, keepdims=True)
            total = jnp.sum(jnp.exp(scores - peak), axis=2, keepdims=True)
            log_total = peak + jnp.log(total)
            probability = jnp.exp(scores - log_total).astype(bf16)
            mixed = jnp.einsum("hqk,khd->qhd", probability, heads(values), preferred_element_type=f32)
            return mixed.reshape(chip_rows, -1).astype(bf16), log_total

        def attend_back(queries, keys, values, log_total, grad_out):
            scores = jnp.einsum("qhd,khd->hqk", heads(queries), heads(keys), preferred_element_type=f32)
            scores = scores * HEAD_DIM ** (-0.5) + bias[None]
            probability = jnp.exp(scores - log_total)
            grad_p = jnp.einsum("qhd,khd->hqk", heads(grad_out), heads(values), preferred_element_type=f32)
            inner = jnp.sum(probability * grad_p, axis=2, keepdims=True)
            grad_s = (probability * (grad_p - inner)).astype(bf16)
            scale = HEAD_DIM ** (-0.5)
            gq = jnp.einsum("hqk,khd->qhd", grad_s, heads(keys), preferred_element_type=f32) * scale
            gk = jnp.einsum("hqk,qhd->khd", grad_s, heads(queries), preferred_element_type=f32) * scale
            gv = jnp.einsum(
                "hqk,qhd->khd", probability.astype(bf16), heads(grad_out), preferred_element_type=f32
            )
            flat = lambda a: a.reshape(a.shape[0], -1)
            return flat(gq), flat(gk), flat(gv)

        def layer_forward(value, weights, attn_gain, ffn_gain, first_values):
            w_query, w_key, w_value, w_out, w_gate, w_up, w_down = weights
            attn_input = value
            normed, attn_factor = normalize(value, attn_gain)
            key_own = rotate(dot_nt(normed, w_key), sine).astype(bf16)
            raw = dot_nt(normed, w_value)
            if first_values is not None:
                raw = 0.5 * raw + 0.5 * first_values.astype(f32)
            value_own = raw.astype(bf16)
            sent = from_first(jnp.concatenate([key_own, value_own], axis=1))
            width = key_own.shape[1]
            queries = rotate(dot_nt(normed, w_query), sine).astype(bf16)
            keys = jnp.concatenate([sent[:, :width], key_own], axis=0)
            values = jnp.concatenate([sent[:, width:], value_own], axis=0)
            mixture, log_total = attend(queries, keys, values)
            value = value + core_sum(dot_nn(mixture, w_out))
            ffn_input = value
            normed_ffn, ffn_factor = normalize(value, ffn_gain)
            gate = dot_nt(normed_ffn, w_gate)
            up = dot_nt(normed_ffn, w_up)
            hidden = (jax.nn.silu(gate) * up).astype(bf16)
            value = value + core_sum(dot_nn(hidden, w_down))
            saved = (
                attn_input, attn_factor, normed, queries, keys, values, mixture, log_total,
                ffn_input, ffn_factor, normed_ffn, gate, up, hidden,
            )
            return value, value_own, saved

        def layer_backward(grad, weights, attn_gain, ffn_gain, saved, extra, is_second):
            w_query, w_key, w_value, w_out, w_gate, w_up, w_down = weights
            (
                attn_input, attn_factor, normed, queries, keys, values, mixture, log_total,
                ffn_input, ffn_factor, normed_ffn, gate, up, hidden,
            ) = saved
            grad_full = both_cores(grad.astype(bf16))
            grad_hidden = dot_nt(grad_full, w_down)
            sig = jax.nn.sigmoid(gate)
            grad_gate = (grad_hidden * up * sig * (1.0 + gate * (1.0 - sig))).astype(bf16)
            grad_up = (grad_hidden * gate * sig).astype(bf16)
            g_down = dot_tn(hidden, grad_full).astype(bf16)
            partial = dot_nn(grad_gate, w_gate) + dot_nn(grad_up, w_up)
            g_gate = dot_tn(grad_gate, normed_ffn).astype(bf16)
            g_up = dot_tn(grad_up, normed_ffn).astype(bf16)
            if is_second:
                b_down, b_up = scatter_y_first([g_down, g_up])
                (b_gate,) = scatter_x_first([g_gate])
            else:
                b_down, b_gate = scatter_x_first([g_down, g_gate])
                (b_up,) = scatter_y_first([g_up])
            grad_norm, g_ffn_gain = normalize_back(partial, ffn_input, ffn_factor, ffn_gain)
            grad = grad + grad_norm
            grad_full = both_cores(grad.astype(bf16))
            g_out = dot_tn(mixture, grad_full).astype(bf16)
            grad_mixture = dot_nt(grad_full, w_out).astype(bf16)
            gq, gk, gv = attend_back(queries, keys, values, log_total, grad_mixture)
            width = gk.shape[1]
            sent = to_first(
                jnp.concatenate([gk[:chip_rows].astype(bf16), gv[:chip_rows].astype(bf16)], axis=1)
            )
            gk = gk[chip_rows:] + sent[:, :width].astype(f32)
            gv = gv[chip_rows:] + sent[:, width:].astype(f32)
            grad_query = rotate(gq, -sine).astype(bf16)
            grad_key = rotate(gk, -sine).astype(bf16)
            if is_second:
                grad_mix = gv.astype(bf16).astype(f32)
                grad_value = (0.5 * grad_mix).astype(bf16)
                extra = 0.5 * grad_mix
            else:
                grad_value = (gv + extra).astype(bf16)
            partial = (
                dot_nn(grad_query, w_query) + dot_nn(grad_key, w_key) + dot_nn(grad_value, w_value)
            )
            g_query = dot_tn(grad_query, normed).astype(bf16)
            g_key = dot_tn(grad_key, normed).astype(bf16)
            g_value = dot_tn(grad_value, normed).astype(bf16)
            b_out, b_value = scatter_y_first([g_out, g_value])
            b_query, b_key = scatter_x_first([g_query, g_key])
            grad_norm, g_attn_gain = normalize_back(partial, attn_input, attn_factor, attn_gain)
            grad = grad + grad_norm
            blocks = (b_query, b_key, b_value, b_out, b_gate, b_up, b_down)
            return grad, blocks, (g_attn_gain, g_ffn_gain), extra

        residual, first_values, saved_one = layer_forward(
            residual, weights_one, gains[0], gains[1], None
        )
        residual, _, saved_two = layer_forward(
            residual, weights_two, gains[2], gains[3], first_values
        )
        output = unspread(residual.astype(bf16))
        grad = spread(out_grad).astype(f32)
        grad, blocks_two, gains_two, extra = layer_backward(
            grad, weights_two, gains[2], gains[3], saved_two, None, True
        )
        grad, blocks_one, gains_one, _ = layer_backward(
            grad, weights_one, gains[0], gains[1], saved_one, extra, False
        )
        input_grad = unspread(grad.astype(bf16)).astype(f32)

        gain_grads = turn(jnp.stack(gains_one + gains_two), row, 1)
        gain_grads = lax.psum(gain_grads, ("xo", "xi", "core", "row", "col"))
        gain_grads = lax.dynamic_slice_in_dim(gain_grads, col * quarter, quarter, 1)

        def outs(blocks):
            kinds = (True, True, True, False, True, True, False)
            return [finish(b, t) for b, t in zip(blocks, kinds)]

        one, two = outs(blocks_one), outs(blocks_two)
        return (
            output, input_grad,
            gain_grads[0], *one[:4], gain_grads[1], *one[4:],
            gain_grads[2], *two[:4], gain_grads[3], *two[4:],
        )

    return body


def solution(mesh):
    devices = mesh.devices
    dp, rows, cols = devices.shape
    split = Mesh(
        devices.reshape(dp // 4, 2, 2, rows, cols), ("xo", "xi", "core", "row", "col")
    )
    dp_axes = ("xo", "xi", "core")
    token = P(None, dp_axes + ("row",), "col")
    group = P(None, dp_axes)
    gain = P("col")
    tall, wide = P("row", "col"), P("col", "row")
    layer = (gain, tall, tall, tall, wide, gain, tall, tall, wide)
    return jax.shard_map(
        make_body(cols),
        mesh=split,
        in_specs=(token, group, group) + layer + layer + (token,),
        out_specs=(token, token) + layer + layer,
        check_vma=False,
    )
```

```python
import jax
import jax.numpy as jnp
from jax import lax
from jax.experimental import pallas as pl
from jax.experimental.pallas import tpu as pltpu
from jax.sharding import Mesh, PartitionSpec as P

D = 1024
HEAD_DIM = 64
norm_eps = 1e-06
rope_base = 10000.0
scale = HEAD_DIM ** (-0.5)
bf16 = jnp.bfloat16
f32 = jnp.float32
PAIR = 2 * HEAD_DIM

SWAP = [(0, 1), (1, 0)]
VMEM = pltpu.CompilerParams(vmem_limit_bytes=56 << 20)


def dot_nt(left, right):
    return lax.dot_general(left, right, (((1,), (1,)), ((), ())), preferred_element_type=f32)


def dot_nn(left, right):
    return lax.dot_general(left, right, (((1,), (0,)), ((), ())), preferred_element_type=f32)


def dot_tn(left, right):
    return lax.dot_general(left, right, (((0,), (0,)), ((), ())), preferred_element_type=f32)


def swap_core(value):
    return lax.ppermute(value, "core", SWAP)


def swap_x(value):
    return lax.ppermute(value, "xi", SWAP)


def swap_y(value):
    return lax.ppermute(value, "row", SWAP)


def after(value, *milestones):
    return lax.optimization_barrier((value,) + milestones)[0] if milestones else value


def turn(array, by, axis):
    first, second = jnp.split(array, 2, axis=axis)
    return jnp.where(by == 0, array, jnp.concatenate([second, first], axis=axis))


def rotated(values, cos_ref, sin_ref):
    width = values.shape[1]
    half = HEAD_DIM // 2
    lane = lax.broadcasted_iota(jnp.int32, values.shape, 1) % HEAD_DIM
    other = jnp.where(
        lane < half, pltpu.roll(values, width - half, 1), pltpu.roll(values, half, 1)
    )
    cos, sin = cos_ref[...], sin_ref[...]
    times = width // PAIR
    if times > 1:
        cos = jnp.concatenate([cos] * times, axis=1)
        sin = jnp.concatenate([sin] * times, axis=1)
    return values * cos + other * sin


def project(normed, weight, cos, sin, kinds, mix):
    rows, block = normed.shape[0], 256
    steps = weight.shape[0] // block
    turned = sum(kinds)

    def kernel(n_ref, w_ref, cos_ref, sin_ref, *rest):
        out_ref = rest[-1]
        step = pl.program_id(0)
        result = dot_nt(n_ref[...], w_ref[...])

        @pl.when(step < turned)
        def _():
            out_ref[...] = rotated(result, cos_ref, sin_ref).astype(bf16)

        @pl.when(step >= turned)
        def _():
            if mix is None:
                out_ref[...] = result.astype(bf16)
            else:
                out_ref[...] = (0.5 * result + 0.5 * rest[0][...].astype(f32)).astype(bf16)

    whole = lambda shape: pl.BlockSpec(shape, lambda i: (0, 0))
    in_specs = [
        whole((rows, D)),
        pl.BlockSpec((block, D), lambda i: (i, 0)),
        whole((rows, PAIR)),
        whole((rows, PAIR)),
    ]
    operands = [normed, weight, cos, sin]
    if mix is not None:
        skip = mix.shape[1] // block - (steps - turned)
        in_specs.append(
            pl.BlockSpec((rows, block), lambda i: (0, jnp.maximum(i - turned, 0) + skip))
        )
        operands.append(mix)
    return pl.pallas_call(
        kernel,
        grid=(steps,),
        in_specs=in_specs,
        out_specs=pl.BlockSpec((rows, block), lambda i: (0, i)),
        out_shape=jax.ShapeDtypeStruct((rows, weight.shape[0]), bf16),
        compiler_params=VMEM,
        cost_estimate=pl.CostEstimate(
            flops=1,
            bytes_accessed=1,
            transcendentals=0,
        ),
    )(*operands)


def assemble(whole, by_y, by_x, low, high, cols, counts):
    rows, width = whole.shape[0] // cols, whole.shape[1]
    size = rows // sum(counts)
    half = cols // 2

    def kernel(whole_ref, y_ref, x_ref, low_ref, high_ref, *outs):
        step = pl.program_id(0)
        at = 0
        for out, count in zip(outs, counts):
            for j in range(count):
                piece = slice(at, at + size)
                out[j, :, :width] = whole_ref[piece]
                out[j, :, width : 2 * width] = y_ref[piece]
                out[j, :, 2 * width : 3 * width] = x_ref[piece]

                @pl.when(step < half)
                def _():
                    out[j, :, 3 * width :] = low_ref[piece]

                @pl.when(step >= half)
                def _():
                    out[j, :, 3 * width :] = high_ref[piece]

                at += size

    block = lambda index: pl.BlockSpec((rows, width), index)
    outs = pl.pallas_call(
        kernel,
        grid=(cols,),
        in_specs=[
            block(lambda i: (i, 0)),
            block(lambda i: (i, 0)),
            block(lambda i: (i, 0)),
            block(lambda i: (jnp.minimum(i, half - 1), 0)),
            block(lambda i: (jnp.maximum(i - half, 0), 0)),
        ],
        out_specs=[pl.BlockSpec((c, size, 4 * width), lambda i: (0, i, 0)) for c in counts],
        out_shape=[jax.ShapeDtypeStruct((c, cols * size, 4 * width), bf16) for c in counts],
        compiler_params=VMEM,
        cost_estimate=pl.CostEstimate(flops=1, bytes_accessed=1, transcendentals=0),
    )(whole, by_y, by_x, low, high)
    return [o.reshape(-1, 4 * width) for o in outs]


def pair_block(rows, first):
    return pl.BlockSpec((rows, PAIR), lambda i: (0, first + i))


def attend(own, first, bias):
    n, m = own.shape[0], first.shape[0]
    width = own.shape[1] // 3
    pairs = width // PAIR

    def kernel(q_ref, ka_ref, kb_ref, va_ref, vb_ref, bias_ref, out_ref, total_ref):
        for h in range(2):
            lanes = slice(h * HEAD_DIM, (h + 1) * HEAD_DIM)
            keys = jnp.concatenate([ka_ref[:, lanes], kb_ref[:, lanes]], axis=0)
            values = jnp.concatenate([va_ref[:, lanes], vb_ref[:, lanes]], axis=0)
            scores = dot_nt(keys, q_ref[:, lanes]) * scale + bias_ref[...]
            peak = jnp.max(scores, axis=0, keepdims=True)
            weight = jnp.exp(scores - peak)
            total = jnp.sum(weight, axis=0, keepdims=True)
            mixed = dot_tn(values, weight.astype(bf16))
            out_ref[:, lanes] = (mixed / total).T.astype(bf16)
            total_ref[0, h, :, :] = peak + jnp.log(total)

    return pl.pallas_call(
        kernel,
        grid=(pairs,),
        in_specs=[
            pair_block(n, 0),
            pair_block(m, 0),
            pair_block(n, pairs),
            pair_block(m, pairs),
            pair_block(n, 2 * pairs),
            pl.BlockSpec((m + n, n), lambda i: (0, 0)),
        ],
        out_specs=[pair_block(n, 0), pl.BlockSpec((1, 2, 1, n), lambda i: (i, 0, 0, 0))],
        out_shape=[
            jax.ShapeDtypeStruct((n, width), bf16),
            jax.ShapeDtypeStruct((pairs, 2, 1, n), f32),
        ],
        compiler_params=VMEM,
        cost_estimate=pl.CostEstimate(
            flops=1, bytes_accessed=1, transcendentals=0
        ),
    )(own, first, own, first, own, bias)


def attend_back(own, first, bias, totals, mixture, grad_out, tables, extra):
    n, m = own.shape[0], first.shape[0]
    width = own.shape[1] // 3
    pairs = width // PAIR
    cos_own, sin_own, cos_first, sin_first = tables

    def kernel(
        q_ref, ka_ref, kb_ref, va_ref, vb_ref, bias_ref, total_ref, mix_ref, go_ref,
        co_ref, so_ref, cf_ref, sf_ref, *rest
    ):
        gq_ref, gka_ref, gkb_ref, gva_ref, gvb_ref = rest[-5:]
        queries_back, keys_back, values_back = [], [], []
        for h in range(2):
            lanes = slice(h * HEAD_DIM, (h + 1) * HEAD_DIM)
            keys = jnp.concatenate([ka_ref[:, lanes], kb_ref[:, lanes]], axis=0)
            values = jnp.concatenate([va_ref[:, lanes], vb_ref[:, lanes]], axis=0)
            queries, grads = q_ref[:, lanes], go_ref[:, lanes]
            inner = jnp.sum(
                grads.astype(f32) * mix_ref[:, lanes].astype(f32), axis=1, keepdims=True
            )
            inner = jnp.broadcast_to(inner, (n, 128)).T[:1]
            scores = dot_nt(keys, queries) * scale + bias_ref[...]
            weight = jnp.exp(scores - total_ref[0, h, :, :])
            grad_weight = dot_nt(values, grads)
            grad_scores = (weight * (grad_weight - inner)).astype(bf16)
            values_back.append(dot_nn(weight.astype(bf16), grads))
            keys_back.append(dot_nn(grad_scores, queries))
            queries_back.append(dot_tn(keys, grad_scores).T)
        side = lambda pair: jnp.concatenate(pair, axis=1)
        gq_ref[...] = rotated(side(queries_back) * scale, co_ref, so_ref).astype(bf16)
        gk, gv = side(keys_back) * scale, side(values_back)
        gka_ref[...] = rotated(gk[:m], cf_ref, sf_ref).astype(bf16)
        gkb_ref[...] = rotated(gk[m:], co_ref, so_ref).astype(bf16)
        if extra is None:
            gva_ref[...] = (0.5 * gv[:m].astype(bf16).astype(f32)).astype(bf16)
            gvb_ref[...] = (0.5 * gv[m:].astype(bf16).astype(f32)).astype(bf16)
        else:
            gva_ref[...] = (gv[:m] + rest[0][...].astype(f32)).astype(bf16)
            gvb_ref[...] = (gv[m:] + rest[1][...].astype(f32)).astype(bf16)

    whole = lambda shape: pl.BlockSpec(shape, lambda i: (0, 0))
    in_specs = [
        pair_block(n, 0),
        pair_block(m, 0),
        pair_block(n, pairs),
        pair_block(m, pairs),
        pair_block(n, 2 * pairs),
        whole((m + n, n)),
        pl.BlockSpec((1, 2, 1, n), lambda i: (i, 0, 0, 0)),
        pair_block(n, 0),
        pair_block(n, 0),
        whole((n, PAIR)),
        whole((n, PAIR)),
        whole((m, PAIR)),
        whole((m, PAIR)),
    ]
    operands = [own, first, own, first, own, bias, totals, mixture, grad_out]
    operands += [cos_own, -sin_own, cos_first, -sin_first]
    if extra is not None:
        in_specs += [pair_block(m, 0), pair_block(n, 0)]
        operands += list(extra)
    shape = lambda rows: jax.ShapeDtypeStruct((rows, width), bf16)
    return pl.pallas_call(
        kernel,
        grid=(pairs,),
        in_specs=in_specs,
        out_specs=[pair_block(r, 0) for r in (n, m, n, m, n)],
        out_shape=[shape(r) for r in (n, m, n, m, n)],
        compiler_params=VMEM,
        cost_estimate=pl.CostEstimate(
            flops=1, bytes_accessed=1, transcendentals=0
        ),
    )(*operands)


def make_body(col_count):
    ring_up = [(i, (i + 1) % col_count) for i in range(col_count)]
    rounds = []
    for k in range(col_count):
        pairs = []
        for core in range(2):
            for col in range(col_count):
                j = col ^ k
                pairs.append((core * col_count + col, (j & 1) * col_count + (j & ~1) + core))
        rounds.append(pairs)
    backs = [[(b, a) for a, b in pairs] for pairs in rounds]

    def body(
        tokens, segment_ids, prompt_reach,
        attn_gain_1, query_weight_1, key_weight_1, value_weight_1, out_weight_1,
        ffn_gain_1, gate_weight_1, up_weight_1, down_weight_1,
        attn_gain_2, query_weight_2, key_weight_2, value_weight_2, out_weight_2,
        ffn_gain_2, gate_weight_2, up_weight_2, down_weight_2,
        out_grad,
    ):
        xo_count = lax.axis_size("xo")
        xi, core = lax.axis_index("xi"), lax.axis_index("core")
        row, col = lax.axis_index("row"), lax.axis_index("col")
        chip_rows = tokens.shape[1]
        own_rows = chip_rows // 2
        quarter = tokens.shape[2]
        half_d = 2 * quarter
        slot = (col // 2) * 2 + core

        def place(p):
            return (2 * row + xi) ^ (0, 2, 1, 3)[p]

        gains = jnp.stack([attn_gain_1, ffn_gain_1, attn_gain_2, ffn_gain_2])
        high = gains.astype(bf16)
        middle = (gains - high.astype(f32)).astype(bf16)
        low = (gains - high.astype(f32) - middle.astype(f32)).astype(bf16)
        small = jnp.concatenate([high, middle, low, jnp.zeros_like(high)], axis=0)
        def unspread(array):
            pieces = jnp.stack([array[:, p * quarter : (p + 1) * quarter] for p in (0, 1, 2, 3)])
            got = []
            for k in range(col_count):
                p = slot ^ k ^ (2 * row + xi)
                p = (p & 1) * 2 + (p >> 1)
                piece = lax.dynamic_index_in_dim(pieces, p, 0, keepdims=False)
                got.append(lax.ppermute(piece, ("core", "col"), backs[k]))
            got = jnp.stack(got)
            got = jnp.concatenate(
                [lax.dynamic_index_in_dim(got, j ^ col, 0) for j in range(col_count)], axis=0
            )
            return got.reshape(tokens.shape)

        def units(block, transposed):
            if transposed:
                size = block.shape[1] // 2
                block = lax.dynamic_slice_in_dim(block, core * size, size, 1).T
            else:
                size = block.shape[0] // 2
                block = lax.dynamic_slice_in_dim(block, core * size, size, 0)
            return turn(block, xi, 1)

        def stack_attn(w_query, w_key, w_value, w_out):
            return jnp.concatenate(
                [units(w_query, True), units(w_key, True), units(w_value, True), units(w_out, False)]
            )

        def gather_col(block):
            return lax.all_gather(block, "col", axis=0, tiled=True)

        class Crossing:
            def __init__(self, whole, *milestones):
                self.whole = after(whole, *milestones)
                self.sides = (swap_x(self.whole), swap_y(self.whole))

            def complete(self, counts, *milestones):
                by_x, by_y = after(self.sides, *milestones)
                half = by_x.shape[0] // 2
                self.both = (swap_x(by_y[:half]), swap_y(by_x[half:]))
                return assemble(self.whole, by_y, by_x, *self.both, col_count, counts)

        def near_x(block):
            return block[:, :quarter]

        def local_ffn(w_gate, w_up, w_down):
            blocks = (units(w_gate, True), units(w_up, True), units(w_down, False))
            return jnp.concatenate([near_x(b) for b in blocks])

        attn_local_one = near_x(
            stack_attn(query_weight_1, key_weight_1, value_weight_1, out_weight_1)
        )
        attn_local_two = near_x(
            stack_attn(query_weight_2, key_weight_2, value_weight_2, out_weight_2)
        )
        ffn_local_one = local_ffn(gate_weight_1, up_weight_1, down_weight_1)
        ffn_local_two = local_ffn(gate_weight_2, up_weight_2, down_weight_2)
        half = attn_local_one.shape[0] // 2
        qk_whole_one = gather_col(attn_local_one[:half])
        vo_whole_one = gather_col(after(attn_local_one[half:], qk_whole_one))
        attn_whole_one = jnp.concatenate(
            [w.reshape(col_count, -1, quarter) for w in (qk_whole_one, vo_whole_one)], axis=1
        ).reshape(-1, quarter)
        ffn_whole_one = gather_col(after(ffn_local_one, vo_whole_one))
        attn_whole_two = gather_col(after(attn_local_two, ffn_whole_one))

        pieces = jnp.concatenate(
            [
                tokens.reshape(col_count, own_rows, quarter),
                out_grad.reshape(col_count, own_rows, quarter),
                jnp.broadcast_to(small[None], (col_count,) + small.shape),
            ],
            axis=1,
        )
        got = []
        for k in range(col_count):
            piece = lax.dynamic_index_in_dim(pieces, col ^ k, 0, keepdims=False)
            got.append(lax.ppermute(piece, ("core", "col"), rounds[k]))
        got = jnp.stack(got)
        got = jnp.concatenate(
            [
                lax.dynamic_index_in_dim(got, place(p) ^ slot, 0, keepdims=False)
                for p in range(col_count)
            ],
            axis=1,
        )
        residual = got[:own_rows].astype(f32)
        last_grad = got[own_rows : 2 * own_rows].astype(f32)
        small = got[2 * own_rows :].astype(f32)
        gains = small[0:4] + small[4:8] + small[8:12]

        both = jnp.stack([segment_ids, prompt_reach])
        both = jnp.where(core == col % 2, both, swap_core(both))
        both = lax.dynamic_index_in_dim(both, col // 2, 1, keepdims=False)
        segments, reach = both[0], both[1]
        group_len = segments.shape[0]
        size_0 = jnp.sum((segments == 0).astype(jnp.int32))
        size_1 = jnp.sum((segments == 1).astype(jnp.int32))
        starts = jnp.where(segments == 0, 0, jnp.where(segments == 1, size_0, size_0 + size_1))
        index = jnp.arange(group_len, dtype=jnp.int32)
        positions = index - starts + reach

        def mine(array):
            return turn(lax.dynamic_slice_in_dim(array, row * chip_rows, chip_rows, 0), core, 0)

        def leading(array):
            return turn(array[:chip_rows], core, 0)

        inverse = rope_base ** (-(jnp.arange(HEAD_DIM // 2, dtype=f32) * 2.0) / HEAD_DIM)

        def tables(position):
            angles = position.astype(f32)[:, None] * inverse[None, :]
            cosine, sine = jnp.cos(angles), jnp.sin(angles)
            return (
                jnp.concatenate([cosine] * 4, axis=1),
                jnp.concatenate([-sine, sine, -sine, sine], axis=1),
            )

        cos_own, sin_own = tables(mine(positions))
        cos_first, sin_first = tables(leading(positions))
        rope = (cos_own, sin_own, cos_first, sin_first)
        query_index, query_seg, query_reach = mine(index), mine(segments), mine(reach)
        first_index = jnp.where(row == 0, group_len, leading(index))
        key_index = jnp.concatenate([first_index, query_index])
        key_seg = jnp.concatenate([leading(segments), query_seg])
        allowed = (query_seg[None, :] == key_seg[:, None]) & (
            key_index[:, None] <= query_index[None, :]
        ) | (key_index[:, None] < query_reach[None, :])
        bias = jnp.where(allowed, 0.0, -1e30).astype(f32)

        def over_xo(total):
            if xo_count > 1:
                total = lax.psum(total, "xo")
            return total

        def scatter_col(array):
            return lax.psum_scatter(array, "col", scatter_dimension=0, tiled=True)

        def add(left, right):
            return (left.astype(f32) + right.astype(f32)).astype(bf16)

        def both_blocks(block):
            return jnp.stack([block, swap_core(block)])

        def finish(pair, at, size, transposed):
            pair = turn(pair[:, at : at + size].reshape(2 * size, half_d), core, 0)
            return (pair.T if transposed else pair).astype(f32)

        def quarters(array, *places):
            if len(places) == 1:
                return array[:, places[0] * quarter : (places[0] + 1) * quarter]
            return jnp.concatenate(
                [array[:, p * quarter : (p + 1) * quarter] for p in places], axis=1
            )

        class Return:
            def __init__(self, by_x, by_y):
                stack = lambda parts: jnp.concatenate(parts) if len(parts) > 1 else parts[0]
                self.near = [stack([n for n, _ in parts]) for parts in (by_x, by_y)]
                far = [stack([f for _, f in parts]) for parts in (by_x, by_y)]
                self.sent = (swap_x(far[0]), swap_y(far[1]))

            def second(self, *milestones):
                sent = after(self.sent, *milestones)
                totals = [add(a, b) for a, b in zip(self.near, sent)]
                self.near = [t[:, :quarter] for t in totals]
                self.sent = (swap_y(totals[0][:, quarter:]), swap_x(totals[1][:, quarter:]))

            def last(self, *milestones):
                sent = after(self.sent, *milestones)
                return [add(a, b) for a, b in zip(self.near, sent)]

        def pack_parts(parts):
            packed = [p.reshape(col_count, -1, quarter) for p in parts]
            return jnp.concatenate(packed, axis=1).reshape(-1, quarter)

        def scatter(packed):
            return over_xo(scatter_col(packed))

        def return_ffn(gate, up, down):
            half = down[0].shape[0] // 2
            low = (quarters(down[0], 0, 1)[:half], quarters(down[0], 2, 3)[:half])
            high = (quarters(down[0], 0, 2)[half:], quarters(down[0], 1, 3)[half:])
            return Return([gate, low], [up, high])

        def last_ffn(returned, *milestones):
            first, second = returned.last(*milestones)
            rows = first.shape[0] * 2 // 3
            down = jnp.concatenate([first[rows:], second[rows:]])
            return pack_parts([first[:rows], second[:rows], down])

        def sides(left, right, x_first):
            stay, go = ((0, 1), (2, 3)) if x_first else ((0, 2), (1, 3))
            return (
                dot_tn(left, quarters(right, *stay)).astype(bf16),
                dot_tn(left, quarters(right, *go)).astype(bf16),
            )

        def finish_all(total, kinds, spare=0):
            total = turn(jnp.concatenate([total, swap_x(total)], axis=1), xi, 1)
            pair = both_blocks(total)
            size = (total.shape[0] - spare) // len(kinds)
            blocks = [finish(pair, j * size, size, kind) for j, kind in enumerate(kinds)]
            return (blocks, pair[:, len(kinds) * size :]) if spare else blocks

        def finish_ffn(total, *milestones):
            return finish_all(after(total, *milestones), (True, True, False))

        def finish_attn(total, *milestones, spare=0):
            return finish_all(after(total, *milestones), (True, True, True, False), spare)

        def return_attn(grads, extra_rows=None):
            pack = lambda pair: jnp.concatenate(
                [g.reshape(col_count, -1, D) for g in pair], axis=1
            ).reshape(-1, D)
            rest = list(grads[2:])
            if extra_rows is not None:
                rest.append(jnp.concatenate([extra_rows] * col_count))
            qk, vo = pack(grads[:2]), pack(rest)
            pairs = [
                (quarters(qk, 0, 1), quarters(qk, 2, 3)),
                (quarters(vo, 0, 2), quarters(vo, 1, 3)),
            ]
            return Return(pairs[:1], pairs[1:])

        def both_cores(own):
            return jnp.concatenate([own, swap_core(own)], axis=0)

        def core_sum(partial):
            sent = swap_core(partial[own_rows:].astype(bf16))
            return partial[:own_rows] + sent.astype(f32)

        def normalize(value, gain):
            factor = lax.rsqrt(jnp.mean(value * value, axis=1, keepdims=True) + norm_eps)
            return (value * factor * gain[None, :]).astype(bf16), factor

        def normalize_back(grad_normed, value, factor, gain):
            unit = value * factor
            gain_grad = jnp.sum(grad_normed * unit, axis=0)
            grad_unit = grad_normed * gain[None, :]
            inner = jnp.mean(grad_unit * unit, axis=1, keepdims=True)
            return factor * (grad_unit - unit * inner), gain_grad

        def flip_row(array):
            return jnp.concatenate(
                [array[:, p * quarter : (p + 1) * quarter] for p in (1, 0, 3, 2)], axis=1
            )

        def attn_forward(value, weights, gain, mix, start):
            w_qkv, w_out = weights
            width = w_out.shape[0]
            normed_own, factor = normalize(value, gain)
            normed_first = both_cores(flip_row(lax.ppermute(normed_own, "row", [(0, 1)])))
            normed = both_cores(normed_own)
            own = project(normed, w_qkv, cos_own, sin_own, (1, 1, 1, 1, 0, 0), mix and mix[0])
            first = project(
                normed_first, w_qkv[width:], cos_first, sin_first, (1, 1, 0, 0), mix and mix[1]
            )
            mixture, totals = attend(own, first, bias)
            mixture = after(mixture, *start(normed_first))
            result = value + core_sum(dot_nn(mixture, w_out))
            return result, (value, factor, normed, normed_first, own, first, mixture, totals)

        def ffn_forward(value, weights, gain, deadline):
            w_gate, w_up, w_down = weights
            normed_own, factor = normalize(value, gain)
            normed = both_cores(normed_own)
            gate = dot_nt(normed, w_gate)
            up = dot_nt(normed, w_up)
            hidden = (jax.nn.silu(gate) * up).astype(bf16)
            hidden = after(hidden, *deadline)
            return value + core_sum(dot_nn(hidden, w_down)), (value, factor, normed, gate, up, hidden)

        def ffn_backward(grad, weights, gain, saved, kinds):
            w_gate, w_up, w_down = weights
            value, factor, normed, gate, up, hidden = saved
            grad_full = both_cores(grad.astype(bf16))
            grad_hidden = dot_nt(grad_full, w_down)
            sig = jax.nn.sigmoid(gate)
            grad_gate = (grad_hidden * up * sig * (1.0 + gate * (1.0 - sig))).astype(bf16)
            grad_up = (grad_hidden * gate * sig).astype(bf16)
            grad_normed = core_sum(dot_nn(grad_gate, w_gate) + dot_nn(grad_up, w_up))
            pairs = ((grad_gate, normed), (grad_up, normed), (hidden, grad_full))
            grads = [sides(*pair, k) for pair, k in zip(pairs[:2], kinds)]
            grads.append((dot_tn(*pairs[2]).astype(bf16),))
            step, gain_grad = normalize_back(grad_normed, value, factor, gain)
            return grad + step, grads, gain_grad

        def attn_backward(grad, weights, gain, saved, extra, milestones, late):
            w_qkv, w_out = weights
            width = w_out.shape[0]
            value, factor, normed, normed_first, own, first, mixture, totals = saved
            grad_full = both_cores(grad.astype(bf16))
            grad_mixture = after(dot_nt(grad_full, w_out).astype(bf16), *milestones)
            gq, gk_first, gk, gv_first, gv = attend_back(
                own, first, bias, totals, mixture, grad_mixture, rope, extra
            )
            gk_first, gv_first = after((gk_first, gv_first), *late)
            w_query, w_key, w_value = w_qkv[:width], w_qkv[width : 2 * width], w_qkv[2 * width :]
            operand = core_sum(dot_nn(gk_first, w_key) + dot_nn(gv_first, w_value)).astype(bf16)
            sent = flip_row(lax.ppermute(operand, "row", [(1, 0)])).astype(f32)
            grad_normed = core_sum(dot_nn(gq, w_query) + dot_nn(gk, w_key) + dot_nn(gv, w_value))
            done = gq
            gq, gk, gv, gk_first, gv_first = after((gq, gk, gv, gk_first, gv_first), operand)
            grads = [
                dot_tn(gq, normed).astype(bf16),
                (dot_tn(gk, normed) + dot_tn(gk_first, normed_first)).astype(bf16),
                (dot_tn(gv, normed) + dot_tn(gv_first, normed_first)).astype(bf16),
                dot_tn(mixture, grad_full).astype(bf16),
            ]
            step, gain_grad = normalize_back(grad_normed + sent, value, factor, gain)
            return grad + step, grads, gain_grad, (gv_first, gv), done

        cross = Crossing(attn_whole_one, got)
        attn_one = cross.complete((3, 1), bias, cos_own, cos_first)
        cross_ffn = Crossing(ffn_whole_one, *cross.both)
        residual, kept_attn_one = attn_forward(
            residual, attn_one, gains[0], None, lambda _: (*cross_ffn.sides, attn_whole_two)
        )
        own_one, first_one = kept_attn_one[4], kept_attn_one[5]
        ffn_one = cross_ffn.complete((1, 1, 1))
        cross = Crossing(attn_whole_two, *cross_ffn.both)
        ffn_whole_two = gather_col(after(ffn_local_two, attn_whole_two))
        residual, kept_ffn_one = ffn_forward(residual, ffn_one, gains[1], (*cross.sides, ffn_whole_two))
        attn_two = cross.complete((3, 1))
        ffn_two = []

        def start_ffn_two(normed_first):
            ffn_two.append(Crossing(ffn_whole_two, normed_first, *cross.both))
            return ffn_two[0].sides

        residual, kept_attn_two = attn_forward(
            residual, attn_two, gains[2], (own_one, first_one), start_ffn_two
        )
        ffn_two = ffn_two[0].complete((1, 1, 1))
        residual, kept_ffn_two = ffn_forward(residual, ffn_two, gains[3], ())
        output = unspread(residual.astype(bf16))

        kinds = (True, False)

        def leaves(grads):
            return [a for pair in grads for a in pair]

        grad, g_ffn_two, gain_ffn_two = ffn_backward(
            last_grad, ffn_two, gains[3], kept_ffn_two, kinds
        )
        r_ffn_two = return_ffn(*g_ffn_two)
        grad, g_attn_two, gain_attn_two, extra, done_attn_two = attn_backward(
            grad, attn_two, gains[2], kept_attn_two, None, (output, *leaves(g_ffn_two)), ()
        )
        r_attn_two = return_attn(g_attn_two)
        r_ffn_two.second(grad)
        grad, g_ffn_one, gain_ffn_one = ffn_backward(grad, ffn_one, gains[1], kept_ffn_one, kinds)
        p_ffn_two = last_ffn(r_ffn_two, grad, *leaves(g_ffn_one))
        t_ffn_two = scatter(p_ffn_two)
        r_ffn_one = return_ffn(*g_ffn_one)
        grad, g_attn_one, gain_attn_one, _, done_attn_one = attn_backward(
            grad, attn_one, gains[0], kept_attn_one, extra,
            (p_ffn_two, *leaves(g_ffn_one)), r_ffn_one.sent,
        )
        r_attn_two.second(*r_ffn_one.sent)
        r_ffn_one.second()
        gain_rows = jnp.stack([gain_attn_one, gain_ffn_one, gain_attn_two, gain_ffn_two])
        gain_rows = jnp.pad(gain_rows, ((0, 12), (0, 0))).astype(bf16)
        r_attn_one = return_attn(g_attn_one, gain_rows)
        p_attn_two = pack_parts(r_attn_two.last(*r_attn_one.near))
        t_attn_two = scatter(p_attn_two)
        p_ffn_one = last_ffn(r_ffn_one)
        r_attn_one.second(p_ffn_one)
        t_ffn_one = scatter(p_ffn_one)
        p_attn_one = pack_parts(r_attn_one.last())
        t_attn_one = scatter(after(p_attn_one, t_ffn_one))
        b_ffn_two = finish_ffn(t_ffn_two, p_ffn_one)
        b_attn_two = finish_attn(t_attn_two, p_ffn_one)
        b_ffn_one = finish_ffn(t_ffn_one)
        b_attn_one, gain_sums = finish_attn(t_attn_one, spare=16)
        input_grad = unspread(grad.astype(bf16)).astype(f32)

        total = gain_sums[0, :4].astype(f32) + gain_sums[1, :4].astype(f32)
        total = turn(jnp.concatenate([total, swap_y(total)], axis=1), row, 1)
        total = lax.dynamic_slice_in_dim(total, col * quarter, quarter, 1)

        return (
            output, input_grad,
            total[0], *b_attn_one, total[1], *b_ffn_one,
            total[2], *b_attn_two, total[3], *b_ffn_two,
        )

    return body


def solution(mesh):
    devices = mesh.devices
    dp, rows, cols = devices.shape
    split = Mesh(devices.reshape(dp // 4, 2, 2, rows, cols), ("xo", "xi", "core", "row", "col"))
    dp_axes = ("xo", "xi", "core")
    token = P(None, dp_axes + ("row",), "col")
    group = P(None, dp_axes)
    gain = P("col")
    tall, wide = P("row", "col"), P("col", "row")
    layer = (gain, tall, tall, tall, wide, gain, tall, tall, wide)
    return jax.shard_map(
        make_body(cols),
        mesh=split,
        in_specs=(token, group, group) + layer + layer + (token,),
        out_specs=(token, token) + layer + layer,
        check_vma=False,
    )
```

```python
import jax
import jax.numpy as jnp
from jax import lax
from jax.experimental import pallas as pl
from jax.experimental.pallas import tpu as pltpu
from jax.sharding import Mesh, PartitionSpec as P

D = 1024
HEAD_DIM = 64
norm_eps = 1e-06
rope_base = 10000.0
scale = HEAD_DIM ** (-0.5)
bf16 = jnp.bfloat16
f32 = jnp.float32
PAIR = 2 * HEAD_DIM

SWAP = [(0, 1), (1, 0)]
VMEM = pltpu.CompilerParams(vmem_limit_bytes=56 << 20)


def dot_nt(left, right):
    return lax.dot_general(left, right, (((1,), (1,)), ((), ())), preferred_element_type=f32)


def dot_nn(left, right):
    return lax.dot_general(left, right, (((1,), (0,)), ((), ())), preferred_element_type=f32)


def dot_tn(left, right):
    return lax.dot_general(left, right, (((0,), (0,)), ((), ())), preferred_element_type=f32)


def swap_core(value):
    return lax.ppermute(value, "core", SWAP)


def swap_x(value):
    return lax.ppermute(value, "xi", SWAP)


def swap_y(value):
    return lax.ppermute(value, "row", SWAP)


def after(value, *milestones):
    return lax.optimization_barrier((value,) + milestones)[0] if milestones else value


def turn(array, by, axis):
    first, second = jnp.split(array, 2, axis=axis)
    return jnp.where(by == 0, array, jnp.concatenate([second, first], axis=axis))


def rotated(values, cos_ref, sin_ref):
    width = values.shape[1]
    half = HEAD_DIM // 2
    lane = lax.broadcasted_iota(jnp.int32, values.shape, 1) % HEAD_DIM
    other = jnp.where(
        lane < half, pltpu.roll(values, width - half, 1), pltpu.roll(values, half, 1)
    )
    cos, sin = cos_ref[...], sin_ref[...]
    times = width // PAIR
    if times > 1:
        cos = jnp.concatenate([cos] * times, axis=1)
        sin = jnp.concatenate([sin] * times, axis=1)
    return values * cos + other * sin


def project(normed, turned_weight, plain_weight, skip, cos, sin, mix):
    rows, block = normed.shape[0], 256
    turned = turned_weight.shape[0] // block - skip
    plain = plain_weight.shape[0] // block

    def kernel(n_ref, t_ref, p_ref, cos_ref, sin_ref, *rest):
        out_ref = rest[-1]
        step = pl.program_id(0)

        @pl.when(step < turned)
        def _():
            result = dot_nt(n_ref[...], t_ref[...])
            out_ref[...] = rotated(result, cos_ref, sin_ref).astype(bf16)

        @pl.when(step >= turned)
        def _():
            result = dot_nt(n_ref[...], p_ref[...])
            if mix is not None:
                result = 0.5 * result + 0.5 * rest[0][...].astype(f32)
            out_ref[...] = result.astype(bf16)

    whole = lambda shape: pl.BlockSpec(shape, lambda i: (0, 0))
    later = lambda i: jnp.maximum(i - turned, 0)
    in_specs = [
        whole((rows, D)),
        pl.BlockSpec((block, D), lambda i: (skip + jnp.minimum(i, turned - 1), 0)),
        pl.BlockSpec((block, D), lambda i: (later(i), 0)),
        whole((rows, PAIR)),
        whole((rows, PAIR)),
    ]
    operands = [normed, turned_weight, plain_weight, cos, sin]
    if mix is not None:
        before = mix.shape[1] // block - plain
        in_specs.append(pl.BlockSpec((rows, block), lambda i: (0, before + later(i))))
        operands.append(mix)
    return pl.pallas_call(
        kernel,
        grid=(turned + plain,),
        in_specs=in_specs,
        out_specs=pl.BlockSpec((rows, block), lambda i: (0, i)),
        out_shape=jax.ShapeDtypeStruct((rows, (turned + plain) * block), bf16),
        compiler_params=VMEM,
        cost_estimate=pl.CostEstimate(flops=1, bytes_accessed=1, transcendentals=0),
    )(*operands)


def assemble(whole, by_y, by_x, low, high, cols, counts):
    rows, width = whole.shape[0] // cols, whole.shape[1]
    size = rows // sum(counts)
    half = cols // 2

    def kernel(whole_ref, y_ref, x_ref, low_ref, high_ref, *outs):
        step = pl.program_id(0)
        at = 0
        for out, count in zip(outs, counts):
            for j in range(count):
                piece = slice(at, at + size)
                out[j, :, :width] = whole_ref[piece]
                out[j, :, width : 2 * width] = y_ref[piece]
                out[j, :, 2 * width : 3 * width] = x_ref[piece]

                @pl.when(step < half)
                def _():
                    out[j, :, 3 * width :] = low_ref[piece]

                @pl.when(step >= half)
                def _():
                    out[j, :, 3 * width :] = high_ref[piece]

                at += size

    block = lambda index: pl.BlockSpec((rows, width), index)
    outs = pl.pallas_call(
        kernel,
        grid=(cols,),
        in_specs=[
            block(lambda i: (i, 0)),
            block(lambda i: (i, 0)),
            block(lambda i: (i, 0)),
            block(lambda i: (jnp.minimum(i, half - 1), 0)),
            block(lambda i: (jnp.maximum(i - half, 0), 0)),
        ],
        out_specs=[pl.BlockSpec((c, size, 4 * width), lambda i: (0, i, 0)) for c in counts],
        out_shape=[jax.ShapeDtypeStruct((c, cols * size, 4 * width), bf16) for c in counts],
        compiler_params=VMEM,
        cost_estimate=pl.CostEstimate(flops=1, bytes_accessed=1, transcendentals=0),
    )(whole, by_y, by_x, low, high)
    return [o.reshape(-1, 4 * width) for o in outs]


def pair_block(rows, first):
    return pl.BlockSpec((rows, PAIR), lambda i: (0, first + i))


def attend(own, first, bias):
    n, m = own.shape[0], first.shape[0]
    width = own.shape[1] // 3
    pairs = width // PAIR

    def kernel(q_ref, ka_ref, kb_ref, va_ref, vb_ref, bias_ref, out_ref, total_ref):
        for h in range(2):
            lanes = slice(h * HEAD_DIM, (h + 1) * HEAD_DIM)
            keys = jnp.concatenate([ka_ref[:, lanes], kb_ref[:, lanes]], axis=0)
            values = jnp.concatenate([va_ref[:, lanes], vb_ref[:, lanes]], axis=0)
            scores = dot_nt(keys, q_ref[:, lanes]) * scale + bias_ref[...]
            peak = jnp.max(scores, axis=0, keepdims=True)
            weight = jnp.exp(scores - peak)
            total = jnp.sum(weight, axis=0, keepdims=True)
            mixed = dot_tn(values, weight.astype(bf16))
            out_ref[:, lanes] = (mixed / total).T.astype(bf16)
            total_ref[0, h, :, :] = peak + jnp.log(total)

    return pl.pallas_call(
        kernel,
        grid=(pairs,),
        in_specs=[
            pair_block(n, 0),
            pair_block(m, 0),
            pair_block(n, pairs),
            pair_block(m, pairs),
            pair_block(n, 2 * pairs),
            pl.BlockSpec((m + n, n), lambda i: (0, 0)),
        ],
        out_specs=[pair_block(n, 0), pl.BlockSpec((1, 2, 1, n), lambda i: (i, 0, 0, 0))],
        out_shape=[
            jax.ShapeDtypeStruct((n, width), bf16),
            jax.ShapeDtypeStruct((pairs, 2, 1, n), f32),
        ],
        compiler_params=VMEM,
        cost_estimate=pl.CostEstimate(
            flops=1, bytes_accessed=1, transcendentals=0
        ),
    )(own, first, own, first, own, bias)


def attend_back(own, first, bias, totals, mixture, grad_out, tables, extra):
    n, m = own.shape[0], first.shape[0]
    width = own.shape[1] // 3
    pairs = width // PAIR
    cos_own, sin_own, cos_first, sin_first = tables

    def kernel(
        q_ref, ka_ref, kb_ref, va_ref, vb_ref, bias_ref, total_ref, mix_ref, go_ref,
        co_ref, so_ref, cf_ref, sf_ref, *rest
    ):
        gq_ref, gka_ref, gkb_ref, gva_ref, gvb_ref = rest[-5:]
        queries_back, keys_back, values_back = [], [], []
        for h in range(2):
            lanes = slice(h * HEAD_DIM, (h + 1) * HEAD_DIM)
            keys = jnp.concatenate([ka_ref[:, lanes], kb_ref[:, lanes]], axis=0)
            values = jnp.concatenate([va_ref[:, lanes], vb_ref[:, lanes]], axis=0)
            queries, grads = q_ref[:, lanes], go_ref[:, lanes]
            inner = jnp.sum(
                grads.astype(f32) * mix_ref[:, lanes].astype(f32), axis=1, keepdims=True
            )
            inner = jnp.broadcast_to(inner, (n, 128)).T[:1]
            scores = dot_nt(keys, queries) * scale + bias_ref[...]
            weight = jnp.exp(scores - total_ref[0, h, :, :])
            grad_weight = dot_nt(values, grads)
            grad_scores = (weight * (grad_weight - inner)).astype(bf16)
            values_back.append(dot_nn(weight.astype(bf16), grads))
            keys_back.append(dot_nn(grad_scores, queries))
            queries_back.append(dot_tn(keys, grad_scores).T)
        side = lambda pair: jnp.concatenate(pair, axis=1)
        gq_ref[...] = rotated(side(queries_back) * scale, co_ref, so_ref).astype(bf16)
        gk, gv = side(keys_back) * scale, side(values_back)
        gka_ref[...] = rotated(gk[:m], cf_ref, sf_ref).astype(bf16)
        gkb_ref[...] = rotated(gk[m:], co_ref, so_ref).astype(bf16)
        if extra is None:
            gva_ref[...] = (0.5 * gv[:m].astype(bf16).astype(f32)).astype(bf16)
            gvb_ref[...] = (0.5 * gv[m:].astype(bf16).astype(f32)).astype(bf16)
        else:
            gva_ref[...] = (gv[:m] + rest[0][...].astype(f32)).astype(bf16)
            gvb_ref[...] = (gv[m:] + rest[1][...].astype(f32)).astype(bf16)

    whole = lambda shape: pl.BlockSpec(shape, lambda i: (0, 0))
    in_specs = [
        pair_block(n, 0),
        pair_block(m, 0),
        pair_block(n, pairs),
        pair_block(m, pairs),
        pair_block(n, 2 * pairs),
        whole((m + n, n)),
        pl.BlockSpec((1, 2, 1, n), lambda i: (i, 0, 0, 0)),
        pair_block(n, 0),
        pair_block(n, 0),
        whole((n, PAIR)),
        whole((n, PAIR)),
        whole((m, PAIR)),
        whole((m, PAIR)),
    ]
    operands = [own, first, own, first, own, bias, totals, mixture, grad_out]
    operands += [cos_own, -sin_own, cos_first, -sin_first]
    if extra is not None:
        in_specs += [pair_block(m, 0), pair_block(n, 0)]
        operands += list(extra)
    shape = lambda rows: jax.ShapeDtypeStruct((rows, width), bf16)
    return pl.pallas_call(
        kernel,
        grid=(pairs,),
        in_specs=in_specs,
        out_specs=[pair_block(r, 0) for r in (n, m, n, m, n)],
        out_shape=[shape(r) for r in (n, m, n, m, n)],
        compiler_params=VMEM,
        cost_estimate=pl.CostEstimate(
            flops=1, bytes_accessed=1, transcendentals=0
        ),
    )(*operands)


def make_body(col_count):
    ring_up = [(i, (i + 1) % col_count) for i in range(col_count)]
    rounds = []
    for k in range(col_count):
        pairs = []
        for core in range(2):
            for col in range(col_count):
                j = col ^ k
                pairs.append((core * col_count + col, (j & 1) * col_count + (j & ~1) + core))
        rounds.append(pairs)
    backs = [[(b, a) for a, b in pairs] for pairs in rounds]

    def body(
        tokens, segment_ids, prompt_reach,
        attn_gain_1, query_weight_1, key_weight_1, value_weight_1, out_weight_1,
        ffn_gain_1, gate_weight_1, up_weight_1, down_weight_1,
        attn_gain_2, query_weight_2, key_weight_2, value_weight_2, out_weight_2,
        ffn_gain_2, gate_weight_2, up_weight_2, down_weight_2,
        out_grad,
    ):
        xo_count = lax.axis_size("xo")
        xi, core = lax.axis_index("xi"), lax.axis_index("core")
        row, col = lax.axis_index("row"), lax.axis_index("col")
        chip_rows = tokens.shape[1]
        own_rows = chip_rows // 2
        quarter = tokens.shape[2]
        half_d = 2 * quarter
        slot = (col // 2) * 2 + core

        def place(p):
            return (2 * row + xi) ^ (0, 2, 1, 3)[p]

        gains = jnp.stack([attn_gain_1, ffn_gain_1, attn_gain_2, ffn_gain_2])
        high = gains.astype(bf16)
        middle = (gains - high.astype(f32)).astype(bf16)
        low = (gains - high.astype(f32) - middle.astype(f32)).astype(bf16)
        small = jnp.concatenate([high, middle, low, jnp.zeros_like(high)], axis=0)
        def unspread(array):
            pieces = jnp.stack([array[:, p * quarter : (p + 1) * quarter] for p in (0, 1, 2, 3)])
            got = []
            for k in range(col_count):
                p = slot ^ k ^ (2 * row + xi)
                p = (p & 1) * 2 + (p >> 1)
                piece = lax.dynamic_index_in_dim(pieces, p, 0, keepdims=False)
                got.append(lax.ppermute(piece, ("core", "col"), backs[k]))
            got = jnp.stack(got)
            got = jnp.concatenate(
                [lax.dynamic_index_in_dim(got, j ^ col, 0) for j in range(col_count)], axis=0
            )
            return got.reshape(tokens.shape)

        def units(block, transposed):
            if transposed:
                size = block.shape[1] // 2
                block = lax.dynamic_slice_in_dim(block, core * size, size, 1).T
            else:
                size = block.shape[0] // 2
                block = lax.dynamic_slice_in_dim(block, core * size, size, 0)
            return turn(block, xi, 1)

        def stack_attn(w_query, w_key, w_value, w_out):
            return jnp.concatenate(
                [units(w_query, True), units(w_key, True), units(w_value, True), units(w_out, False)]
            )

        def gather_col(block):
            return lax.all_gather(block, "col", axis=0, tiled=True)

        class Crossing:
            def __init__(self, whole, *milestones):
                self.whole = after(whole, *milestones)
                self.sides = (swap_x(self.whole), swap_y(self.whole))

            def complete(self, counts, *milestones):
                by_x, by_y = after(self.sides, *milestones)
                half = by_x.shape[0] // 2
                self.both = (swap_x(by_y[:half]), swap_y(by_x[half:]))
                return assemble(self.whole, by_y, by_x, *self.both, col_count, counts)

        def near_x(block):
            return block[:, :quarter]

        def local_ffn(w_gate, w_up, w_down):
            blocks = (units(w_gate, True), units(w_up, True), units(w_down, False))
            return jnp.concatenate([near_x(b) for b in blocks])

        attn_local_one = near_x(
            stack_attn(query_weight_1, key_weight_1, value_weight_1, out_weight_1)
        )
        attn_local_two = near_x(
            stack_attn(query_weight_2, key_weight_2, value_weight_2, out_weight_2)
        )
        ffn_local_one = local_ffn(gate_weight_1, up_weight_1, down_weight_1)
        ffn_local_two = local_ffn(gate_weight_2, up_weight_2, down_weight_2)
        half = attn_local_one.shape[0] // 2
        qk_whole_one = gather_col(attn_local_one[:half])
        vo_whole_one = gather_col(after(attn_local_one[half:], qk_whole_one))
        attn_whole_one = jnp.concatenate(
            [w.reshape(col_count, -1, quarter) for w in (qk_whole_one, vo_whole_one)], axis=1
        ).reshape(-1, quarter)
        ffn_whole_one = gather_col(after(ffn_local_one, vo_whole_one))
        attn_whole_two = gather_col(after(attn_local_two, ffn_whole_one))

        def spread(arrays, *milestones):
            pieces = after(jnp.concatenate(arrays, axis=1), *milestones)
            got = []
            for k in range(col_count):
                piece = lax.dynamic_index_in_dim(pieces, col ^ k, 0, keepdims=False)
                got.append(lax.ppermute(piece, ("core", "col"), rounds[k]))
            got = jnp.stack(got)
            return jnp.concatenate(
                [
                    lax.dynamic_index_in_dim(got, place(p) ^ slot, 0, keepdims=False)
                    for p in range(col_count)
                ],
                axis=1,
            )

        by_piece = lambda array: array.reshape(col_count, own_rows, quarter)
        got = spread(
            [by_piece(tokens), jnp.broadcast_to(small[None], (col_count,) + small.shape)],
            vo_whole_one,
        )
        residual = got[:own_rows].astype(f32)
        small = got[own_rows:].astype(f32)
        gains = small[0:4] + small[4:8] + small[8:12]

        both = jnp.stack([segment_ids, prompt_reach])
        both = jnp.where(core == col % 2, both, swap_core(both))
        both = lax.dynamic_index_in_dim(both, col // 2, 1, keepdims=False)
        segments, reach = both[0], both[1]
        group_len = segments.shape[0]
        size_0 = jnp.sum((segments == 0).astype(jnp.int32))
        size_1 = jnp.sum((segments == 1).astype(jnp.int32))
        starts = jnp.where(segments == 0, 0, jnp.where(segments == 1, size_0, size_0 + size_1))
        index = jnp.arange(group_len, dtype=jnp.int32)
        positions = index - starts + reach

        def mine(array):
            return turn(lax.dynamic_slice_in_dim(array, row * chip_rows, chip_rows, 0), core, 0)

        def leading(array):
            return turn(array[:chip_rows], core, 0)

        inverse = rope_base ** (-(jnp.arange(HEAD_DIM // 2, dtype=f32) * 2.0) / HEAD_DIM)

        def tables(position):
            angles = position.astype(f32)[:, None] * inverse[None, :]
            cosine, sine = jnp.cos(angles), jnp.sin(angles)
            return (
                jnp.concatenate([cosine] * 4, axis=1),
                jnp.concatenate([-sine, sine, -sine, sine], axis=1),
            )

        cos_own, sin_own = tables(mine(positions))
        cos_first, sin_first = tables(leading(positions))
        rope = (cos_own, sin_own, cos_first, sin_first)
        query_index, query_seg, query_reach = mine(index), mine(segments), mine(reach)
        first_index = jnp.where(row == 0, group_len, leading(index))
        key_index = jnp.concatenate([first_index, query_index])
        key_seg = jnp.concatenate([leading(segments), query_seg])
        allowed = (query_seg[None, :] == key_seg[:, None]) & (
            key_index[:, None] <= query_index[None, :]
        ) | (key_index[:, None] < query_reach[None, :])
        bias = jnp.where(allowed, 0.0, -1e30).astype(f32)

        def over_xo(total):
            if xo_count > 1:
                total = lax.psum(total, "xo")
            return total

        def scatter_col(array):
            return lax.psum_scatter(array, "col", scatter_dimension=0, tiled=True)

        def add(left, right):
            return (left.astype(f32) + right.astype(f32)).astype(bf16)

        def both_blocks(block):
            return jnp.stack([block, swap_core(block)])

        def finish(pair, at, size, transposed):
            pair = turn(pair[:, at : at + size].reshape(2 * size, half_d), core, 0)
            return (pair.T if transposed else pair).astype(f32)

        def quarters(array, *places):
            if len(places) == 1:
                return array[:, places[0] * quarter : (places[0] + 1) * quarter]
            return jnp.concatenate(
                [array[:, p * quarter : (p + 1) * quarter] for p in places], axis=1
            )

        class Return:
            def __init__(self, by_x, by_y):
                stack = lambda parts: jnp.concatenate(parts) if len(parts) > 1 else parts[0]
                self.near = [stack([n for n, _ in parts]) for parts in (by_x, by_y)]
                far = [stack([f for _, f in parts]) for parts in (by_x, by_y)]
                self.sent = (swap_x(far[0]), swap_y(far[1]))

            def second(self, milestones=(), before_y=()):
                sent = after(self.sent, *milestones)
                totals = [add(a, b) for a, b in zip(self.near, sent)]
                self.near = [t[:, :quarter] for t in totals]
                far = [t[:, quarter:] for t in totals]
                self.sent = (swap_y(after(far[0], *before_y)), swap_x(far[1]))

            def last(self, *milestones):
                sent = after(self.sent, *milestones)
                return [add(a, b) for a, b in zip(self.near, sent)]

        def pack_parts(parts):
            packed = [p.reshape(col_count, -1, quarter) for p in parts]
            return jnp.concatenate(packed, axis=1).reshape(-1, quarter)

        def scatter(packed):
            return over_xo(scatter_col(packed))

        def return_ffn(gate, up, down):
            half = down[0].shape[0] // 2
            low = (quarters(down[0], 0, 1)[:half], quarters(down[0], 2, 3)[:half])
            high = (quarters(down[0], 0, 2)[half:], quarters(down[0], 1, 3)[half:])
            return Return([gate, low], [up, high])

        def last_ffn(returned, *milestones):
            first, second = returned.last(*milestones)
            rows = first.shape[0] * 2 // 3
            return [first[:rows], second[:rows], jnp.concatenate([first[rows:], second[rows:]])]

        def sides(left, right, x_first):
            stay, go = ((0, 1), (2, 3)) if x_first else ((0, 2), (1, 3))
            return (
                dot_tn(left, quarters(right, *stay)).astype(bf16),
                dot_tn(left, quarters(right, *go)).astype(bf16),
            )

        def finish_all(total, kinds, spare=0):
            total = turn(jnp.concatenate([total, swap_x(total)], axis=1), xi, 1)
            pair = both_blocks(total)
            size = (total.shape[0] - spare) // len(kinds)
            blocks = [finish(pair, j * size, size, kind) for j, kind in enumerate(kinds)]
            return (blocks, pair[:, len(kinds) * size :]) if spare else blocks

        def finish_ffn(total, *milestones):
            return finish_all(after(total, *milestones), (True, True, False))

        def finish_attn(total, *milestones, spare=0):
            return finish_all(after(total, *milestones), (True, True, True, False), spare)

        def return_attn(grads, extra_rows=None):
            pack = lambda pair: jnp.concatenate(
                [g.reshape(col_count, -1, D) for g in pair], axis=1
            ).reshape(-1, D)
            rest = list(grads[2:])
            if extra_rows is not None:
                rest.append(jnp.concatenate([extra_rows] * col_count))
            qk, vo = pack(grads[:2]), pack(rest)
            pairs = [
                (quarters(qk, 0, 1), quarters(qk, 2, 3)),
                (quarters(vo, 0, 2), quarters(vo, 1, 3)),
            ]
            return Return(pairs[:1], pairs[1:])

        def both_cores(own):
            return jnp.concatenate([own, swap_core(own)], axis=0)

        def core_sum(partial):
            sent = swap_core(partial[own_rows:].astype(bf16))
            return partial[:own_rows] + sent.astype(f32)

        def normalize(value, gain):
            factor = lax.rsqrt(jnp.mean(value * value, axis=1, keepdims=True) + norm_eps)
            return (value * factor * gain[None, :]).astype(bf16), factor

        def normalize_back(grad_normed, value, factor, gain):
            unit = value * factor
            gain_grad = jnp.sum(grad_normed * unit, axis=0)
            grad_unit = grad_normed * gain[None, :]
            inner = jnp.mean(grad_unit * unit, axis=1, keepdims=True)
            return factor * (grad_unit - unit * inner), gain_grad

        def flip_row(array):
            return jnp.concatenate(
                [array[:, p * quarter : (p + 1) * quarter] for p in (1, 0, 3, 2)], axis=1
            )

        def attn_forward(value, weights, gain, mix, start, *milestones):
            w_qk, w_value, w_out = weights
            normed_own, factor = normalize(value, gain)
            normed_first = both_cores(flip_row(lax.ppermute(after(normed_own, *milestones), "row", [(0, 1)])))
            normed = both_cores(normed_own)
            skip = w_qk.shape[0] // 512
            own = project(normed, w_qk, w_value, 0, cos_own, sin_own, mix and mix[0])
            first = project(normed_first, w_qk, w_value, skip, cos_first, sin_first, mix and mix[1])
            mixture, totals = attend(own, first, bias)
            mixture = after(mixture, *start(normed_first))
            result = value + core_sum(dot_nn(mixture, w_out))
            return result, (value, factor, normed, normed_first, own, first, mixture, totals)

        def ffn_forward(value, weights, gain, deadline):
            w_gate, w_up, w_down = weights
            normed_own, factor = normalize(value, gain)
            normed = both_cores(normed_own)
            gate = dot_nt(normed, w_gate)
            up = dot_nt(normed, w_up)
            hidden = (jax.nn.silu(gate) * up).astype(bf16)
            hidden = after(hidden, *deadline)
            return value + core_sum(dot_nn(hidden, w_down)), (value, factor, normed, gate, up, hidden)

        def ffn_backward(grad, weights, gain, saved, kinds, late):
            w_gate, w_up, w_down = weights
            value, factor, normed, gate, up, hidden = saved
            grad_full = both_cores(grad.astype(bf16))
            grad_hidden = dot_nt(grad_full, w_down)
            sig = jax.nn.sigmoid(gate)
            grad_gate = (grad_hidden * up * sig * (1.0 + gate * (1.0 - sig))).astype(bf16)
            grad_up = (grad_hidden * gate * sig).astype(bf16)
            grad_normed = core_sum(dot_nn(grad_gate, w_gate) + dot_nn(grad_up, w_up))
            lefts = after((grad_gate, grad_up, hidden), *late)
            pairs = tuple(zip(lefts, (normed, normed, grad_full)))
            grads = [sides(*pair, k) for pair, k in zip(pairs[:2], kinds)]
            grads.append((dot_tn(*pairs[2]).astype(bf16),))
            step, gain_grad = normalize_back(grad_normed, value, factor, gain)
            return grad + step, grads, gain_grad

        def attn_backward(grad, weights, gain, saved, extra, milestones, late):
            w_qk, w_value, w_out = weights
            value, factor, normed, normed_first, own, first, mixture, totals = saved
            grad_full = both_cores(grad.astype(bf16))
            grad_mixture = after(dot_nt(grad_full, w_out).astype(bf16), *milestones)
            gq, gk_first, gk, gv_first, gv = attend_back(
                own, first, bias, totals, mixture, grad_mixture, rope, extra
            )
            gk_first, gv_first = after((gk_first, gv_first), *late)
            w_query, w_key = jnp.split(w_qk, 2)
            operand = core_sum(dot_nn(gk_first, w_key) + dot_nn(gv_first, w_value)).astype(bf16)
            sent_raw = lax.ppermute(operand, "row", [(1, 0)])
            sent = flip_row(sent_raw).astype(f32)
            grad_normed = core_sum(dot_nn(gq, w_query) + dot_nn(gk, w_key) + dot_nn(gv, w_value))
            done = gq
            gq, gk, gv, gk_first, gv_first = after((gq, gk, gv, gk_first, gv_first), operand)
            grads = [
                dot_tn(gq, normed).astype(bf16),
                (dot_tn(gk, normed) + dot_tn(gk_first, normed_first)).astype(bf16),
                (dot_tn(gv, normed) + dot_tn(gv_first, normed_first)).astype(bf16),
                dot_tn(mixture, grad_full).astype(bf16),
            ]
            step, gain_grad = normalize_back(grad_normed + sent, value, factor, gain)
            return grad + step, grads, gain_grad, (gv_first, gv), (done, operand, sent_raw)

        cross_one = Crossing(attn_whole_one)
        attn_one = cross_one.complete((2, 1, 1), bias, cos_own, cos_first)
        crossings = []

        def start_ffn_one(normed_first):
            crossings.append(Crossing(ffn_whole_one, normed_first, *cross_one.both))
            return (*crossings[0].sides, attn_whole_two)

        residual, kept_attn_one = attn_forward(
            residual, attn_one, gains[0], None, start_ffn_one, *cross_one.both
        )
        own_one, first_one = kept_attn_one[4], kept_attn_one[5]
        cross_ffn = crossings[0]
        ffn_one = cross_ffn.complete((1, 1, 1))
        cross = Crossing(attn_whole_two, *cross_ffn.both)
        ffn_whole_two = gather_col(after(ffn_local_two, attn_whole_two))
        residual, kept_ffn_one = ffn_forward(residual, ffn_one, gains[1], (*cross.sides, ffn_whole_two))
        attn_two = cross.complete((2, 1, 1))
        residual = after(residual, *cross.both)
        ffn_two = []

        def start_ffn_two(normed_first):
            ffn_two.append(Crossing(ffn_whole_two, normed_first, *cross.both))
            return ffn_two[0].sides

        residual, kept_attn_two = attn_forward(
            residual, attn_two, gains[2], (own_one, first_one), start_ffn_two
        )
        ffn_two = ffn_two[0].complete((1, 1, 1))
        last_grad = spread([by_piece(out_grad)], residual)
        residual, kept_ffn_two = ffn_forward(residual, ffn_two, gains[3], (last_grad,))
        output = unspread(residual.astype(bf16))

        kinds = (True, False)

        def leaves(grads):
            return [a for pair in grads for a in pair]

        grad, g_ffn_two, gain_ffn_two = ffn_backward(
            last_grad.astype(f32), ffn_two, gains[3], kept_ffn_two, kinds, ()
        )
        r_ffn_two = return_ffn(*g_ffn_two)
        grad, g_attn_two, gain_attn_two, extra, done_attn_two = attn_backward(
            grad, attn_two, gains[2], kept_attn_two, None, (output, *leaves(g_ffn_two)), ()
        )
        r_attn_two = return_attn(g_attn_two)
        r_ffn_two.second((grad,))
        grad, g_ffn_one, gain_ffn_one = ffn_backward(
            grad, ffn_one, gains[1], kept_ffn_one, kinds, r_attn_two.sent
        )
        r_attn_two.second()
        p_ffn_two = last_ffn(r_ffn_two, grad, *leaves(g_ffn_one))
        r_ffn_one = return_ffn(*after(tuple(g_ffn_one), *r_attn_two.sent))
        grad, g_attn_one, gain_attn_one, _, (done_attn_one, operand, sent) = attn_backward(
            grad, attn_one, gains[0], kept_attn_one, extra,
            (*p_ffn_two, *leaves(g_ffn_one), *r_attn_two.sent), r_ffn_one.sent,
        )
        t_ffn_two = scatter(pack_parts(p_ffn_two))
        r_ffn_one.second((), (sent,))
        gain_rows = jnp.stack([gain_attn_one, gain_ffn_one, gain_attn_two, gain_ffn_two])
        gain_rows = jnp.pad(gain_rows, ((0, 12), (0, 0))).astype(bf16)
        r_attn_one = return_attn(g_attn_one, gain_rows)
        p_attn_two = pack_parts(r_attn_two.last())
        t_attn_two = scatter(p_attn_two)
        p_ffn_one = pack_parts(last_ffn(r_ffn_one, t_attn_two, t_ffn_two))
        t_ffn_one = scatter(p_ffn_one)
        r_attn_one.second((p_ffn_one,))
        p_attn_one = pack_parts(r_attn_one.last(t_ffn_one))
        t_attn_one = scatter(p_attn_one)
        b_ffn_two = finish_ffn(t_ffn_two, p_ffn_one)
        b_attn_two = finish_attn(t_attn_two, p_ffn_one)
        b_ffn_one = finish_ffn(t_ffn_one)
        b_attn_one, gain_sums = finish_attn(t_attn_one, spare=16)
        grad = after(grad, p_ffn_one)
        input_grad = unspread(grad.astype(bf16)).astype(f32)

        total = gain_sums[0, :4].astype(f32) + gain_sums[1, :4].astype(f32)
        total = turn(jnp.concatenate([total, swap_y(total)], axis=1), row, 1)
        total = lax.dynamic_slice_in_dim(total, col * quarter, quarter, 1)

        return (
            output, input_grad,
            total[0], *b_attn_one, total[1], *b_ffn_one,
            total[2], *b_attn_two, total[3], *b_ffn_two,
        )

    return body


def solution(mesh):
    devices = mesh.devices
    dp, rows, cols = devices.shape
    split = Mesh(devices.reshape(dp // 4, 2, 2, rows, cols), ("xo", "xi", "core", "row", "col"))
    dp_axes = ("xo", "xi", "core")
    token = P(None, dp_axes + ("row",), "col")
    group = P(None, dp_axes)
    gain = P("col")
    tall, wide = P("row", "col"), P("col", "row")
    layer = (gain, tall, tall, tall, wide, gain, tall, tall, wide)
    return jax.shard_map(
        make_body(cols),
        mesh=split,
        in_specs=(token, group, group) + layer + layer + (token,),
        out_specs=(token, token) + layer + layer,
        check_vma=False,
    )
```

```python
import jax
import jax.numpy as jnp
from jax import lax
from jax.experimental import pallas as pl
from jax.experimental.pallas import tpu as pltpu
from jax.sharding import Mesh, PartitionSpec as P

D = 1024
HEAD_DIM = 64
norm_eps = 1e-06
rope_base = 10000.0
scale = HEAD_DIM ** (-0.5)
bf16 = jnp.bfloat16
f32 = jnp.float32
PAIR = 2 * HEAD_DIM

SWAP = [(0, 1), (1, 0)]
VMEM = pltpu.CompilerParams(vmem_limit_bytes=56 << 20)


def dot_nt(left, right):
    return lax.dot_general(left, right, (((1,), (1,)), ((), ())), preferred_element_type=f32)


def dot_nn(left, right):
    return lax.dot_general(left, right, (((1,), (0,)), ((), ())), preferred_element_type=f32)


def dot_tn(left, right):
    return lax.dot_general(left, right, (((0,), (0,)), ((), ())), preferred_element_type=f32)


def swap_core(value):
    return lax.ppermute(value, "core", SWAP)


def swap_x(value):
    return lax.ppermute(value, "xi", SWAP)


def swap_y(value):
    return lax.ppermute(value, "row", SWAP)


def after(value, *milestones):
    return lax.optimization_barrier((value,) + milestones)[0] if milestones else value


def turn(array, by, axis):
    first, second = jnp.split(array, 2, axis=axis)
    return jnp.where(by == 0, array, jnp.concatenate([second, first], axis=axis))


def rotated(values, cos_ref, sin_ref):
    width = values.shape[1]
    half = HEAD_DIM // 2
    lane = lax.broadcasted_iota(jnp.int32, values.shape, 1) % HEAD_DIM
    other = jnp.where(
        lane < half, pltpu.roll(values, width - half, 1), pltpu.roll(values, half, 1)
    )
    cos, sin = cos_ref[...], sin_ref[...]
    times = width // PAIR
    if times > 1:
        cos = jnp.concatenate([cos] * times, axis=1)
        sin = jnp.concatenate([sin] * times, axis=1)
    return values * cos + other * sin


def project(normed, turned_weight, plain_weight, skip, cos, sin, mix):
    rows, block = normed.shape[0], 256
    turned = turned_weight.shape[0] // block - skip
    plain = plain_weight.shape[0] // block

    def kernel(n_ref, t_ref, p_ref, cos_ref, sin_ref, *rest):
        out_ref = rest[-1]
        step = pl.program_id(0)

        @pl.when(step < turned)
        def _():
            result = dot_nt(n_ref[...], t_ref[...])
            out_ref[...] = rotated(result, cos_ref, sin_ref).astype(bf16)

        @pl.when(step >= turned)
        def _():
            result = dot_nt(n_ref[...], p_ref[...])
            if mix is not None:
                result = 0.5 * result + 0.5 * rest[0][...].astype(f32)
            out_ref[...] = result.astype(bf16)

    whole = lambda shape: pl.BlockSpec(shape, lambda i: (0, 0))
    later = lambda i: jnp.maximum(i - turned, 0)
    in_specs = [
        whole((rows, D)),
        pl.BlockSpec((block, D), lambda i: (skip + jnp.minimum(i, turned - 1), 0)),
        pl.BlockSpec((block, D), lambda i: (later(i), 0)),
        whole((rows, PAIR)),
        whole((rows, PAIR)),
    ]
    operands = [normed, turned_weight, plain_weight, cos, sin]
    if mix is not None:
        before = mix.shape[1] // block - plain
        in_specs.append(pl.BlockSpec((rows, block), lambda i: (0, before + later(i))))
        operands.append(mix)
    return pl.pallas_call(
        kernel,
        grid=(turned + plain,),
        in_specs=in_specs,
        out_specs=pl.BlockSpec((rows, block), lambda i: (0, i)),
        out_shape=jax.ShapeDtypeStruct((rows, (turned + plain) * block), bf16),
        compiler_params=VMEM,
        cost_estimate=pl.CostEstimate(flops=1, bytes_accessed=1, transcendentals=0),
    )(*operands)


def assemble(whole, by_y, by_x, low, high, cols, counts):
    rows, width = whole.shape[0] // cols, whole.shape[1]
    size = rows // sum(counts)
    half = cols // 2

    def kernel(whole_ref, y_ref, x_ref, low_ref, high_ref, *outs):
        step = pl.program_id(0)
        at = 0
        for out, count in zip(outs, counts):
            for j in range(count):
                piece = slice(at, at + size)
                out[j, :, :width] = whole_ref[piece]
                out[j, :, width : 2 * width] = y_ref[piece]
                out[j, :, 2 * width : 3 * width] = x_ref[piece]

                @pl.when(step < half)
                def _():
                    out[j, :, 3 * width :] = low_ref[piece]

                @pl.when(step >= half)
                def _():
                    out[j, :, 3 * width :] = high_ref[piece]

                at += size

    block = lambda index: pl.BlockSpec((rows, width), index)
    outs = pl.pallas_call(
        kernel,
        grid=(cols,),
        in_specs=[
            block(lambda i: (i, 0)),
            block(lambda i: (i, 0)),
            block(lambda i: (i, 0)),
            block(lambda i: (jnp.minimum(i, half - 1), 0)),
            block(lambda i: (jnp.maximum(i - half, 0), 0)),
        ],
        out_specs=[pl.BlockSpec((c, size, 4 * width), lambda i: (0, i, 0)) for c in counts],
        out_shape=[jax.ShapeDtypeStruct((c, cols * size, 4 * width), bf16) for c in counts],
        compiler_params=VMEM,
        cost_estimate=pl.CostEstimate(flops=1, bytes_accessed=1, transcendentals=0),
    )(whole, by_y, by_x, low, high)
    return [o.reshape(-1, 4 * width) for o in outs]


def assemble_sides(whole_x, far_x, whole_y, far_y, cols, outs):
    rows, width = whole_x.shape[0] // cols, whole_x.shape[1]
    quarter = width // 2

    def kernel(x_ref, xf_ref, y_ref, yf_ref, *out_refs):
        for out, pieces in zip(out_refs, outs):
            for j, parts in enumerate(pieces):
                at = 0
                for over_x, first, size in parts:
                    here, there = slice(at, at + size), slice(first, first + size)
                    if over_x:
                        out[j, here, :width] = x_ref[there]
                        out[j, here, width:] = xf_ref[there]
                    else:
                        for q, ref in enumerate((y_ref, yf_ref, y_ref, yf_ref)):
                            side = slice(q // 2 * quarter, (q // 2 + 1) * quarter)
                            out[j, here, q * quarter : (q + 1) * quarter] = ref[there, side]
                    at += size

    sizes = [sum(p[2] for p in pieces[0]) for pieces in outs]
    results = pl.pallas_call(
        kernel,
        grid=(cols,),
        in_specs=[pl.BlockSpec((rows, width), lambda i: (i, 0))] * 4,
        out_specs=[
            pl.BlockSpec((len(p), n, 2 * width), lambda i: (0, i, 0)) for p, n in zip(outs, sizes)
        ],
        out_shape=[
            jax.ShapeDtypeStruct((len(p), cols * n, 2 * width), bf16) for p, n in zip(outs, sizes)
        ],
        compiler_params=VMEM,
        cost_estimate=pl.CostEstimate(flops=1, bytes_accessed=1, transcendentals=0),
    )(whole_x, far_x, whole_y, far_y)
    return [r.reshape(-1, 2 * width) for r in results]


def pair_block(rows, first):
    return pl.BlockSpec((rows, PAIR), lambda i: (0, first + i))


def attend(own, first, bias):
    n, m = own.shape[0], first.shape[0]
    width = own.shape[1] // 3
    pairs = width // PAIR

    def kernel(q_ref, ka_ref, kb_ref, va_ref, vb_ref, bias_ref, out_ref, total_ref):
        for h in range(2):
            lanes = slice(h * HEAD_DIM, (h + 1) * HEAD_DIM)
            keys = jnp.concatenate([ka_ref[:, lanes], kb_ref[:, lanes]], axis=0)
            values = jnp.concatenate([va_ref[:, lanes], vb_ref[:, lanes]], axis=0)
            scores = dot_nt(keys, q_ref[:, lanes]) * scale + bias_ref[...]
            peak = jnp.max(scores, axis=0, keepdims=True)
            weight = jnp.exp(scores - peak)
            total = jnp.sum(weight, axis=0, keepdims=True)
            mixed = dot_tn(values, weight.astype(bf16))
            out_ref[:, lanes] = (mixed / total).T.astype(bf16)
            total_ref[0, h, :, :] = peak + jnp.log(total)

    return pl.pallas_call(
        kernel,
        grid=(pairs,),
        in_specs=[
            pair_block(n, 0),
            pair_block(m, 0),
            pair_block(n, pairs),
            pair_block(m, pairs),
            pair_block(n, 2 * pairs),
            pl.BlockSpec((m + n, n), lambda i: (0, 0)),
        ],
        out_specs=[pair_block(n, 0), pl.BlockSpec((1, 2, 1, n), lambda i: (i, 0, 0, 0))],
        out_shape=[
            jax.ShapeDtypeStruct((n, width), bf16),
            jax.ShapeDtypeStruct((pairs, 2, 1, n), f32),
        ],
        compiler_params=VMEM,
        cost_estimate=pl.CostEstimate(
            flops=1, bytes_accessed=1, transcendentals=0
        ),
    )(own, first, own, first, own, bias)


def attend_back(own, first, bias, totals, mixture, grad_out, tables, extra):
    n, m = own.shape[0], first.shape[0]
    width = own.shape[1] // 3
    pairs = width // PAIR
    cos_own, sin_own, cos_first, sin_first = tables

    def kernel(
        q_ref, ka_ref, kb_ref, va_ref, vb_ref, bias_ref, total_ref, mix_ref, go_ref,
        co_ref, so_ref, cf_ref, sf_ref, *rest
    ):
        gq_ref, gka_ref, gkb_ref, gva_ref, gvb_ref = rest[-5:]
        queries_back, keys_back, values_back = [], [], []
        for h in range(2):
            lanes = slice(h * HEAD_DIM, (h + 1) * HEAD_DIM)
            keys = jnp.concatenate([ka_ref[:, lanes], kb_ref[:, lanes]], axis=0)
            values = jnp.concatenate([va_ref[:, lanes], vb_ref[:, lanes]], axis=0)
            queries, grads = q_ref[:, lanes], go_ref[:, lanes]
            inner = jnp.sum(
                grads.astype(f32) * mix_ref[:, lanes].astype(f32), axis=1, keepdims=True
            )
            inner = jnp.broadcast_to(inner, (n, 128)).T[:1]
            scores = dot_nt(keys, queries) * scale + bias_ref[...]
            weight = jnp.exp(scores - total_ref[0, h, :, :])
            grad_weight = dot_nt(values, grads)
            grad_scores = (weight * (grad_weight - inner)).astype(bf16)
            values_back.append(dot_nn(weight.astype(bf16), grads))
            keys_back.append(dot_nn(grad_scores, queries))
            queries_back.append(dot_tn(keys, grad_scores).T)
        side = lambda pair: jnp.concatenate(pair, axis=1)
        gq_ref[...] = rotated(side(queries_back) * scale, co_ref, so_ref).astype(bf16)
        gk, gv = side(keys_back) * scale, side(values_back)
        gka_ref[...] = rotated(gk[:m], cf_ref, sf_ref).astype(bf16)
        gkb_ref[...] = rotated(gk[m:], co_ref, so_ref).astype(bf16)
        if extra is None:
            gva_ref[...] = (0.5 * gv[:m].astype(bf16).astype(f32)).astype(bf16)
            gvb_ref[...] = (0.5 * gv[m:].astype(bf16).astype(f32)).astype(bf16)
        else:
            gva_ref[...] = (gv[:m] + rest[0][...].astype(f32)).astype(bf16)
            gvb_ref[...] = (gv[m:] + rest[1][...].astype(f32)).astype(bf16)

    whole = lambda shape: pl.BlockSpec(shape, lambda i: (0, 0))
    in_specs = [
        pair_block(n, 0),
        pair_block(m, 0),
        pair_block(n, pairs),
        pair_block(m, pairs),
        pair_block(n, 2 * pairs),
        whole((m + n, n)),
        pl.BlockSpec((1, 2, 1, n), lambda i: (i, 0, 0, 0)),
        pair_block(n, 0),
        pair_block(n, 0),
        whole((n, PAIR)),
        whole((n, PAIR)),
        whole((m, PAIR)),
        whole((m, PAIR)),
    ]
    operands = [own, first, own, first, own, bias, totals, mixture, grad_out]
    operands += [cos_own, -sin_own, cos_first, -sin_first]
    if extra is not None:
        in_specs += [pair_block(m, 0), pair_block(n, 0)]
        operands += list(extra)
    shape = lambda rows: jax.ShapeDtypeStruct((rows, width), bf16)
    return pl.pallas_call(
        kernel,
        grid=(pairs,),
        in_specs=in_specs,
        out_specs=[pair_block(r, 0) for r in (n, m, n, m, n)],
        out_shape=[shape(r) for r in (n, m, n, m, n)],
        compiler_params=VMEM,
        cost_estimate=pl.CostEstimate(
            flops=1, bytes_accessed=1, transcendentals=0
        ),
    )(*operands)


def make_body(col_count):
    ring_up = [(i, (i + 1) % col_count) for i in range(col_count)]
    rounds = []
    for k in range(col_count):
        pairs = []
        for core in range(2):
            for col in range(col_count):
                j = col ^ k
                pairs.append((core * col_count + col, (j & 1) * col_count + (j & ~1) + core))
        rounds.append(pairs)
    backs = [[(b, a) for a, b in pairs] for pairs in rounds]

    def body(
        tokens, segment_ids, prompt_reach,
        attn_gain_1, query_weight_1, key_weight_1, value_weight_1, out_weight_1,
        ffn_gain_1, gate_weight_1, up_weight_1, down_weight_1,
        attn_gain_2, query_weight_2, key_weight_2, value_weight_2, out_weight_2,
        ffn_gain_2, gate_weight_2, up_weight_2, down_weight_2,
        out_grad,
    ):
        xo_count = lax.axis_size("xo")
        xi, core = lax.axis_index("xi"), lax.axis_index("core")
        row, col = lax.axis_index("row"), lax.axis_index("col")
        chip_rows = tokens.shape[1]
        own_rows = chip_rows // 2
        quarter = tokens.shape[2]
        half_d = 2 * quarter
        slot = (col // 2) * 2 + core

        def place(p):
            return (2 * row + xi) ^ (0, 2, 1, 3)[p]

        gains = jnp.stack([attn_gain_1, ffn_gain_1, attn_gain_2, ffn_gain_2])
        high = gains.astype(bf16)
        middle = (gains - high.astype(f32)).astype(bf16)
        low = (gains - high.astype(f32) - middle.astype(f32)).astype(bf16)
        small = jnp.concatenate([high, middle, low, jnp.zeros_like(high)], axis=0)
        def unspread(array):
            pieces = jnp.stack([array[:, p * quarter : (p + 1) * quarter] for p in (0, 1, 2, 3)])
            got = []
            for k in range(col_count):
                p = slot ^ k ^ (2 * row + xi)
                p = (p & 1) * 2 + (p >> 1)
                piece = lax.dynamic_index_in_dim(pieces, p, 0, keepdims=False)
                got.append(lax.ppermute(piece, ("core", "col"), backs[k]))
            got = jnp.stack(got)
            got = jnp.concatenate(
                [lax.dynamic_index_in_dim(got, j ^ col, 0) for j in range(col_count)], axis=0
            )
            return got.reshape(tokens.shape)

        def units(block, transposed):
            if transposed:
                size = block.shape[1] // 2
                block = lax.dynamic_slice_in_dim(block, core * size, size, 1).T
            else:
                size = block.shape[0] // 2
                block = lax.dynamic_slice_in_dim(block, core * size, size, 0)
            return turn(block, xi, 1)

        def stack_attn(w_query, w_key, w_value, w_out):
            return jnp.concatenate(
                [units(w_query, True), units(w_key, True), units(w_value, True), units(w_out, False)]
            )

        def gather_col(block):
            return lax.all_gather(block, "col", axis=0, tiled=True)

        class Crossing:
            def __init__(self, whole, *milestones):
                self.whole = after(whole, *milestones)
                self.sides = (swap_x(self.whole), swap_y(self.whole))

            def complete(self, counts, *milestones):
                by_x, by_y = after(self.sides, *milestones)
                half = by_x.shape[0] // 2
                self.both = (swap_x(by_y[:half]), swap_y(by_x[half:]))
                return assemble(self.whole, by_y, by_x, *self.both, col_count, counts)

        def near_x(block):
            return block[:, :quarter]

        def local_ffn(w_gate, w_up, w_down):
            blocks = (units(w_gate, True), units(w_up, True), units(w_down, False))
            return jnp.concatenate([near_x(b) for b in blocks])

        attn_local_one = near_x(
            stack_attn(query_weight_1, key_weight_1, value_weight_1, out_weight_1)
        )
        ffn_local_one = local_ffn(gate_weight_1, up_weight_1, down_weight_1)
        gate_two, up_two = units(gate_weight_2, True), units(up_weight_2, True)
        down_two = units(down_weight_2, False)
        wide, low = gate_two.shape[0], gate_two.shape[0] // 2
        tall = query_weight_2.shape[1] // 2
        qk_two = jnp.concatenate([units(query_weight_2, True), units(key_weight_2, True)])
        attn_y_two = jnp.concatenate([units(value_weight_2, True), units(out_weight_2, False)])
        ffn_y_two = jnp.concatenate([up_two, down_two[low:]])
        own = jnp.concatenate([near_x(qk_two), near_x(gate_two), near_x(down_two[:low])])
        both_rows = jnp.concatenate([own, swap_y(own)], axis=1)
        attn_x_two, ffn_x_two = both_rows[: 2 * tall], both_rows[2 * tall :]
        half = attn_local_one.shape[0] // 2
        qk_whole_one = gather_col(attn_local_one[:half])
        vo_whole_one = gather_col(after(attn_local_one[half:], qk_whole_one))
        attn_whole_one = jnp.concatenate(
            [w.reshape(col_count, -1, quarter) for w in (qk_whole_one, vo_whole_one)], axis=1
        ).reshape(-1, quarter)
        ffn_whole_one = gather_col(after(ffn_local_one, vo_whole_one))
        attn_whole_two = gather_col(after(jnp.concatenate([attn_x_two, attn_y_two]), ffn_whole_one))

        def halves(whole):
            whole = whole.reshape(col_count, 2, -1, half_d)
            return whole[:, 0].reshape(-1, half_d), whole[:, 1].reshape(-1, half_d)

        def spread(arrays, *milestones):
            pieces = after(jnp.concatenate(arrays, axis=1), *milestones)
            got = []
            for k in range(col_count):
                piece = lax.dynamic_index_in_dim(pieces, col ^ k, 0, keepdims=False)
                got.append(lax.ppermute(piece, ("core", "col"), rounds[k]))
            got = jnp.stack(got)
            return jnp.concatenate(
                [
                    lax.dynamic_index_in_dim(got, place(p) ^ slot, 0, keepdims=False)
                    for p in range(col_count)
                ],
                axis=1,
            )

        by_piece = lambda array: array.reshape(col_count, own_rows, quarter)
        got = spread(
            [by_piece(tokens), jnp.broadcast_to(small[None], (col_count,) + small.shape)],
            vo_whole_one,
        )
        residual = got[:own_rows].astype(f32)
        small = got[own_rows:].astype(f32)
        gains = small[0:4] + small[4:8] + small[8:12]

        both = jnp.stack([segment_ids, prompt_reach])
        both = jnp.where(core == col % 2, both, swap_core(both))
        both = lax.dynamic_index_in_dim(both, col // 2, 1, keepdims=False)
        segments, reach = both[0], both[1]
        group_len = segments.shape[0]
        size_0 = jnp.sum((segments == 0).astype(jnp.int32))
        size_1 = jnp.sum((segments == 1).astype(jnp.int32))
        starts = jnp.where(segments == 0, 0, jnp.where(segments == 1, size_0, size_0 + size_1))
        index = jnp.arange(group_len, dtype=jnp.int32)
        positions = index - starts + reach

        def mine(array):
            return turn(lax.dynamic_slice_in_dim(array, row * chip_rows, chip_rows, 0), core, 0)

        def leading(array):
            return turn(array[:chip_rows], core, 0)

        inverse = rope_base ** (-(jnp.arange(HEAD_DIM // 2, dtype=f32) * 2.0) / HEAD_DIM)

        def tables(position):
            angles = position.astype(f32)[:, None] * inverse[None, :]
            cosine, sine = jnp.cos(angles), jnp.sin(angles)
            return (
                jnp.concatenate([cosine] * 4, axis=1),
                jnp.concatenate([-sine, sine, -sine, sine], axis=1),
            )

        cos_own, sin_own = tables(mine(positions))
        cos_first, sin_first = tables(leading(positions))
        rope = (cos_own, sin_own, cos_first, sin_first)
        query_index, query_seg, query_reach = mine(index), mine(segments), mine(reach)
        first_index = jnp.where(row == 0, group_len, leading(index))
        key_index = jnp.concatenate([first_index, query_index])
        key_seg = jnp.concatenate([leading(segments), query_seg])
        allowed = (query_seg[None, :] == key_seg[:, None]) & (
            key_index[:, None] <= query_index[None, :]
        ) | (key_index[:, None] < query_reach[None, :])
        bias = jnp.where(allowed, 0.0, -1e30).astype(f32)

        def over_xo(total):
            if xo_count > 1:
                total = lax.psum(total, "xo")
            return total

        def scatter_col(array):
            return lax.psum_scatter(array, "col", scatter_dimension=0, tiled=True)

        def add(left, right):
            return (left.astype(f32) + right.astype(f32)).astype(bf16)

        def both_blocks(block):
            return jnp.stack([block, swap_core(block)])

        def finish(pair, at, size, transposed):
            pair = turn(pair[:, at : at + size].reshape(2 * size, half_d), core, 0)
            return (pair.T if transposed else pair).astype(f32)

        def quarters(array, *places):
            if len(places) == 1:
                return array[:, places[0] * quarter : (places[0] + 1) * quarter]
            return jnp.concatenate(
                [array[:, p * quarter : (p + 1) * quarter] for p in places], axis=1
            )

        class Return:
            def __init__(self, by_x, by_y):
                stack = lambda parts: jnp.concatenate(parts) if len(parts) > 1 else parts[0]
                self.near = [stack([n for n, _ in parts]) for parts in (by_x, by_y)]
                far = [stack([f for _, f in parts]) for parts in (by_x, by_y)]
                self.sent = (swap_x(far[0]), swap_y(far[1]))

            def second(self, milestones=(), before_y=()):
                sent = after(self.sent, *milestones)
                totals = [add(a, b) for a, b in zip(self.near, sent)]
                self.near = [t[:, :quarter] for t in totals]
                far = [t[:, quarter:] for t in totals]
                self.sent = (swap_y(after(far[0], *before_y)), swap_x(far[1]))

            def last(self, *milestones):
                sent = after(self.sent, *milestones)
                return [add(a, b) for a, b in zip(self.near, sent)]

        def return_sides(near_x, far_x, near_y, far_y):
            return near_x, swap_x(far_x), near_y, swap_y(far_y)

        def scatter_sides(sides, *milestones):
            near_x, sent_x, near_y, sent_y = sides
            sent_x, sent_y = after((sent_x, sent_y), *milestones)
            parts = [
                add(n, r).reshape(col_count, -1, half_d)
                for n, r in ((near_x, sent_x), (near_y, sent_y))
            ]
            packed = jnp.concatenate(parts, axis=1).reshape(-1, half_d)
            return packed, over_xo(scatter_col(packed))

        def settle_sides(total, *milestones):
            total = after(total, *milestones)
            half = total.shape[0] // 2
            first, second = total[:half], turn(total[half:], xi, 1)
            first = add(first[:, :quarter], swap_y(first[:, quarter:]))
            first = turn(jnp.concatenate([first, swap_x(first)], axis=1), xi, 1)
            return first, add(second, swap_x(second))

        def by_col(array):
            return array.reshape(col_count, -1, array.shape[-1])

        def flat(array):
            return array.reshape(-1, array.shape[-1])

        def return_ffn_two(gate, up, down):
            down = by_col(down[0])
            part = lambda rows, *places: quarters(flat(rows), *places)
            lower, upper = down[:, :low], down[:, low:]
            join = lambda a, b: flat(jnp.concatenate([by_col(a), by_col(b)], axis=1))
            return return_sides(
                join(gate[0], part(lower, 0, 1)), join(gate[1], part(lower, 2, 3)),
                join(up[0], part(upper, 0, 2)), join(up[1], part(upper, 1, 3)),
            )

        def return_attn_two(grads):
            qk = flat(jnp.concatenate([by_col(g) for g in grads[:2]], axis=1))
            vo = flat(jnp.concatenate([by_col(g) for g in grads[2:]], axis=1))
            return return_sides(
                quarters(qk, 0, 1), quarters(qk, 2, 3), quarters(vo, 0, 2), quarters(vo, 1, 3)
            )

        def finish_rows(total, sizes):
            pair, blocks, at = both_blocks(total), [], 0
            for size, transposed in sizes:
                blocks.append(finish(pair, at, size, transposed))
                at += size
            return blocks

        def finish_ffn_two(total, *milestones):
            first, second = settle_sides(total, *milestones)
            rows = [first[:wide], second[:wide], first[wide:], second[wide:]]
            return finish_rows(
                jnp.concatenate(rows), ((wide, True), (wide, True), (wide, False))
            )

        def finish_attn_two(total, *milestones):
            total = jnp.concatenate(settle_sides(total, *milestones))
            return finish_rows(
                total, ((tall, True), (tall, True), (tall, True), (tall, False))
            )

        def pack_parts(parts):
            packed = [p.reshape(col_count, -1, quarter) for p in parts]
            return jnp.concatenate(packed, axis=1).reshape(-1, quarter)

        def scatter(packed):
            return over_xo(scatter_col(packed))

        def return_ffn(gate, up, down):
            half = down[0].shape[0] // 2
            low = (quarters(down[0], 0, 1)[:half], quarters(down[0], 2, 3)[:half])
            high = (quarters(down[0], 0, 2)[half:], quarters(down[0], 1, 3)[half:])
            return Return([gate, low], [up, high])

        def last_ffn(returned, *milestones):
            first, second = returned.last(*milestones)
            rows = first.shape[0] * 2 // 3
            return [first[:rows], second[:rows], jnp.concatenate([first[rows:], second[rows:]])]

        def sides(left, right, x_first):
            stay, go = ((0, 1), (2, 3)) if x_first else ((0, 2), (1, 3))
            return (
                dot_tn(left, quarters(right, *stay)).astype(bf16),
                dot_tn(left, quarters(right, *go)).astype(bf16),
            )

        def finish_all(total, kinds, spare=0):
            total = turn(jnp.concatenate([total, swap_x(total)], axis=1), xi, 1)
            pair = both_blocks(total)
            size = (total.shape[0] - spare) // len(kinds)
            blocks = [finish(pair, j * size, size, kind) for j, kind in enumerate(kinds)]
            return (blocks, pair[:, len(kinds) * size :]) if spare else blocks

        def finish_ffn(total, *milestones):
            return finish_all(after(total, *milestones), (True, True, False))

        def finish_attn(total, *milestones, spare=0):
            return finish_all(after(total, *milestones), (True, True, True, False), spare)

        def return_attn(grads, extra_rows=None):
            pack = lambda pair: jnp.concatenate(
                [g.reshape(col_count, -1, D) for g in pair], axis=1
            ).reshape(-1, D)
            rest = list(grads[2:])
            if extra_rows is not None:
                rest.append(jnp.concatenate([extra_rows] * col_count))
            qk, vo = pack(grads[:2]), pack(rest)
            pairs = [
                (quarters(qk, 0, 1), quarters(qk, 2, 3)),
                (quarters(vo, 0, 2), quarters(vo, 1, 3)),
            ]
            return Return(pairs[:1], pairs[1:])

        def both_cores(own):
            return jnp.concatenate([own, swap_core(own)], axis=0)

        def core_sum(partial):
            sent = swap_core(partial[own_rows:].astype(bf16))
            return partial[:own_rows] + sent.astype(f32)

        def normalize(value, gain):
            factor = lax.rsqrt(jnp.mean(value * value, axis=1, keepdims=True) + norm_eps)
            return (value * factor * gain[None, :]).astype(bf16), factor

        def normalize_back(grad_normed, value, factor, gain):
            unit = value * factor
            gain_grad = jnp.sum(grad_normed * unit, axis=0)
            grad_unit = grad_normed * gain[None, :]
            inner = jnp.mean(grad_unit * unit, axis=1, keepdims=True)
            return factor * (grad_unit - unit * inner), gain_grad

        def flip_row(array):
            return jnp.concatenate(
                [array[:, p * quarter : (p + 1) * quarter] for p in (1, 0, 3, 2)], axis=1
            )

        def attn_forward(value, weights, gain, mix, start, *milestones):
            w_qk, w_value, w_out = weights
            normed_own, factor = normalize(value, gain)
            normed_first = both_cores(flip_row(lax.ppermute(after(normed_own, *milestones), "row", [(0, 1)])))
            normed = both_cores(normed_own)
            skip = w_qk.shape[0] // 512
            own = project(normed, w_qk, w_value, 0, cos_own, sin_own, mix and mix[0])
            first = project(normed_first, w_qk, w_value, skip, cos_first, sin_first, mix and mix[1])
            mixture, totals = attend(own, first, bias)
            mixture = after(mixture, *start(normed_first))
            result = value + core_sum(dot_nn(mixture, w_out))
            return result, (value, factor, normed, normed_first, own, first, mixture, totals)

        def ffn_forward(value, weights, gain, deadline):
            w_gate, w_up, w_down = weights
            normed_own, factor = normalize(value, gain)
            normed = both_cores(normed_own)
            gate = dot_nt(normed, w_gate)
            up = dot_nt(normed, w_up)
            hidden = (jax.nn.silu(gate) * up).astype(bf16)
            hidden = after(hidden, *deadline)
            return value + core_sum(dot_nn(hidden, w_down)), (value, factor, normed, gate, up, hidden)

        def ffn_backward(grad, weights, gain, saved, kinds, late):
            w_gate, w_up, w_down = weights
            value, factor, normed, gate, up, hidden = saved
            grad_full = both_cores(grad.astype(bf16))
            grad_hidden = dot_nt(grad_full, w_down)
            sig = jax.nn.sigmoid(gate)
            grad_gate = (grad_hidden * up * sig * (1.0 + gate * (1.0 - sig))).astype(bf16)
            grad_up = (grad_hidden * gate * sig).astype(bf16)
            grad_normed = core_sum(dot_nn(grad_gate, w_gate) + dot_nn(grad_up, w_up))
            lefts = (grad_gate, grad_up, after(hidden, *late))
            pairs = tuple(zip(lefts, (normed, normed, grad_full)))
            grads = [sides(*pair, k) for pair, k in zip(pairs[:2], kinds)]
            grads.append((dot_tn(*pairs[2]).astype(bf16),))
            step, gain_grad = normalize_back(grad_normed, value, factor, gain)
            return grad + step, grads, gain_grad

        def attn_backward(grad, weights, gain, saved, extra, milestones, late):
            w_qk, w_value, w_out = weights
            value, factor, normed, normed_first, own, first, mixture, totals = saved
            grad_full = both_cores(grad.astype(bf16))
            grad_mixture = after(dot_nt(grad_full, w_out).astype(bf16), *milestones)
            gq, gk_first, gk, gv_first, gv = attend_back(
                own, first, bias, totals, mixture, grad_mixture, rope, extra
            )
            gk_first, gv_first = after((gk_first, gv_first), *late)
            w_query, w_key = jnp.split(w_qk, 2)
            operand = core_sum(dot_nn(gk_first, w_key) + dot_nn(gv_first, w_value)).astype(bf16)
            sent_raw = lax.ppermute(operand, "row", [(1, 0)])
            sent = flip_row(sent_raw).astype(f32)
            grad_normed = core_sum(dot_nn(gq, w_query) + dot_nn(gk, w_key) + dot_nn(gv, w_value))
            done = gq
            gq, gk, gv, gk_first, gv_first = after((gq, gk, gv, gk_first, gv_first), operand)
            grads = [
                dot_tn(gq, normed).astype(bf16),
                (dot_tn(gk, normed) + dot_tn(gk_first, normed_first)).astype(bf16),
                (dot_tn(gv, normed) + dot_tn(gv_first, normed_first)).astype(bf16),
                dot_tn(mixture, grad_full).astype(bf16),
            ]
            step, gain_grad = normalize_back(grad_normed + sent, value, factor, gain)
            return grad + step, grads, gain_grad, (gv_first, gv), (done, operand, sent_raw)

        cross_one = Crossing(attn_whole_one)
        attn_one = cross_one.complete((2, 1, 1), bias, cos_own, cos_first)
        crossings = []

        def start_ffn_one(normed_first):
            crossings.append(Crossing(ffn_whole_one, normed_first, *cross_one.both))
            return (*crossings[0].sides, attn_whole_two)

        residual, kept_attn_one = attn_forward(
            residual, attn_one, gains[0], None, start_ffn_one, *cross_one.both
        )
        own_one, first_one = kept_attn_one[4], kept_attn_one[5]
        ffn_whole_two = gather_col(after(jnp.concatenate([ffn_x_two, ffn_y_two]), attn_whole_two))
        cross_ffn = crossings[0]
        ffn_one = cross_ffn.complete((1, 1, 1))
        wx, wy = halves(after(attn_whole_two, *cross_ffn.both))
        far = (swap_x(wx), swap_y(wy))
        residual, kept_ffn_one = ffn_forward(residual, ffn_one, gains[1], far)
        attn_two = assemble_sides(
            wx, far[0], wy, far[1], col_count,
            (
                (((True, 0, tall),), ((True, tall, tall),)),
                (((False, 0, tall),),),
                (((False, tall, tall),),),
            ),
        )
        ffn_sides, grads = [], []

        def start_ffn_two(normed_first):
            wx, wy = after(halves(ffn_whole_two), normed_first, *far)
            ffn_sides.extend((wx, swap_x(wx), wy, swap_y(wy)))
            grads.append(spread([by_piece(out_grad)], normed_first))
            return ffn_sides[1], ffn_sides[3], grads[0]

        residual, kept_attn_two = attn_forward(
            residual, attn_two, gains[2], (own_one, first_one), start_ffn_two
        )
        ffn_two = assemble_sides(
            *ffn_sides, col_count,
            (
                (((True, 0, wide),),),
                (((False, 0, wide),),),
                (((True, wide, low), (False, wide, low)),),
            ),
        )
        last_grad = grads[0]
        residual, kept_ffn_two = ffn_forward(residual, ffn_two, gains[3], ())
        output = unspread(residual.astype(bf16))

        kinds = (True, False)

        def leaves(grads):
            return [a for pair in grads for a in pair]

        grad, g_ffn_two, gain_ffn_two = ffn_backward(
            last_grad.astype(f32), ffn_two, gains[3], kept_ffn_two, kinds, (output,)
        )
        r_ffn_two = return_ffn_two(*g_ffn_two)
        grad, g_attn_two, gain_attn_two, extra, done_attn_two = attn_backward(
            grad, attn_two, gains[2], kept_attn_two, None, tuple(leaves(g_ffn_two)), (r_ffn_two[1], r_ffn_two[3])
        )
        r_attn_two = return_attn_two(g_attn_two)
        sent_attn_two = (r_attn_two[1], r_attn_two[3])
        grad, g_ffn_one, gain_ffn_one = ffn_backward(
            grad, ffn_one, gains[1], kept_ffn_one, kinds, ()
        )
        r_ffn_one = return_ffn(*after(tuple(g_ffn_one), *sent_attn_two))
        p_ffn_two, t_ffn_two = scatter_sides(r_ffn_two, *leaves(g_ffn_one))
        p_attn_two, t_attn_two = scatter_sides(r_attn_two, *leaves(g_ffn_one))
        grad, g_attn_one, gain_attn_one, _, (done_attn_one, operand, sent) = attn_backward(
            grad, attn_one, gains[0], kept_attn_one, extra,
            (p_attn_two, p_ffn_two, *leaves(g_ffn_one)), r_ffn_one.sent,
        )
        r_ffn_one.second((), (sent,))
        gain_rows = jnp.stack([gain_attn_one, gain_ffn_one, gain_attn_two, gain_ffn_two])
        gain_rows = jnp.pad(gain_rows, ((0, 12), (0, 0))).astype(bf16)
        r_attn_one = return_attn(g_attn_one, gain_rows)
        p_ffn_one = pack_parts(last_ffn(r_ffn_one, t_attn_two, t_ffn_two, *r_attn_one.near))
        t_ffn_one = scatter(p_ffn_one)
        r_attn_one.second((p_ffn_one,))
        b_ffn_two = finish_ffn_two(t_ffn_two, p_ffn_one)
        b_attn_two = finish_attn_two(t_attn_two, p_ffn_one)
        p_attn_one = pack_parts(r_attn_one.last(t_ffn_one, *b_ffn_two, *b_attn_two))
        t_attn_one = scatter(p_attn_one)
        b_ffn_one = finish_ffn(t_ffn_one)
        b_attn_one, gain_sums = finish_attn(t_attn_one, spare=16)
        grad = after(grad, p_ffn_one)
        input_grad = unspread(grad.astype(bf16)).astype(f32)

        total = gain_sums[0, :4].astype(f32) + gain_sums[1, :4].astype(f32)
        total = turn(jnp.concatenate([total, swap_y(total)], axis=1), row, 1)
        total = lax.dynamic_slice_in_dim(total, col * quarter, quarter, 1)

        return (
            output, input_grad,
            total[0], *b_attn_one, total[1], *b_ffn_one,
            total[2], *b_attn_two, total[3], *b_ffn_two,
        )

    return body


def solution(mesh):
    devices = mesh.devices
    dp, rows, cols = devices.shape
    split = Mesh(devices.reshape(dp // 4, 2, 2, rows, cols), ("xo", "xi", "core", "row", "col"))
    dp_axes = ("xo", "xi", "core")
    token = P(None, dp_axes + ("row",), "col")
    group = P(None, dp_axes)
    gain = P("col")
    tall, wide = P("row", "col"), P("col", "row")
    layer = (gain, tall, tall, tall, wide, gain, tall, tall, wide)
    return jax.shard_map(
        make_body(cols),
        mesh=split,
        in_specs=(token, group, group) + layer + layer + (token,),
        out_specs=(token, token) + layer + layer,
        check_vma=False,
    )
```

```python
import jax
import jax.numpy as jnp
from jax import lax
from jax.experimental import pallas as pl
from jax.experimental.pallas import tpu as pltpu
from jax.sharding import Mesh, PartitionSpec as P

D = 1024
HEAD_DIM = 64
norm_eps = 1e-06
rope_base = 10000.0
scale = HEAD_DIM ** (-0.5)
bf16 = jnp.bfloat16
f32 = jnp.float32
PAIR = 2 * HEAD_DIM

SWAP = [(0, 1), (1, 0)]
VMEM = pltpu.CompilerParams(vmem_limit_bytes=56 << 20)


def dot_nt(left, right):
    return lax.dot_general(left, right, (((1,), (1,)), ((), ())), preferred_element_type=f32)


def dot_nn(left, right):
    return lax.dot_general(left, right, (((1,), (0,)), ((), ())), preferred_element_type=f32)


def dot_tn(left, right):
    return lax.dot_general(left, right, (((0,), (0,)), ((), ())), preferred_element_type=f32)


def swap_core(value):
    return lax.ppermute(value, "core", SWAP)


def swap_x(value):
    return lax.ppermute(value, "xi", SWAP)


def swap_y(value):
    return lax.ppermute(value, "row", SWAP)


def after(value, *milestones):
    return lax.optimization_barrier((value,) + milestones)[0] if milestones else value


def turn(array, by, axis):
    first, second = jnp.split(array, 2, axis=axis)
    return jnp.where(by == 0, array, jnp.concatenate([second, first], axis=axis))


def rotated(values, cos_ref, sin_ref):
    width = values.shape[1]
    half = HEAD_DIM // 2
    lane = lax.broadcasted_iota(jnp.int32, values.shape, 1) % HEAD_DIM
    other = jnp.where(
        lane < half, pltpu.roll(values, width - half, 1), pltpu.roll(values, half, 1)
    )
    cos, sin = cos_ref[...], sin_ref[...]
    times = width // PAIR
    if times > 1:
        cos = jnp.concatenate([cos] * times, axis=1)
        sin = jnp.concatenate([sin] * times, axis=1)
    return values * cos + other * sin


def project(normed, turned_weight, plain_weight, skip, cos, sin, mix):
    rows, block = normed.shape[0], 256
    turned = turned_weight.shape[0] // block - skip
    plain = plain_weight.shape[0] // block

    def kernel(n_ref, t_ref, p_ref, cos_ref, sin_ref, *rest):
        out_ref = rest[-1]
        step = pl.program_id(0)

        @pl.when(step < turned)
        def _():
            result = dot_nt(n_ref[...], t_ref[...])
            out_ref[...] = rotated(result, cos_ref, sin_ref).astype(bf16)

        @pl.when(step >= turned)
        def _():
            result = dot_nt(n_ref[...], p_ref[...])
            if mix is not None:
                result = 0.5 * result + 0.5 * rest[0][...].astype(f32)
            out_ref[...] = result.astype(bf16)

    whole = lambda shape: pl.BlockSpec(shape, lambda i: (0, 0))
    later = lambda i: jnp.maximum(i - turned, 0)
    in_specs = [
        whole((rows, D)),
        pl.BlockSpec((block, D), lambda i: (skip + jnp.minimum(i, turned - 1), 0)),
        pl.BlockSpec((block, D), lambda i: (later(i), 0)),
        whole((rows, PAIR)),
        whole((rows, PAIR)),
    ]
    operands = [normed, turned_weight, plain_weight, cos, sin]
    if mix is not None:
        before = mix.shape[1] // block - plain
        in_specs.append(pl.BlockSpec((rows, block), lambda i: (0, before + later(i))))
        operands.append(mix)
    return pl.pallas_call(
        kernel,
        grid=(turned + plain,),
        in_specs=in_specs,
        out_specs=pl.BlockSpec((rows, block), lambda i: (0, i)),
        out_shape=jax.ShapeDtypeStruct((rows, (turned + plain) * block), bf16),
        compiler_params=VMEM,
        cost_estimate=pl.CostEstimate(flops=1, bytes_accessed=1, transcendentals=0),
    )(*operands)


def assemble(whole, by_y, by_x, low, high, cols, counts):
    rows, width = whole.shape[0] // cols, whole.shape[1]
    size = rows // sum(counts)
    half = cols // 2

    def kernel(whole_ref, y_ref, x_ref, low_ref, high_ref, *outs):
        step = pl.program_id(0)
        at = 0
        for out, count in zip(outs, counts):
            for j in range(count):
                piece = slice(at, at + size)
                out[j, :, :width] = whole_ref[piece]
                out[j, :, width : 2 * width] = y_ref[piece]
                out[j, :, 2 * width : 3 * width] = x_ref[piece]

                @pl.when(step < half)
                def _():
                    out[j, :, 3 * width :] = low_ref[piece]

                @pl.when(step >= half)
                def _():
                    out[j, :, 3 * width :] = high_ref[piece]

                at += size

    block = lambda index: pl.BlockSpec((rows, width), index)
    outs = pl.pallas_call(
        kernel,
        grid=(cols,),
        in_specs=[
            block(lambda i: (i, 0)),
            block(lambda i: (i, 0)),
            block(lambda i: (i, 0)),
            block(lambda i: (jnp.minimum(i, half - 1), 0)),
            block(lambda i: (jnp.maximum(i - half, 0), 0)),
        ],
        out_specs=[pl.BlockSpec((c, size, 4 * width), lambda i: (0, i, 0)) for c in counts],
        out_shape=[jax.ShapeDtypeStruct((c, cols * size, 4 * width), bf16) for c in counts],
        compiler_params=VMEM,
        cost_estimate=pl.CostEstimate(flops=1, bytes_accessed=1, transcendentals=0),
    )(whole, by_y, by_x, low, high)
    return [o.reshape(-1, 4 * width) for o in outs]


def assemble_sides(whole_x, far_x, whole_y, far_y, cols, outs):
    rows, width = whole_x.shape[0] // cols, whole_x.shape[1]
    quarter = width // 2

    def kernel(x_ref, xf_ref, y_ref, yf_ref, *out_refs):
        for out, pieces in zip(out_refs, outs):
            for j, parts in enumerate(pieces):
                at = 0
                for over_x, first, size in parts:
                    here, there = slice(at, at + size), slice(first, first + size)
                    if over_x:
                        out[j, here, :width] = x_ref[there]
                        out[j, here, width:] = xf_ref[there]
                    else:
                        for q, ref in enumerate((y_ref, yf_ref, y_ref, yf_ref)):
                            side = slice(q // 2 * quarter, (q // 2 + 1) * quarter)
                            out[j, here, q * quarter : (q + 1) * quarter] = ref[there, side]
                    at += size

    sizes = [sum(p[2] for p in pieces[0]) for pieces in outs]
    results = pl.pallas_call(
        kernel,
        grid=(cols,),
        in_specs=[pl.BlockSpec((rows, width), lambda i: (i, 0))] * 4,
        out_specs=[
            pl.BlockSpec((len(p), n, 2 * width), lambda i: (0, i, 0)) for p, n in zip(outs, sizes)
        ],
        out_shape=[
            jax.ShapeDtypeStruct((len(p), cols * n, 2 * width), bf16) for p, n in zip(outs, sizes)
        ],
        compiler_params=VMEM,
        cost_estimate=pl.CostEstimate(flops=1, bytes_accessed=1, transcendentals=0),
    )(whole_x, far_x, whole_y, far_y)
    return [r.reshape(-1, 2 * width) for r in results]


def pair_block(rows, first):
    return pl.BlockSpec((rows, PAIR), lambda i: (0, first + i))


def attend(own, first, bias):
    n, m = own.shape[0], first.shape[0]
    width = own.shape[1] // 3
    pairs = width // PAIR

    def kernel(q_ref, ka_ref, kb_ref, va_ref, vb_ref, bias_ref, out_ref, total_ref):
        for h in range(2):
            lanes = slice(h * HEAD_DIM, (h + 1) * HEAD_DIM)
            keys = jnp.concatenate([ka_ref[:, lanes], kb_ref[:, lanes]], axis=0)
            values = jnp.concatenate([va_ref[:, lanes], vb_ref[:, lanes]], axis=0)
            scores = dot_nt(keys, q_ref[:, lanes]) * scale + bias_ref[...]
            peak = jnp.max(scores, axis=0, keepdims=True)
            weight = jnp.exp(scores - peak)
            total = jnp.sum(weight, axis=0, keepdims=True)
            mixed = dot_tn(values, weight.astype(bf16))
            out_ref[:, lanes] = (mixed / total).T.astype(bf16)
            total_ref[0, h, :, :] = peak + jnp.log(total)

    return pl.pallas_call(
        kernel,
        grid=(pairs,),
        in_specs=[
            pair_block(n, 0),
            pair_block(m, 0),
            pair_block(n, pairs),
            pair_block(m, pairs),
            pair_block(n, 2 * pairs),
            pl.BlockSpec((m + n, n), lambda i: (0, 0)),
        ],
        out_specs=[pair_block(n, 0), pl.BlockSpec((1, 2, 1, n), lambda i: (i, 0, 0, 0))],
        out_shape=[
            jax.ShapeDtypeStruct((n, width), bf16),
            jax.ShapeDtypeStruct((pairs, 2, 1, n), f32),
        ],
        compiler_params=VMEM,
        cost_estimate=pl.CostEstimate(
            flops=1, bytes_accessed=1, transcendentals=0
        ),
    )(own, first, own, first, own, bias)


def attend_back(own, first, bias, totals, mixture, grad_out, tables, extra):
    n, m = own.shape[0], first.shape[0]
    width = own.shape[1] // 3
    pairs = width // PAIR
    cos_own, sin_own, cos_first, sin_first = tables

    def kernel(
        q_ref, ka_ref, kb_ref, va_ref, vb_ref, bias_ref, total_ref, mix_ref, go_ref,
        co_ref, so_ref, cf_ref, sf_ref, *rest
    ):
        gq_ref, gka_ref, gkb_ref, gva_ref, gvb_ref = rest[-5:]
        queries_back, keys_back, values_back = [], [], []
        for h in range(2):
            lanes = slice(h * HEAD_DIM, (h + 1) * HEAD_DIM)
            keys = jnp.concatenate([ka_ref[:, lanes], kb_ref[:, lanes]], axis=0)
            values = jnp.concatenate([va_ref[:, lanes], vb_ref[:, lanes]], axis=0)
            queries, grads = q_ref[:, lanes], go_ref[:, lanes]
            inner = jnp.sum(
                grads.astype(f32) * mix_ref[:, lanes].astype(f32), axis=1, keepdims=True
            )
            inner = jnp.broadcast_to(inner, (n, 128)).T[:1]
            scores = dot_nt(keys, queries) * scale + bias_ref[...]
            weight = jnp.exp(scores - total_ref[0, h, :, :])
            grad_weight = dot_nt(values, grads)
            grad_scores = (weight * (grad_weight - inner)).astype(bf16)
            values_back.append(dot_nn(weight.astype(bf16), grads))
            keys_back.append(dot_nn(grad_scores, queries))
            queries_back.append(dot_tn(keys, grad_scores).T)
        side = lambda pair: jnp.concatenate(pair, axis=1)
        gq_ref[...] = rotated(side(queries_back) * scale, co_ref, so_ref).astype(bf16)
        gk, gv = side(keys_back) * scale, side(values_back)
        gka_ref[...] = rotated(gk[:m], cf_ref, sf_ref).astype(bf16)
        gkb_ref[...] = rotated(gk[m:], co_ref, so_ref).astype(bf16)
        if extra is None:
            gva_ref[...] = (0.5 * gv[:m].astype(bf16).astype(f32)).astype(bf16)
            gvb_ref[...] = (0.5 * gv[m:].astype(bf16).astype(f32)).astype(bf16)
        else:
            gva_ref[...] = (gv[:m] + rest[0][...].astype(f32)).astype(bf16)
            gvb_ref[...] = (gv[m:] + rest[1][...].astype(f32)).astype(bf16)

    whole = lambda shape: pl.BlockSpec(shape, lambda i: (0, 0))
    in_specs = [
        pair_block(n, 0),
        pair_block(m, 0),
        pair_block(n, pairs),
        pair_block(m, pairs),
        pair_block(n, 2 * pairs),
        whole((m + n, n)),
        pl.BlockSpec((1, 2, 1, n), lambda i: (i, 0, 0, 0)),
        pair_block(n, 0),
        pair_block(n, 0),
        whole((n, PAIR)),
        whole((n, PAIR)),
        whole((m, PAIR)),
        whole((m, PAIR)),
    ]
    operands = [own, first, own, first, own, bias, totals, mixture, grad_out]
    operands += [cos_own, -sin_own, cos_first, -sin_first]
    if extra is not None:
        in_specs += [pair_block(m, 0), pair_block(n, 0)]
        operands += list(extra)
    shape = lambda rows: jax.ShapeDtypeStruct((rows, width), bf16)
    return pl.pallas_call(
        kernel,
        grid=(pairs,),
        in_specs=in_specs,
        out_specs=[pair_block(r, 0) for r in (n, m, n, m, n)],
        out_shape=[shape(r) for r in (n, m, n, m, n)],
        compiler_params=VMEM,
        cost_estimate=pl.CostEstimate(
            flops=1, bytes_accessed=1, transcendentals=0
        ),
    )(*operands)


def make_body(col_count):
    ring_up = [(i, (i + 1) % col_count) for i in range(col_count)]
    rounds = []
    for k in range(col_count):
        pairs = []
        for core in range(2):
            for col in range(col_count):
                j = col ^ k
                pairs.append((core * col_count + col, (j & 1) * col_count + (j & ~1) + core))
        rounds.append(pairs)
    backs = [[(b, a) for a, b in pairs] for pairs in rounds]

    def body(
        tokens, segment_ids, prompt_reach,
        attn_gain_1, query_weight_1, key_weight_1, value_weight_1, out_weight_1,
        ffn_gain_1, gate_weight_1, up_weight_1, down_weight_1,
        attn_gain_2, query_weight_2, key_weight_2, value_weight_2, out_weight_2,
        ffn_gain_2, gate_weight_2, up_weight_2, down_weight_2,
        out_grad,
    ):
        xo_count = lax.axis_size("xo")
        xi, core = lax.axis_index("xi"), lax.axis_index("core")
        row, col = lax.axis_index("row"), lax.axis_index("col")
        chip_rows = tokens.shape[1]
        own_rows = chip_rows // 2
        quarter = tokens.shape[2]
        half_d = 2 * quarter
        slot = (col // 2) * 2 + core

        def place(p):
            return (2 * row + xi) ^ (0, 2, 1, 3)[p]

        gains = jnp.stack([attn_gain_1, ffn_gain_1, attn_gain_2, ffn_gain_2])
        high = gains.astype(bf16)
        middle = (gains - high.astype(f32)).astype(bf16)
        low = (gains - high.astype(f32) - middle.astype(f32)).astype(bf16)
        small = jnp.concatenate([high, middle, low, jnp.zeros_like(high)], axis=0)
        def unspread(array):
            pieces = jnp.stack([array[:, p * quarter : (p + 1) * quarter] for p in (0, 1, 2, 3)])
            got = []
            for k in range(col_count):
                p = slot ^ k ^ (2 * row + xi)
                p = (p & 1) * 2 + (p >> 1)
                piece = lax.dynamic_index_in_dim(pieces, p, 0, keepdims=False)
                got.append(lax.ppermute(piece, ("core", "col"), backs[k]))
            got = jnp.stack(got)
            got = jnp.concatenate(
                [lax.dynamic_index_in_dim(got, j ^ col, 0) for j in range(col_count)], axis=0
            )
            return got.reshape(tokens.shape)

        def units(block, transposed):
            if transposed:
                size = block.shape[1] // 2
                block = lax.dynamic_slice_in_dim(block, core * size, size, 1).T
            else:
                size = block.shape[0] // 2
                block = lax.dynamic_slice_in_dim(block, core * size, size, 0)
            return turn(block, xi, 1)

        def stack_attn(w_query, w_key, w_value, w_out):
            return jnp.concatenate(
                [units(w_query, True), units(w_key, True), units(w_value, True), units(w_out, False)]
            )

        def gather_col(block):
            return lax.all_gather(block, "col", axis=0, tiled=True)

        class Crossing:
            def __init__(self, whole, *milestones):
                self.whole = after(whole, *milestones)
                self.sides = (swap_x(self.whole), swap_y(self.whole))

            def complete(self, counts, *milestones):
                by_x, by_y = after(self.sides, *milestones)
                half = by_x.shape[0] // 2
                self.both = (swap_x(by_y[:half]), swap_y(by_x[half:]))
                return assemble(self.whole, by_y, by_x, *self.both, col_count, counts)

        def near_x(block):
            return block[:, :quarter]

        def local_ffn(w_gate, w_up, w_down):
            blocks = (units(w_gate, True), units(w_up, True), units(w_down, False))
            return jnp.concatenate([near_x(b) for b in blocks])

        attn_local_one = near_x(
            stack_attn(query_weight_1, key_weight_1, value_weight_1, out_weight_1)
        )
        ffn_local_one = local_ffn(gate_weight_1, up_weight_1, down_weight_1)
        gate_two, up_two = units(gate_weight_2, True), units(up_weight_2, True)
        down_two = units(down_weight_2, False)
        wide, low = gate_two.shape[0], gate_two.shape[0] // 2
        tall = query_weight_2.shape[1] // 2
        qk_two = jnp.concatenate([units(query_weight_2, True), units(key_weight_2, True)])
        attn_y_two = jnp.concatenate([units(value_weight_2, True), units(out_weight_2, False)])
        ffn_y_two = jnp.concatenate([up_two, down_two[low:]])
        own = jnp.concatenate([near_x(qk_two), near_x(gate_two), near_x(down_two[:low])])
        both_rows = jnp.concatenate([own, swap_y(own)], axis=1)
        attn_x_two, ffn_x_two = both_rows[: 2 * tall], both_rows[2 * tall :]
        half = attn_local_one.shape[0] // 2
        qk_whole_one = gather_col(attn_local_one[:half])
        vo_whole_one = gather_col(after(attn_local_one[half:], qk_whole_one))
        attn_whole_one = jnp.concatenate(
            [w.reshape(col_count, -1, quarter) for w in (qk_whole_one, vo_whole_one)], axis=1
        ).reshape(-1, quarter)
        ffn_whole_one = gather_col(after(ffn_local_one, vo_whole_one))
        attn_whole_two = gather_col(after(jnp.concatenate([attn_x_two, attn_y_two]), ffn_whole_one))

        def halves(whole):
            whole = whole.reshape(col_count, 2, -1, half_d)
            return whole[:, 0].reshape(-1, half_d), whole[:, 1].reshape(-1, half_d)

        def spread(arrays, *milestones):
            pieces = after(jnp.concatenate(arrays, axis=1), *milestones)
            got = []
            for k in range(col_count):
                piece = lax.dynamic_index_in_dim(pieces, col ^ k, 0, keepdims=False)
                got.append(lax.ppermute(piece, ("core", "col"), rounds[k]))
            got = jnp.stack(got)
            return jnp.concatenate(
                [
                    lax.dynamic_index_in_dim(got, place(p) ^ slot, 0, keepdims=False)
                    for p in range(col_count)
                ],
                axis=1,
            )

        by_piece = lambda array: array.reshape(col_count, own_rows, quarter)
        got = spread(
            [by_piece(tokens), jnp.broadcast_to(small[None], (col_count,) + small.shape)],
            vo_whole_one,
        )
        residual = got[:own_rows].astype(f32)
        small = got[own_rows:].astype(f32)
        gains = small[0:4] + small[4:8] + small[8:12]

        both = jnp.stack([segment_ids, prompt_reach])
        both = jnp.where(core == col % 2, both, swap_core(both))
        both = lax.dynamic_index_in_dim(both, col // 2, 1, keepdims=False)
        segments, reach = both[0], both[1]
        group_len = segments.shape[0]
        size_0 = jnp.sum((segments == 0).astype(jnp.int32))
        size_1 = jnp.sum((segments == 1).astype(jnp.int32))
        starts = jnp.where(segments == 0, 0, jnp.where(segments == 1, size_0, size_0 + size_1))
        index = jnp.arange(group_len, dtype=jnp.int32)
        positions = index - starts + reach

        def mine(array):
            return turn(lax.dynamic_slice_in_dim(array, row * chip_rows, chip_rows, 0), core, 0)

        def leading(array):
            return turn(array[:chip_rows], core, 0)

        inverse = rope_base ** (-(jnp.arange(HEAD_DIM // 2, dtype=f32) * 2.0) / HEAD_DIM)

        def tables(position):
            angles = position.astype(f32)[:, None] * inverse[None, :]
            cosine, sine = jnp.cos(angles), jnp.sin(angles)
            return (
                jnp.concatenate([cosine] * 4, axis=1),
                jnp.concatenate([-sine, sine, -sine, sine], axis=1),
            )

        cos_own, sin_own = tables(mine(positions))
        cos_first, sin_first = tables(leading(positions))
        rope = (cos_own, sin_own, cos_first, sin_first)
        query_index, query_seg, query_reach = mine(index), mine(segments), mine(reach)
        first_index = jnp.where(row == 0, group_len, leading(index))
        key_index = jnp.concatenate([first_index, query_index])
        key_seg = jnp.concatenate([leading(segments), query_seg])
        allowed = (query_seg[None, :] == key_seg[:, None]) & (
            key_index[:, None] <= query_index[None, :]
        ) | (key_index[:, None] < query_reach[None, :])
        bias = jnp.where(allowed, 0.0, -1e30).astype(f32)

        def over_xo(total):
            if xo_count > 1:
                total = lax.psum(total, "xo")
            return total

        def scatter_col(array):
            return lax.psum_scatter(array, "col", scatter_dimension=0, tiled=True)

        def add(left, right):
            return (left.astype(f32) + right.astype(f32)).astype(bf16)

        def both_blocks(block):
            return jnp.stack([block, swap_core(block)])

        def finish(pair, at, size, transposed):
            pair = turn(pair[:, at : at + size].reshape(2 * size, half_d), core, 0)
            return (pair.T if transposed else pair).astype(f32)

        def quarters(array, *places):
            if len(places) == 1:
                return array[:, places[0] * quarter : (places[0] + 1) * quarter]
            return jnp.concatenate(
                [array[:, p * quarter : (p + 1) * quarter] for p in places], axis=1
            )

        class Return:
            def __init__(self, by_x, by_y):
                stack = lambda parts: jnp.concatenate(parts) if len(parts) > 1 else parts[0]
                self.near = [stack([n for n, _ in parts]) for parts in (by_x, by_y)]
                far = [stack([f for _, f in parts]) for parts in (by_x, by_y)]
                self.sent = (swap_x(far[0]), swap_y(far[1]))

            def second(self, milestones=(), before_y=()):
                sent = after(self.sent, *milestones)
                totals = [add(a, b) for a, b in zip(self.near, sent)]
                self.near = [t[:, :quarter] for t in totals]
                far = [t[:, quarter:] for t in totals]
                self.sent = (swap_y(after(far[0], *before_y)), swap_x(far[1]))

            def last(self, *milestones):
                sent = after(self.sent, *milestones)
                return [add(a, b) for a, b in zip(self.near, sent)]

        def return_sides(near_x, far_x, near_y, far_y):
            return near_x, swap_x(far_x), near_y, swap_y(far_y)

        def scatter_sides(sides, *milestones):
            near_x, sent_x, near_y, sent_y = sides
            sent_x, sent_y = after((sent_x, sent_y), *milestones)
            parts = [
                add(n, r).reshape(col_count, -1, half_d)
                for n, r in ((near_x, sent_x), (near_y, sent_y))
            ]
            packed = jnp.concatenate(parts, axis=1).reshape(-1, half_d)
            return packed, over_xo(scatter_col(packed))

        def settle_sides(total, *milestones):
            total = after(total, *milestones)
            half = total.shape[0] // 2
            first, second = total[:half], turn(total[half:], xi, 1)
            first = add(first[:, :quarter], swap_y(first[:, quarter:]))
            first = turn(jnp.concatenate([first, swap_x(first)], axis=1), xi, 1)
            return first, add(second, swap_x(second))

        def by_col(array):
            return array.reshape(col_count, -1, array.shape[-1])

        def flat(array):
            return array.reshape(-1, array.shape[-1])

        def return_ffn_two(gate, up, down):
            down = by_col(down[0])
            part = lambda rows, *places: quarters(flat(rows), *places)
            lower, upper = down[:, :low], down[:, low:]
            join = lambda a, b: flat(jnp.concatenate([by_col(a), by_col(b)], axis=1))
            return return_sides(
                join(gate[0], part(lower, 0, 1)), join(gate[1], part(lower, 2, 3)),
                join(up[0], part(upper, 0, 2)), join(up[1], part(upper, 1, 3)),
            )

        def return_attn_two(grads):
            qk = flat(jnp.concatenate([by_col(g) for g in grads[:2]], axis=1))
            vo = flat(jnp.concatenate([by_col(g) for g in grads[2:]], axis=1))
            return return_sides(
                quarters(qk, 0, 1), quarters(qk, 2, 3), quarters(vo, 0, 2), quarters(vo, 1, 3)
            )

        def finish_rows(total, sizes):
            pair, blocks, at = both_blocks(total), [], 0
            for size, transposed in sizes:
                blocks.append(finish(pair, at, size, transposed))
                at += size
            return blocks

        def finish_ffn_two(total, *milestones):
            first, second = settle_sides(total, *milestones)
            rows = [first[:wide], second[:wide], first[wide:], second[wide:]]
            return finish_rows(
                jnp.concatenate(rows), ((wide, True), (wide, True), (wide, False))
            )

        def finish_attn_two(total, *milestones):
            total = jnp.concatenate(settle_sides(total, *milestones))
            return finish_rows(
                total, ((tall, True), (tall, True), (tall, True), (tall, False))
            )

        def pack_parts(parts):
            packed = [p.reshape(col_count, -1, quarter) for p in parts]
            return jnp.concatenate(packed, axis=1).reshape(-1, quarter)

        def scatter(packed):
            return over_xo(scatter_col(packed))

        def return_ffn(gate, up, down):
            half = down[0].shape[0] // 2
            low = (quarters(down[0], 0, 1)[:half], quarters(down[0], 2, 3)[:half])
            high = (quarters(down[0], 0, 2)[half:], quarters(down[0], 1, 3)[half:])
            return Return([gate, low], [up, high])

        def last_ffn(returned, *milestones):
            first, second = returned.last(*milestones)
            rows = first.shape[0] * 2 // 3
            return [first[:rows], second[:rows], jnp.concatenate([first[rows:], second[rows:]])]

        def sides(left, right, x_first):
            stay, go = ((0, 1), (2, 3)) if x_first else ((0, 2), (1, 3))
            return (
                dot_tn(left, quarters(right, *stay)).astype(bf16),
                dot_tn(left, quarters(right, *go)).astype(bf16),
            )

        def finish_all(total, kinds, spare=0):
            total = turn(jnp.concatenate([total, swap_x(total)], axis=1), xi, 1)
            pair = both_blocks(total)
            size = (total.shape[0] - spare) // len(kinds)
            blocks = [finish(pair, j * size, size, kind) for j, kind in enumerate(kinds)]
            return (blocks, pair[:, len(kinds) * size :]) if spare else blocks

        def finish_ffn(total, *milestones):
            return finish_all(after(total, *milestones), (True, True, False))

        def finish_attn(total, *milestones, spare=0):
            return finish_all(after(total, *milestones), (True, True, True, False), spare)

        def return_attn(grads, extra_rows=None):
            pack = lambda pair: jnp.concatenate(
                [g.reshape(col_count, -1, D) for g in pair], axis=1
            ).reshape(-1, D)
            rest = list(grads[2:])
            if extra_rows is not None:
                rest.append(jnp.concatenate([extra_rows] * col_count))
            qk, vo = pack(grads[:2]), pack(rest)
            pairs = [
                (quarters(qk, 0, 1), quarters(qk, 2, 3)),
                (quarters(vo, 0, 2), quarters(vo, 1, 3)),
            ]
            return Return(pairs[:1], pairs[1:])

        def both_cores(own):
            return jnp.concatenate([own, swap_core(own)], axis=0)

        def core_sum(partial):
            sent = swap_core(partial[own_rows:].astype(bf16))
            return partial[:own_rows] + sent.astype(f32)

        def normalize(value, gain):
            factor = lax.rsqrt(jnp.mean(value * value, axis=1, keepdims=True) + norm_eps)
            return (value * factor * gain[None, :]).astype(bf16), factor

        def normalize_back(grad_normed, value, factor, gain):
            unit = value * factor
            gain_grad = jnp.sum(grad_normed * unit, axis=0)
            grad_unit = grad_normed * gain[None, :]
            inner = jnp.mean(grad_unit * unit, axis=1, keepdims=True)
            return factor * (grad_unit - unit * inner), gain_grad

        def flip_row(array):
            return jnp.concatenate(
                [array[:, p * quarter : (p + 1) * quarter] for p in (1, 0, 3, 2)], axis=1
            )

        def attn_forward(value, weights, gain, mix, start, *milestones):
            w_qk, w_value, w_out = weights
            normed_own, factor = normalize(value, gain)
            normed_first = both_cores(flip_row(lax.ppermute(after(normed_own, *milestones), "row", [(0, 1)])))
            normed = both_cores(normed_own)
            skip = w_qk.shape[0] // 512
            own = project(normed, w_qk, w_value, 0, cos_own, sin_own, mix and mix[0])
            first = project(normed_first, w_qk, w_value, skip, cos_first, sin_first, mix and mix[1])
            mixture, totals = attend(own, first, bias)
            mixture = after(mixture, *start(normed_first))
            result = value + core_sum(dot_nn(mixture, w_out))
            return result, (value, factor, normed, normed_first, own, first, mixture, totals)

        def ffn_forward(value, weights, gain, deadline):
            w_gate, w_up, w_down = weights
            normed_own, factor = normalize(value, gain)
            normed = both_cores(normed_own)
            gate = dot_nt(normed, w_gate)
            up = dot_nt(normed, w_up)
            hidden = (jax.nn.silu(gate) * up).astype(bf16)
            hidden = after(hidden, *deadline)
            return value + core_sum(dot_nn(hidden, w_down)), (value, factor, normed, gate, up, hidden)

        def ffn_backward(grad, weights, gain, saved, kinds, late):
            w_gate, w_up, w_down = weights
            value, factor, normed, gate, up, hidden = saved
            grad_full = both_cores(grad.astype(bf16))
            grad_hidden = dot_nt(grad_full, w_down)
            sig = jax.nn.sigmoid(gate)
            grad_gate = (grad_hidden * up * sig * (1.0 + gate * (1.0 - sig))).astype(bf16)
            grad_up = (grad_hidden * gate * sig).astype(bf16)
            grad_normed = core_sum(dot_nn(grad_gate, w_gate) + dot_nn(grad_up, w_up))
            lefts = (grad_gate, grad_up, after(hidden, *late))
            pairs = tuple(zip(lefts, (normed, normed, grad_full)))
            grads = [sides(*pair, k) for pair, k in zip(pairs[:2], kinds)]
            grads.append((dot_tn(*pairs[2]).astype(bf16),))
            step, gain_grad = normalize_back(grad_normed, value, factor, gain)
            return grad + step, grads, gain_grad

        def attn_backward(grad, weights, gain, saved, extra, milestones, late):
            w_qk, w_value, w_out = weights
            value, factor, normed, normed_first, own, first, mixture, totals = saved
            grad_full = both_cores(grad.astype(bf16))
            grad_mixture = after(dot_nt(grad_full, w_out).astype(bf16), *milestones)
            gq, gk_first, gk, gv_first, gv = attend_back(
                own, first, bias, totals, mixture, grad_mixture, rope, extra
            )
            gk_first, gv_first = after((gk_first, gv_first), *late)
            w_query, w_key = jnp.split(w_qk, 2)
            operand = core_sum(dot_nn(gk_first, w_key) + dot_nn(gv_first, w_value)).astype(bf16)
            sent_raw = lax.ppermute(operand, "row", [(1, 0)])
            sent = flip_row(sent_raw).astype(f32)
            grad_normed = core_sum(dot_nn(gq, w_query) + dot_nn(gk, w_key) + dot_nn(gv, w_value))
            done = gq
            gq, gk, gv, gk_first, gv_first = after((gq, gk, gv, gk_first, gv_first), operand)
            grads = [
                dot_tn(gq, normed).astype(bf16),
                (dot_tn(gk, normed) + dot_tn(gk_first, normed_first)).astype(bf16),
                (dot_tn(gv, normed) + dot_tn(gv_first, normed_first)).astype(bf16),
                dot_tn(mixture, grad_full).astype(bf16),
            ]
            step, gain_grad = normalize_back(grad_normed + sent, value, factor, gain)
            return grad + step, grads, gain_grad, (gv_first, gv), (done, operand, sent_raw)

        cross_one = Crossing(attn_whole_one)
        attn_one = cross_one.complete((2, 1, 1), bias, cos_own, cos_first)
        crossings = []

        def start_ffn_one(normed_first):
            crossings.append(Crossing(ffn_whole_one, normed_first, *cross_one.both))
            return (*crossings[0].sides, attn_whole_two)

        residual, kept_attn_one = attn_forward(
            residual, attn_one, gains[0], None, start_ffn_one, *cross_one.both
        )
        own_one, first_one = kept_attn_one[4], kept_attn_one[5]
        ffn_whole_two = gather_col(after(jnp.concatenate([ffn_x_two, ffn_y_two]), attn_whole_two))
        cross_ffn = crossings[0]
        ffn_one = cross_ffn.complete((1, 1, 1))
        wx, wy = halves(after(attn_whole_two, *cross_ffn.both))
        far = (swap_x(wx), swap_y(wy))
        residual, kept_ffn_one = ffn_forward(residual, ffn_one, gains[1], far)
        attn_two = assemble_sides(
            wx, far[0], wy, far[1], col_count,
            (
                (((True, 0, tall),), ((True, tall, tall),)),
                (((False, 0, tall),),),
                (((False, tall, tall),),),
            ),
        )
        ffn_sides, grads = [], []

        def start_ffn_two(normed_first):
            wx, wy = after(halves(ffn_whole_two), normed_first, *far)
            ffn_sides.extend((wx, swap_x(wx), wy, swap_y(wy)))
            grads.append(spread([by_piece(out_grad)], normed_first))
            return ffn_sides[1], ffn_sides[3], grads[0]

        residual, kept_attn_two = attn_forward(
            residual, attn_two, gains[2], (own_one, first_one), start_ffn_two
        )
        ffn_two = assemble_sides(
            *ffn_sides, col_count,
            (
                (((True, 0, wide),),),
                (((False, 0, wide),),),
                (((True, wide, low), (False, wide, low)),),
            ),
        )
        last_grad = grads[0]
        residual, kept_ffn_two = ffn_forward(residual, ffn_two, gains[3], ())
        output = unspread(residual.astype(bf16))

        kinds = (True, False)

        def leaves(grads):
            return [a for pair in grads for a in pair]

        grad, g_ffn_two, gain_ffn_two = ffn_backward(
            last_grad.astype(f32), ffn_two, gains[3], kept_ffn_two, kinds, ()
        )
        r_ffn_two = return_ffn_two(*g_ffn_two)
        grad, g_attn_two, gain_attn_two, extra, done_attn_two = attn_backward(
            grad, attn_two, gains[2], kept_attn_two, None, tuple(leaves(g_ffn_two)), (r_ffn_two[1], r_ffn_two[3], output)
        )
        r_attn_two = return_attn_two(g_attn_two)
        sent_attn_two = (r_attn_two[1], r_attn_two[3])
        grad, g_ffn_one, gain_ffn_one = ffn_backward(
            grad, ffn_one, gains[1], kept_ffn_one, kinds, ()
        )
        r_ffn_one = return_ffn(*after(tuple(g_ffn_one), *sent_attn_two))
        p_ffn_two, t_ffn_two = scatter_sides(r_ffn_two, *leaves(g_ffn_one))
        p_attn_two, t_attn_two = scatter_sides(r_attn_two, *leaves(g_ffn_one))
        grad, g_attn_one, gain_attn_one, _, (done_attn_one, operand, sent) = attn_backward(
            grad, attn_one, gains[0], kept_attn_one, extra,
            (p_attn_two, p_ffn_two, *leaves(g_ffn_one)), r_ffn_one.sent,
        )
        r_ffn_one.second((), (sent,))
        gain_rows = jnp.stack([gain_attn_one, gain_ffn_one, gain_attn_two, gain_ffn_two])
        gain_rows = jnp.pad(gain_rows, ((0, 12), (0, 0))).astype(bf16)
        r_attn_one = return_attn(g_attn_one, gain_rows)
        p_ffn_one = pack_parts(last_ffn(r_ffn_one, *r_attn_one.near))
        t_ffn_one = scatter(p_ffn_one)
        r_attn_one.second((p_ffn_one,))
        b_ffn_two = finish_ffn_two(t_ffn_two, p_ffn_one)
        b_attn_two = finish_attn_two(t_attn_two, p_ffn_one)
        p_attn_one = pack_parts(r_attn_one.last(t_ffn_one, *b_ffn_two, *b_attn_two))
        t_attn_one = scatter(p_attn_one)
        b_ffn_one = finish_ffn(t_ffn_one)
        b_attn_one, gain_sums = finish_attn(t_attn_one, spare=16)
        grad = after(grad, p_ffn_one)
        input_grad = unspread(grad.astype(bf16)).astype(f32)

        total = gain_sums[0, :4].astype(f32) + gain_sums[1, :4].astype(f32)
        total = turn(jnp.concatenate([total, swap_y(total)], axis=1), row, 1)
        total = lax.dynamic_slice_in_dim(total, col * quarter, quarter, 1)

        return (
            output, input_grad,
            total[0], *b_attn_one, total[1], *b_ffn_one,
            total[2], *b_attn_two, total[3], *b_ffn_two,
        )

    return body


def solution(mesh):
    devices = mesh.devices
    dp, rows, cols = devices.shape
    split = Mesh(devices.reshape(dp // 4, 2, 2, rows, cols), ("xo", "xi", "core", "row", "col"))
    dp_axes = ("xo", "xi", "core")
    token = P(None, dp_axes + ("row",), "col")
    group = P(None, dp_axes)
    gain = P("col")
    tall, wide = P("row", "col"), P("col", "row")
    layer = (gain, tall, tall, tall, wide, gain, tall, tall, wide)
    return jax.shard_map(
        make_body(cols),
        mesh=split,
        in_specs=(token, group, group) + layer + layer + (token,),
        out_specs=(token, token) + layer + layer,
        check_vma=False,
    )
```

```python
import jax
import jax.numpy as jnp
from jax import lax
from jax.experimental import pallas as pl
from jax.experimental.pallas import tpu as pltpu
from jax.sharding import Mesh, PartitionSpec as P

D = 1024
HEAD_DIM = 64
norm_eps = 1e-06
rope_base = 10000.0
scale = HEAD_DIM ** (-0.5)
bf16 = jnp.bfloat16
f32 = jnp.float32
PAIR = 2 * HEAD_DIM

SWAP = [(0, 1), (1, 0)]
VMEM = pltpu.CompilerParams(vmem_limit_bytes=56 << 20)


def dot_nt(left, right):
    return lax.dot_general(left, right, (((1,), (1,)), ((), ())), preferred_element_type=f32)


def dot_nn(left, right):
    return lax.dot_general(left, right, (((1,), (0,)), ((), ())), preferred_element_type=f32)


def dot_tn(left, right):
    return lax.dot_general(left, right, (((0,), (0,)), ((), ())), preferred_element_type=f32)


def swap_core(value):
    return lax.ppermute(value, "core", SWAP)


def swap_x(value):
    return lax.ppermute(value, "xi", SWAP)


def swap_y(value):
    return lax.ppermute(value, "row", SWAP)


def after(value, *milestones):
    return lax.optimization_barrier((value,) + milestones)[0] if milestones else value


def turn(array, by, axis):
    first, second = jnp.split(array, 2, axis=axis)
    return jnp.where(by == 0, array, jnp.concatenate([second, first], axis=axis))


def rotated(values, cos_ref, sin_ref):
    width = values.shape[1]
    half = HEAD_DIM // 2
    lane = lax.broadcasted_iota(jnp.int32, values.shape, 1) % HEAD_DIM
    other = jnp.where(
        lane < half, pltpu.roll(values, width - half, 1), pltpu.roll(values, half, 1)
    )
    cos, sin = cos_ref[...], sin_ref[...]
    times = width // PAIR
    if times > 1:
        cos = jnp.concatenate([cos] * times, axis=1)
        sin = jnp.concatenate([sin] * times, axis=1)
    return values * cos + other * sin


def project(normed, turned_weight, plain_weight, skip, cos, sin, mix):
    rows, block = normed.shape[0], 256
    turned = turned_weight.shape[0] // block - skip
    plain = plain_weight.shape[0] // block

    def kernel(n_ref, t_ref, p_ref, cos_ref, sin_ref, *rest):
        out_ref = rest[-1]
        step = pl.program_id(0)

        @pl.when(step < turned)
        def _():
            result = dot_nt(n_ref[...], t_ref[...])
            out_ref[...] = rotated(result, cos_ref, sin_ref).astype(bf16)

        @pl.when(step >= turned)
        def _():
            result = dot_nt(n_ref[...], p_ref[...])
            if mix is not None:
                result = 0.5 * result + 0.5 * rest[0][...].astype(f32)
            out_ref[...] = result.astype(bf16)

    whole = lambda shape: pl.BlockSpec(shape, lambda i: (0, 0))
    later = lambda i: jnp.maximum(i - turned, 0)
    in_specs = [
        whole((rows, D)),
        pl.BlockSpec((block, D), lambda i: (skip + jnp.minimum(i, turned - 1), 0)),
        pl.BlockSpec((block, D), lambda i: (later(i), 0)),
        whole((rows, PAIR)),
        whole((rows, PAIR)),
    ]
    operands = [normed, turned_weight, plain_weight, cos, sin]
    if mix is not None:
        before = mix.shape[1] // block - plain
        in_specs.append(pl.BlockSpec((rows, block), lambda i: (0, before + later(i))))
        operands.append(mix)
    return pl.pallas_call(
        kernel,
        grid=(turned + plain,),
        in_specs=in_specs,
        out_specs=pl.BlockSpec((rows, block), lambda i: (0, i)),
        out_shape=jax.ShapeDtypeStruct((rows, (turned + plain) * block), bf16),
        compiler_params=VMEM,
        cost_estimate=pl.CostEstimate(flops=1, bytes_accessed=1, transcendentals=0),
    )(*operands)


def assemble(whole, by_y, by_x, low, high, cols, counts):
    rows, width = whole.shape[0] // cols, whole.shape[1]
    size = rows // sum(counts)
    half = cols // 2

    def kernel(whole_ref, y_ref, x_ref, low_ref, high_ref, *outs):
        step = pl.program_id(0)
        at = 0
        for out, count in zip(outs, counts):
            for j in range(count):
                piece = slice(at, at + size)
                out[j, :, :width] = whole_ref[piece]
                out[j, :, width : 2 * width] = y_ref[piece]
                out[j, :, 2 * width : 3 * width] = x_ref[piece]

                @pl.when(step < half)
                def _():
                    out[j, :, 3 * width :] = low_ref[piece]

                @pl.when(step >= half)
                def _():
                    out[j, :, 3 * width :] = high_ref[piece]

                at += size

    block = lambda index: pl.BlockSpec((rows, width), index)
    outs = pl.pallas_call(
        kernel,
        grid=(cols,),
        in_specs=[
            block(lambda i: (i, 0)),
            block(lambda i: (i, 0)),
            block(lambda i: (i, 0)),
            block(lambda i: (jnp.minimum(i, half - 1), 0)),
            block(lambda i: (jnp.maximum(i - half, 0), 0)),
        ],
        out_specs=[pl.BlockSpec((c, size, 4 * width), lambda i: (0, i, 0)) for c in counts],
        out_shape=[jax.ShapeDtypeStruct((c, cols * size, 4 * width), bf16) for c in counts],
        compiler_params=VMEM,
        cost_estimate=pl.CostEstimate(flops=1, bytes_accessed=1, transcendentals=0),
    )(whole, by_y, by_x, low, high)
    return [o.reshape(-1, 4 * width) for o in outs]


def assemble_sides(whole_x, far_x, whole_y, far_y, cols, outs):
    rows, width = whole_x.shape[0] // cols, whole_x.shape[1]
    quarter = width // 2

    def kernel(x_ref, xf_ref, y_ref, yf_ref, *out_refs):
        for out, pieces in zip(out_refs, outs):
            for j, parts in enumerate(pieces):
                at = 0
                for over_x, first, size in parts:
                    here, there = slice(at, at + size), slice(first, first + size)
                    if over_x:
                        out[j, here, :width] = x_ref[there]
                        out[j, here, width:] = xf_ref[there]
                    else:
                        for q, ref in enumerate((y_ref, yf_ref, y_ref, yf_ref)):
                            side = slice(q // 2 * quarter, (q // 2 + 1) * quarter)
                            out[j, here, q * quarter : (q + 1) * quarter] = ref[there, side]
                    at += size

    sizes = [sum(p[2] for p in pieces[0]) for pieces in outs]
    results = pl.pallas_call(
        kernel,
        grid=(cols,),
        in_specs=[pl.BlockSpec((rows, width), lambda i: (i, 0))] * 4,
        out_specs=[
            pl.BlockSpec((len(p), n, 2 * width), lambda i: (0, i, 0)) for p, n in zip(outs, sizes)
        ],
        out_shape=[
            jax.ShapeDtypeStruct((len(p), cols * n, 2 * width), bf16) for p, n in zip(outs, sizes)
        ],
        compiler_params=VMEM,
        cost_estimate=pl.CostEstimate(flops=1, bytes_accessed=1, transcendentals=0),
    )(whole_x, far_x, whole_y, far_y)
    return [r.reshape(-1, 2 * width) for r in results]


def pair_block(rows, first):
    return pl.BlockSpec((rows, PAIR), lambda i: (0, first + i))


def attend(own, first, bias):
    n, m = own.shape[0], first.shape[0]
    width = own.shape[1] // 3
    pairs = width // PAIR

    def kernel(q_ref, ka_ref, kb_ref, va_ref, vb_ref, bias_ref, out_ref, total_ref):
        for h in range(2):
            lanes = slice(h * HEAD_DIM, (h + 1) * HEAD_DIM)
            keys = jnp.concatenate([ka_ref[:, lanes], kb_ref[:, lanes]], axis=0)
            values = jnp.concatenate([va_ref[:, lanes], vb_ref[:, lanes]], axis=0)
            scores = dot_nt(keys, q_ref[:, lanes]) * scale + bias_ref[...]
            peak = jnp.max(scores, axis=0, keepdims=True)
            weight = jnp.exp(scores - peak)
            total = jnp.sum(weight, axis=0, keepdims=True)
            mixed = dot_tn(values, weight.astype(bf16))
            out_ref[:, lanes] = (mixed / total).T.astype(bf16)
            total_ref[0, h, :, :] = peak + jnp.log(total)

    return pl.pallas_call(
        kernel,
        grid=(pairs,),
        in_specs=[
            pair_block(n, 0),
            pair_block(m, 0),
            pair_block(n, pairs),
            pair_block(m, pairs),
            pair_block(n, 2 * pairs),
            pl.BlockSpec((m + n, n), lambda i: (0, 0)),
        ],
        out_specs=[pair_block(n, 0), pl.BlockSpec((1, 2, 1, n), lambda i: (i, 0, 0, 0))],
        out_shape=[
            jax.ShapeDtypeStruct((n, width), bf16),
            jax.ShapeDtypeStruct((pairs, 2, 1, n), f32),
        ],
        compiler_params=VMEM,
        cost_estimate=pl.CostEstimate(
            flops=1, bytes_accessed=1, transcendentals=0
        ),
    )(own, first, own, first, own, bias)


def attend_back(own, first, bias, totals, mixture, grad_out, tables, extra):
    n, m = own.shape[0], first.shape[0]
    width = own.shape[1] // 3
    pairs = width // PAIR
    cos_own, sin_own, cos_first, sin_first = tables

    def kernel(
        q_ref, ka_ref, kb_ref, va_ref, vb_ref, bias_ref, total_ref, mix_ref, go_ref,
        co_ref, so_ref, cf_ref, sf_ref, *rest
    ):
        gq_ref, gka_ref, gkb_ref, gva_ref, gvb_ref = rest[-5:]
        queries_back, keys_back, values_back = [], [], []
        for h in range(2):
            lanes = slice(h * HEAD_DIM, (h + 1) * HEAD_DIM)
            keys = jnp.concatenate([ka_ref[:, lanes], kb_ref[:, lanes]], axis=0)
            values = jnp.concatenate([va_ref[:, lanes], vb_ref[:, lanes]], axis=0)
            queries, grads = q_ref[:, lanes], go_ref[:, lanes]
            inner = jnp.sum(
                grads.astype(f32) * mix_ref[:, lanes].astype(f32), axis=1, keepdims=True
            )
            inner = jnp.broadcast_to(inner, (n, 128)).T[:1]
            scores = dot_nt(keys, queries) * scale + bias_ref[...]
            weight = jnp.exp(scores - total_ref[0, h, :, :])
            grad_weight = dot_nt(values, grads)
            grad_scores = (weight * (grad_weight - inner)).astype(bf16)
            values_back.append(dot_nn(weight.astype(bf16), grads))
            keys_back.append(dot_nn(grad_scores, queries))
            queries_back.append(dot_tn(keys, grad_scores).T)
        side = lambda pair: jnp.concatenate(pair, axis=1)
        gq_ref[...] = rotated(side(queries_back) * scale, co_ref, so_ref).astype(bf16)
        gk, gv = side(keys_back) * scale, side(values_back)
        gka_ref[...] = rotated(gk[:m], cf_ref, sf_ref).astype(bf16)
        gkb_ref[...] = rotated(gk[m:], co_ref, so_ref).astype(bf16)
        if extra is None:
            gva_ref[...] = (0.5 * gv[:m].astype(bf16).astype(f32)).astype(bf16)
            gvb_ref[...] = (0.5 * gv[m:].astype(bf16).astype(f32)).astype(bf16)
        else:
            gva_ref[...] = (gv[:m] + rest[0][...].astype(f32)).astype(bf16)
            gvb_ref[...] = (gv[m:] + rest[1][...].astype(f32)).astype(bf16)

    whole = lambda shape: pl.BlockSpec(shape, lambda i: (0, 0))
    in_specs = [
        pair_block(n, 0),
        pair_block(m, 0),
        pair_block(n, pairs),
        pair_block(m, pairs),
        pair_block(n, 2 * pairs),
        whole((m + n, n)),
        pl.BlockSpec((1, 2, 1, n), lambda i: (i, 0, 0, 0)),
        pair_block(n, 0),
        pair_block(n, 0),
        whole((n, PAIR)),
        whole((n, PAIR)),
        whole((m, PAIR)),
        whole((m, PAIR)),
    ]
    operands = [own, first, own, first, own, bias, totals, mixture, grad_out]
    operands += [cos_own, -sin_own, cos_first, -sin_first]
    if extra is not None:
        in_specs += [pair_block(m, 0), pair_block(n, 0)]
        operands += list(extra)
    shape = lambda rows: jax.ShapeDtypeStruct((rows, width), bf16)
    return pl.pallas_call(
        kernel,
        grid=(pairs,),
        in_specs=in_specs,
        out_specs=[pair_block(r, 0) for r in (n, m, n, m, n)],
        out_shape=[shape(r) for r in (n, m, n, m, n)],
        compiler_params=VMEM,
        cost_estimate=pl.CostEstimate(
            flops=1, bytes_accessed=1, transcendentals=0
        ),
    )(*operands)


def make_body(col_count):
    ring_up = [(i, (i + 1) % col_count) for i in range(col_count)]
    rounds = []
    for k in range(col_count):
        pairs = []
        for core in range(2):
            for col in range(col_count):
                j = col ^ k
                pairs.append((core * col_count + col, (j & 1) * col_count + (j & ~1) + core))
        rounds.append(pairs)
    backs = [[(b, a) for a, b in pairs] for pairs in rounds]

    def body(
        tokens, segment_ids, prompt_reach,
        attn_gain_1, query_weight_1, key_weight_1, value_weight_1, out_weight_1,
        ffn_gain_1, gate_weight_1, up_weight_1, down_weight_1,
        attn_gain_2, query_weight_2, key_weight_2, value_weight_2, out_weight_2,
        ffn_gain_2, gate_weight_2, up_weight_2, down_weight_2,
        out_grad,
    ):
        xo_count = lax.axis_size("xo")
        xi, core = lax.axis_index("xi"), lax.axis_index("core")
        row, col = lax.axis_index("row"), lax.axis_index("col")
        chip_rows = tokens.shape[1]
        own_rows = chip_rows // 2
        quarter = tokens.shape[2]
        half_d = 2 * quarter
        slot = (col // 2) * 2 + core

        def place(p):
            return (2 * row + xi) ^ (0, 2, 1, 3)[p]

        gains = jnp.stack([attn_gain_1, ffn_gain_1, attn_gain_2, ffn_gain_2])
        high = gains.astype(bf16)
        middle = (gains - high.astype(f32)).astype(bf16)
        low = (gains - high.astype(f32) - middle.astype(f32)).astype(bf16)
        small = jnp.concatenate([high, middle, low, jnp.zeros_like(high)], axis=0)
        def unspread(array):
            pieces = jnp.stack([array[:, p * quarter : (p + 1) * quarter] for p in (0, 1, 2, 3)])
            got = []
            for k in range(col_count):
                p = slot ^ k ^ (2 * row + xi)
                p = (p & 1) * 2 + (p >> 1)
                piece = lax.dynamic_index_in_dim(pieces, p, 0, keepdims=False)
                got.append(lax.ppermute(piece, ("core", "col"), backs[k]))
            got = jnp.stack(got)
            got = jnp.concatenate(
                [lax.dynamic_index_in_dim(got, j ^ col, 0) for j in range(col_count)], axis=0
            )
            return got.reshape(tokens.shape)

        def units(block, transposed):
            if transposed:
                size = block.shape[1] // 2
                block = lax.dynamic_slice_in_dim(block, core * size, size, 1).T
            else:
                size = block.shape[0] // 2
                block = lax.dynamic_slice_in_dim(block, core * size, size, 0)
            return turn(block, xi, 1)

        def stack_attn(w_query, w_key, w_value, w_out):
            return jnp.concatenate(
                [units(w_query, True), units(w_key, True), units(w_value, True), units(w_out, False)]
            )

        def gather_col(block):
            return lax.all_gather(block, "col", axis=0, tiled=True)

        class Crossing:
            def __init__(self, whole, *milestones):
                self.whole = after(whole, *milestones)
                self.sides = (swap_x(self.whole), swap_y(self.whole))

            def complete(self, counts, *milestones):
                by_x, by_y = after(self.sides, *milestones)
                half = by_x.shape[0] // 2
                self.both = (swap_x(by_y[:half]), swap_y(by_x[half:]))
                return assemble(self.whole, by_y, by_x, *self.both, col_count, counts)

        def near_x(block):
            return block[:, :quarter]

        def local_ffn(w_gate, w_up, w_down):
            blocks = (units(w_gate, True), units(w_up, True), units(w_down, False))
            return jnp.concatenate([near_x(b) for b in blocks])

        attn_local_one = near_x(
            stack_attn(query_weight_1, key_weight_1, value_weight_1, out_weight_1)
        )
        ffn_local_one = local_ffn(gate_weight_1, up_weight_1, down_weight_1)
        gate_two, up_two = units(gate_weight_2, True), units(up_weight_2, True)
        down_two = units(down_weight_2, False)
        wide, low = gate_two.shape[0], gate_two.shape[0] // 2
        tall = query_weight_2.shape[1] // 2
        qk_two = jnp.concatenate([units(query_weight_2, True), units(key_weight_2, True)])
        attn_y_two = jnp.concatenate([units(value_weight_2, True), units(out_weight_2, False)])
        ffn_y_two = jnp.concatenate([up_two, down_two[low:]])
        own = jnp.concatenate([near_x(qk_two), near_x(gate_two), near_x(down_two[:low])])
        both_rows = jnp.concatenate([own, swap_y(own)], axis=1)
        attn_x_two, ffn_x_two = both_rows[: 2 * tall], both_rows[2 * tall :]
        half = attn_local_one.shape[0] // 2
        qk_whole_one = gather_col(attn_local_one[:half])
        vo_whole_one = gather_col(after(attn_local_one[half:], qk_whole_one))
        attn_whole_one = jnp.concatenate(
            [w.reshape(col_count, -1, quarter) for w in (qk_whole_one, vo_whole_one)], axis=1
        ).reshape(-1, quarter)
        ffn_whole_one = gather_col(after(ffn_local_one, vo_whole_one))
        attn_whole_two = gather_col(after(jnp.concatenate([attn_x_two, attn_y_two]), ffn_whole_one))

        def halves(whole):
            whole = whole.reshape(col_count, 2, -1, half_d)
            return whole[:, 0].reshape(-1, half_d), whole[:, 1].reshape(-1, half_d)

        def spread(arrays, *milestones):
            pieces = after(jnp.concatenate(arrays, axis=1), *milestones)
            got = []
            for k in range(col_count):
                piece = lax.dynamic_index_in_dim(pieces, col ^ k, 0, keepdims=False)
                got.append(lax.ppermute(piece, ("core", "col"), rounds[k]))
            got = jnp.stack(got)
            return jnp.concatenate(
                [
                    lax.dynamic_index_in_dim(got, place(p) ^ slot, 0, keepdims=False)
                    for p in range(col_count)
                ],
                axis=1,
            )

        by_piece = lambda array: array.reshape(col_count, own_rows, quarter)
        got = spread(
            [by_piece(tokens), jnp.broadcast_to(small[None], (col_count,) + small.shape)],
            vo_whole_one, ffn_local_one,
        )
        residual = got[:own_rows].astype(f32)
        small = got[own_rows:].astype(f32)
        gains = small[0:4] + small[4:8] + small[8:12]

        both = jnp.stack([segment_ids, prompt_reach])
        both = jnp.where(core == col % 2, both, swap_core(both))
        both = lax.dynamic_index_in_dim(both, col // 2, 1, keepdims=False)
        segments, reach = both[0], both[1]
        group_len = segments.shape[0]
        size_0 = jnp.sum((segments == 0).astype(jnp.int32))
        size_1 = jnp.sum((segments == 1).astype(jnp.int32))
        starts = jnp.where(segments == 0, 0, jnp.where(segments == 1, size_0, size_0 + size_1))
        index = jnp.arange(group_len, dtype=jnp.int32)
        positions = index - starts + reach

        def mine(array):
            return turn(lax.dynamic_slice_in_dim(array, row * chip_rows, chip_rows, 0), core, 0)

        def leading(array):
            return turn(array[:chip_rows], core, 0)

        inverse = rope_base ** (-(jnp.arange(HEAD_DIM // 2, dtype=f32) * 2.0) / HEAD_DIM)

        def tables(position):
            angles = position.astype(f32)[:, None] * inverse[None, :]
            cosine, sine = jnp.cos(angles), jnp.sin(angles)
            return (
                jnp.concatenate([cosine] * 4, axis=1),
                jnp.concatenate([-sine, sine, -sine, sine], axis=1),
            )

        cos_own, sin_own = tables(mine(positions))
        cos_first, sin_first = tables(leading(positions))
        rope = (cos_own, sin_own, cos_first, sin_first)
        query_index, query_seg, query_reach = mine(index), mine(segments), mine(reach)
        first_index = jnp.where(row == 0, group_len, leading(index))
        key_index = jnp.concatenate([first_index, query_index])
        key_seg = jnp.concatenate([leading(segments), query_seg])
        allowed = (query_seg[None, :] == key_seg[:, None]) & (
            key_index[:, None] <= query_index[None, :]
        ) | (key_index[:, None] < query_reach[None, :])
        bias = jnp.where(allowed, 0.0, -1e30).astype(f32)

        def over_xo(total):
            if xo_count > 1:
                total = lax.psum(total, "xo")
            return total

        def scatter_col(array):
            return lax.psum_scatter(array, "col", scatter_dimension=0, tiled=True)

        def add(left, right):
            return (left.astype(f32) + right.astype(f32)).astype(bf16)

        def both_blocks(block):
            return jnp.stack([block, swap_core(block)])

        def finish(pair, at, size, transposed):
            pair = turn(pair[:, at : at + size].reshape(2 * size, half_d), core, 0)
            return (pair.T if transposed else pair).astype(f32)

        def quarters(array, *places):
            if len(places) == 1:
                return array[:, places[0] * quarter : (places[0] + 1) * quarter]
            return jnp.concatenate(
                [array[:, p * quarter : (p + 1) * quarter] for p in places], axis=1
            )

        class Return:
            def __init__(self, by_x, by_y):
                stack = lambda parts: jnp.concatenate(parts) if len(parts) > 1 else parts[0]
                self.near = [stack([n for n, _ in parts]) for parts in (by_x, by_y)]
                far = [stack([f for _, f in parts]) for parts in (by_x, by_y)]
                self.sent = (swap_x(far[0]), swap_y(far[1]))

            def second(self, milestones=(), before_y=()):
                sent = after(self.sent, *milestones)
                totals = [add(a, b) for a, b in zip(self.near, sent)]
                self.near = [t[:, :quarter] for t in totals]
                far = [t[:, quarter:] for t in totals]
                self.sent = (swap_y(after(far[0], *before_y)), swap_x(far[1]))

            def last(self, *milestones):
                sent = after(self.sent, *milestones)
                return [add(a, b) for a, b in zip(self.near, sent)]

        def return_sides(near_x, far_x, near_y, far_y):
            return near_x, swap_x(far_x), near_y, swap_y(far_y)

        def scatter_sides(sides, *milestones):
            near_x, sent_x, near_y, sent_y = sides
            sent_x, sent_y = after((sent_x, sent_y), *milestones)
            parts = [
                add(n, r).reshape(col_count, -1, half_d)
                for n, r in ((near_x, sent_x), (near_y, sent_y))
            ]
            packed = jnp.concatenate(parts, axis=1).reshape(-1, half_d)
            return packed, over_xo(scatter_col(packed))

        def settle_sides(total, *milestones):
            total = after(total, *milestones)
            half = total.shape[0] // 2
            first, second = total[:half], turn(total[half:], xi, 1)
            first = add(first[:, :quarter], swap_y(first[:, quarter:]))
            first = turn(jnp.concatenate([first, swap_x(first)], axis=1), xi, 1)
            return first, add(second, swap_x(second))

        def by_col(array):
            return array.reshape(col_count, -1, array.shape[-1])

        def flat(array):
            return array.reshape(-1, array.shape[-1])

        def return_ffn_two(gate, up, down):
            down = by_col(down[0])
            part = lambda rows, *places: quarters(flat(rows), *places)
            lower, upper = down[:, :low], down[:, low:]
            join = lambda a, b: flat(jnp.concatenate([by_col(a), by_col(b)], axis=1))
            return return_sides(
                join(gate[0], part(lower, 0, 1)), join(gate[1], part(lower, 2, 3)),
                join(up[0], part(upper, 0, 2)), join(up[1], part(upper, 1, 3)),
            )

        def return_attn_two(grads):
            qk = flat(jnp.concatenate([by_col(g) for g in grads[:2]], axis=1))
            vo = flat(jnp.concatenate([by_col(g) for g in grads[2:]], axis=1))
            return return_sides(
                quarters(qk, 0, 1), quarters(qk, 2, 3), quarters(vo, 0, 2), quarters(vo, 1, 3)
            )

        def finish_rows(total, sizes):
            pair, blocks, at = both_blocks(total), [], 0
            for size, transposed in sizes:
                blocks.append(finish(pair, at, size, transposed))
                at += size
            return blocks

        def finish_ffn_two(total, *milestones):
            first, second = settle_sides(total, *milestones)
            rows = [first[:wide], second[:wide], first[wide:], second[wide:]]
            return finish_rows(
                jnp.concatenate(rows), ((wide, True), (wide, True), (wide, False))
            )

        def finish_attn_two(total, *milestones):
            total = jnp.concatenate(settle_sides(total, *milestones))
            return finish_rows(
                total, ((tall, True), (tall, True), (tall, True), (tall, False))
            )

        def pack_parts(parts):
            packed = [p.reshape(col_count, -1, quarter) for p in parts]
            return jnp.concatenate(packed, axis=1).reshape(-1, quarter)

        def scatter(packed):
            return over_xo(scatter_col(packed))

        def return_ffn(gate, up, down):
            half = down[0].shape[0] // 2
            low = (quarters(down[0], 0, 1)[:half], quarters(down[0], 2, 3)[:half])
            high = (quarters(down[0], 0, 2)[half:], quarters(down[0], 1, 3)[half:])
            return Return([gate, low], [up, high])

        def last_ffn(returned, *milestones):
            first, second = returned.last(*milestones)
            rows = first.shape[0] * 2 // 3
            return [first[:rows], second[:rows], jnp.concatenate([first[rows:], second[rows:]])]

        def sides(left, right, x_first):
            stay, go = ((0, 1), (2, 3)) if x_first else ((0, 2), (1, 3))
            return (
                dot_tn(left, quarters(right, *stay)).astype(bf16),
                dot_tn(left, quarters(right, *go)).astype(bf16),
            )

        def finish_all(total, kinds, spare=0):
            total = turn(jnp.concatenate([total, swap_x(total)], axis=1), xi, 1)
            pair = both_blocks(total)
            size = (total.shape[0] - spare) // len(kinds)
            blocks = [finish(pair, j * size, size, kind) for j, kind in enumerate(kinds)]
            return (blocks, pair[:, len(kinds) * size :]) if spare else blocks

        def finish_ffn(total, *milestones):
            return finish_all(after(total, *milestones), (True, True, False))

        def finish_attn(total, *milestones, spare=0):
            return finish_all(after(total, *milestones), (True, True, True, False), spare)

        def return_attn(grads, extra_rows=None):
            pack = lambda pair: jnp.concatenate(
                [g.reshape(col_count, -1, D) for g in pair], axis=1
            ).reshape(-1, D)
            rest = list(grads[2:])
            if extra_rows is not None:
                rest.append(jnp.concatenate([extra_rows] * col_count))
            qk, vo = pack(grads[:2]), pack(rest)
            pairs = [
                (quarters(qk, 0, 1), quarters(qk, 2, 3)),
                (quarters(vo, 0, 2), quarters(vo, 1, 3)),
            ]
            return Return(pairs[:1], pairs[1:])

        def both_cores(own):
            return jnp.concatenate([own, swap_core(own)], axis=0)

        def core_sum(partial):
            sent = swap_core(partial[own_rows:].astype(bf16))
            return partial[:own_rows] + sent.astype(f32)

        def normalize(value, gain):
            factor = lax.rsqrt(jnp.mean(value * value, axis=1, keepdims=True) + norm_eps)
            return (value * factor * gain[None, :]).astype(bf16), factor

        def normalize_back(grad_normed, value, factor, gain):
            unit = value * factor
            gain_grad = jnp.sum(grad_normed * unit, axis=0)
            grad_unit = grad_normed * gain[None, :]
            inner = jnp.mean(grad_unit * unit, axis=1, keepdims=True)
            return factor * (grad_unit - unit * inner), gain_grad

        def flip_row(array):
            return jnp.concatenate(
                [array[:, p * quarter : (p + 1) * quarter] for p in (1, 0, 3, 2)], axis=1
            )

        def attn_forward(value, weights, gain, mix, start, *milestones):
            w_qk, w_value, w_out = weights
            normed_own, factor = normalize(value, gain)
            normed_first = both_cores(flip_row(lax.ppermute(after(normed_own, *milestones), "row", [(0, 1)])))
            normed = both_cores(normed_own)
            skip = w_qk.shape[0] // 512
            own = project(normed, w_qk, w_value, 0, cos_own, sin_own, mix and mix[0])
            first = project(normed_first, w_qk, w_value, skip, cos_first, sin_first, mix and mix[1])
            mixture, totals = attend(own, first, bias)
            mixture = after(mixture, *start(normed_first))
            result = value + core_sum(dot_nn(mixture, w_out))
            return result, (value, factor, normed, normed_first, own, first, mixture, totals)

        def ffn_forward(value, weights, gain, deadline):
            w_gate, w_up, w_down = weights
            normed_own, factor = normalize(value, gain)
            normed = both_cores(normed_own)
            gate = dot_nt(normed, w_gate)
            up = dot_nt(normed, w_up)
            hidden = (jax.nn.silu(gate) * up).astype(bf16)
            hidden = after(hidden, *deadline)
            return value + core_sum(dot_nn(hidden, w_down)), (value, factor, normed, gate, up, hidden)

        def ffn_backward(grad, weights, gain, saved, kinds, late):
            w_gate, w_up, w_down = weights
            value, factor, normed, gate, up, hidden = saved
            grad_full = both_cores(grad.astype(bf16))
            grad_hidden = dot_nt(grad_full, w_down)
            sig = jax.nn.sigmoid(gate)
            grad_gate = (grad_hidden * up * sig * (1.0 + gate * (1.0 - sig))).astype(bf16)
            grad_up = (grad_hidden * gate * sig).astype(bf16)
            grad_normed = core_sum(dot_nn(grad_gate, w_gate) + dot_nn(grad_up, w_up))
            lefts = (grad_gate, grad_up, after(hidden, *late))
            pairs = tuple(zip(lefts, (normed, normed, grad_full)))
            grads = [sides(*pair, k) for pair, k in zip(pairs[:2], kinds)]
            grads.append((dot_tn(*pairs[2]).astype(bf16),))
            step, gain_grad = normalize_back(grad_normed, value, factor, gain)
            return grad + step, grads, gain_grad

        def attn_backward(grad, weights, gain, saved, extra, milestones, late):
            w_qk, w_value, w_out = weights
            value, factor, normed, normed_first, own, first, mixture, totals = saved
            grad_full = both_cores(grad.astype(bf16))
            grad_mixture = after(dot_nt(grad_full, w_out).astype(bf16), *milestones)
            gq, gk_first, gk, gv_first, gv = attend_back(
                own, first, bias, totals, mixture, grad_mixture, rope, extra
            )
            gk_first, gv_first = after((gk_first, gv_first), *late)
            w_query, w_key = jnp.split(w_qk, 2)
            operand = core_sum(dot_nn(gk_first, w_key) + dot_nn(gv_first, w_value)).astype(bf16)
            sent_raw = lax.ppermute(operand, "row", [(1, 0)])
            sent = flip_row(sent_raw).astype(f32)
            grad_normed = core_sum(dot_nn(gq, w_query) + dot_nn(gk, w_key) + dot_nn(gv, w_value))
            done = gq
            gq, gk, gv, gk_first, gv_first = after((gq, gk, gv, gk_first, gv_first), operand)
            grads = [
                dot_tn(gq, normed).astype(bf16),
                (dot_tn(gk, normed) + dot_tn(gk_first, normed_first)).astype(bf16),
                (dot_tn(gv, normed) + dot_tn(gv_first, normed_first)).astype(bf16),
                dot_tn(mixture, grad_full).astype(bf16),
            ]
            step, gain_grad = normalize_back(grad_normed + sent, value, factor, gain)
            return grad + step, grads, gain_grad, (gv_first, gv), (done, operand, sent_raw)

        cross_one = Crossing(attn_whole_one)
        attn_one = cross_one.complete((2, 1, 1), bias, cos_own, cos_first)
        crossings = []

        def start_ffn_one(normed_first):
            crossings.append(Crossing(ffn_whole_one, normed_first, *cross_one.both))
            return (*crossings[0].sides, attn_whole_two)

        residual, kept_attn_one = attn_forward(
            residual, attn_one, gains[0], None, start_ffn_one, *cross_one.both
        )
        own_one, first_one = kept_attn_one[4], kept_attn_one[5]
        ffn_whole_two = gather_col(after(jnp.concatenate([ffn_x_two, ffn_y_two]), attn_whole_two))
        cross_ffn = crossings[0]
        ffn_one = cross_ffn.complete((1, 1, 1))
        wx, wy = halves(after(attn_whole_two, *cross_ffn.both))
        far = (swap_x(wx), swap_y(wy))
        residual, kept_ffn_one = ffn_forward(residual, ffn_one, gains[1], far)
        attn_two = assemble_sides(
            wx, far[0], wy, far[1], col_count,
            (
                (((True, 0, tall),), ((True, tall, tall),)),
                (((False, 0, tall),),),
                (((False, tall, tall),),),
            ),
        )
        ffn_sides, grads = [], []

        def start_ffn_two(normed_first):
            wx, wy = after(halves(ffn_whole_two), normed_first, *far)
            ffn_sides.extend((wx, swap_x(wx), wy, swap_y(wy)))
            grads.append(spread([by_piece(out_grad)], normed_first))
            return ffn_sides[1], ffn_sides[3], grads[0]

        residual, kept_attn_two = attn_forward(
            residual, attn_two, gains[2], (own_one, first_one), start_ffn_two
        )
        ffn_two = assemble_sides(
            *ffn_sides, col_count,
            (
                (((True, 0, wide),),),
                (((False, 0, wide),),),
                (((True, wide, low), (False, wide, low)),),
            ),
        )
        last_grad = grads[0]
        residual, kept_ffn_two = ffn_forward(residual, ffn_two, gains[3], ())
        output = unspread(residual.astype(bf16))

        kinds = (True, False)

        def leaves(grads):
            return [a for pair in grads for a in pair]

        grad, g_ffn_two, gain_ffn_two = ffn_backward(
            last_grad.astype(f32), ffn_two, gains[3], kept_ffn_two, kinds, ()
        )
        r_ffn_two = return_ffn_two(*g_ffn_two)
        grad, g_attn_two, gain_attn_two, extra, done_attn_two = attn_backward(
            grad, attn_two, gains[2], kept_attn_two, None, tuple(leaves(g_ffn_two)), (r_ffn_two[1], r_ffn_two[3], output)
        )
        r_attn_two = return_attn_two(g_attn_two)
        sent_attn_two = (r_attn_two[1], r_attn_two[3])
        grad, g_ffn_one, gain_ffn_one = ffn_backward(
            grad, ffn_one, gains[1], kept_ffn_one, kinds, ()
        )
        r_ffn_one = return_ffn(*after(tuple(g_ffn_one), *sent_attn_two))
        p_ffn_two, t_ffn_two = scatter_sides(r_ffn_two, *leaves(g_ffn_one))
        p_attn_two, t_attn_two = scatter_sides(r_attn_two, *leaves(g_ffn_one))
        grad, g_attn_one, gain_attn_one, _, (done_attn_one, operand, sent) = attn_backward(
            grad, attn_one, gains[0], kept_attn_one, extra,
            (p_attn_two, p_ffn_two, *leaves(g_ffn_one)), r_ffn_one.sent,
        )
        r_ffn_one.second((), (sent,))
        gain_rows = jnp.stack([gain_attn_one, gain_ffn_one, gain_attn_two, gain_ffn_two])
        gain_rows = jnp.pad(gain_rows, ((0, 12), (0, 0))).astype(bf16)
        r_attn_one = return_attn(g_attn_one, gain_rows)
        p_ffn_one = pack_parts(last_ffn(r_ffn_one, *r_attn_one.near))
        t_ffn_one = scatter(p_ffn_one)
        r_attn_one.second((p_ffn_one,))
        b_ffn_two = finish_ffn_two(t_ffn_two, p_ffn_one)
        b_attn_two = finish_attn_two(t_attn_two, p_ffn_one)
        p_attn_one = pack_parts(r_attn_one.last(t_ffn_one, *b_ffn_two, *b_attn_two))
        t_attn_one = scatter(p_attn_one)
        b_ffn_one = finish_ffn(t_ffn_one)
        b_attn_one, gain_sums = finish_attn(t_attn_one, spare=16)
        grad = after(grad, p_ffn_one)
        input_grad = unspread(grad.astype(bf16)).astype(f32)

        total = gain_sums[0, :4].astype(f32) + gain_sums[1, :4].astype(f32)
        total = turn(jnp.concatenate([total, swap_y(total)], axis=1), row, 1)
        total = lax.dynamic_slice_in_dim(total, col * quarter, quarter, 1)

        return (
            output, input_grad,
            total[0], *b_attn_one, total[1], *b_ffn_one,
            total[2], *b_attn_two, total[3], *b_ffn_two,
        )

    return body


def solution(mesh):
    devices = mesh.devices
    dp, rows, cols = devices.shape
    split = Mesh(devices.reshape(dp // 4, 2, 2, rows, cols), ("xo", "xi", "core", "row", "col"))
    dp_axes = ("xo", "xi", "core")
    token = P(None, dp_axes + ("row",), "col")
    group = P(None, dp_axes)
    gain = P("col")
    tall, wide = P("row", "col"), P("col", "row")
    layer = (gain, tall, tall, tall, wide, gain, tall, tall, wide)
    return jax.shard_map(
        make_body(cols),
        mesh=split,
        in_specs=(token, group, group) + layer + layer + (token,),
        out_specs=(token, token) + layer + layer,
        check_vma=False,
    )
```
